32 devices in a mesh: circ: 4 (over z), span: 4 (over y, core), axial: 2 (over x).
Axes of the slice: x: 2, y: 2, z: 4, core: 2. Of those that a mesh axis runs over, the one named last changes fastest.
Arguments:
- rotor_outlet: float32 [5, 64, 512], P(None, ('span', 'axial'), 'circ'), may hold values from -6 to 6
- blade_count: int32 [1], replicated, may hold values from 3 to 15
- harmonic_list: int32 [8], replicated, may hold values from 1 to 16
- donor_index: int32 [128], P('span'), may hold values from 0 to 62, as said below
- donor_weight: float32 [128], P('span'), may hold values from 0 to 1
- state: float32 [5, 128, 32, 512], P(None, 'span', 'axial', 'circ'), may hold values from -6 to 6
- time_step: float32 [128, 32, 512], P('span', 'axial', 'circ'), may hold values from 0.05 to 0.4
- flux_jacobian: float32 [3, 5, 5], replicated, may hold values from -2.5 to 2.5
Outputs:
- new_state: float32 [5, 128, 32, 512], P(None, 'span', 'axial', 'circ')
- residual: float32 [5, 128, 32, 512], P(None, 'span', 'axial', 'circ')
The draws below stay inside these ranges and needn't reach their ends.
Inputs may be any that keep to these rules, and one draw needn't show every extreme that they name: `donor_index`: the stator spanwise cells g * 32 to (g + 1) * 32 - 1 form group g; every entry of group g lies between g * 16 - 1 (0 for g = 0) and (g + 1) * 16 - 2; the first entry of each group equals that lower end and the last entry that upper end.
All inputs are finite; a program needn't handle non-finite values.
Results may differ from the reference program's by a relative error of at most 0.0001.
Values sent between devices are 32-bit elements; how exact they have to be, the bound alone decides.
No kernel may reach another device: no remote copies, remote signals or barrier semaphores. Data moves between devices by JAX's collectives and lax.ppermute only.
A program may use at most 128 MiB of HBM per device.

```python
import math
import jax
import jax.numpy as jnp
from jax import lax

NV = 5
NH = 8
SEGMENTS = 4
SL = 32
CL = 128
NS = 128
NA = 32
NTH = 512
RSPAN = 64
RBAND = 16
N_CIRC = 4


def draw_donor_index(key, part):
    key = jax.random.fold_in(key, 11)
    cells = jnp.arange(NS, dtype=jnp.int32)
    group = cells // SL
    within = cells % SL
    lowest = jnp.where(group == 0, 0, group * RBAND - 1).astype(jnp.int32)
    highest = ((group + 1) * RBAND - 2).astype(jnp.int32)
    jitter = jax.random.randint(key, (NS,), -1, 2, dtype=jnp.int32)
    base = group * RBAND - 1 + within * RBAND // SL + jitter
    donor = jnp.clip(base, lowest, highest)
    donor = jnp.where(within == 0, lowest, donor)
    donor = jnp.where(within == SL - 1, highest, donor)
    return donor.astype(jnp.int32)


def with_ends(drawn, rng, least, high):
    longest = drawn.shape.index(max(drawn.shape))
    spots = []
    for shift in (0, 1):
        where = [jax.random.randint(jax.random.fold_in(rng, axis), (), 0, length) for axis, length in enumerate(drawn.shape)]
        where[longest] = (where[longest] + shift) % drawn.shape[longest]
        spots.append(tuple(where))
    return drawn.at[spots[0]].set(least).at[spots[1]].set(high)


def shard_levels(stream_key, dims, split, least, top_value):
    gain = 1.0
    for axis_at, parts in split:
        draws = jax.random.uniform(jax.random.fold_in(jax.random.fold_in(stream_key, 6), axis_at), (parts,), jnp.float32, least / len(split), top_value / len(split))
        gain = gain * jnp.repeat(jnp.exp(draws), dims[axis_at] // parts).reshape((-1,) + (1,) * (len(dims) - 1 - axis_at))
    return gain


def normal_values(stream_key, dims, width, reach, split=(), held_as=jnp.bfloat16):
    array = jax.random.normal(stream_key, dims, jnp.float32) * width
    if len(split) > 0:
        array = shard_levels(stream_key, dims, split, -0.22, 0.18) * array
    return jnp.clip(array, min=-reach, max=reach).astype(held_as)


def setup_inputs(seed: int = 0) -> dict:
    key_list = jax.random.split(jax.random.key(seed), 9)
    rotor_outlet = normal_values(key_list[0], (NV, RSPAN, NTH), 1.0, 6.0, ((1, 8), (2, 4)), jnp.float32)
    blade_count = jax.random.randint(key_list[1], (1,), 3, CL * N_CIRC // (4 * NH)).astype(jnp.int32)
    harmonic_list = with_ends(jax.random.randint(key_list[2], (NH,), 1, 2 * NH + 1), jax.random.fold_in(key_list[2], 1), 1, 2 * NH).astype(jnp.int32)
    donor_index = draw_donor_index(jax.random.fold_in(key_list[8], 71), 0)
    donor_weight = jnp.clip(1.0 * jax.random.uniform(key_list[4], (NS,), jnp.float32) ** shard_levels(key_list[4], (NS,), ((0, 4),), -0.2, 0.2), 0.0, 1.0)
    state = normal_values(key_list[5], (NV, NS, NA, NTH), 1.0, 6.0, ((1, 4), (2, 2), (3, 4)), jnp.float32)
    time_step = jnp.clip(jnp.exp(math.log(0.4) - 2.0794415 * jax.random.uniform(key_list[6], (NS, NA, NTH), jnp.float32) ** shard_levels(key_list[6], (NS, NA, NTH), ((0, 4), (1, 2), (2, 4)), -0.2, 0.2)), 0.05, 0.4)
    flux_jacobian = normal_values(key_list[7], (3, NV, NV), NV ** -0.5, 2.5, (), jnp.float32)
    return dict(rotor_outlet=rotor_outlet, blade_count=blade_count, harmonic_list=harmonic_list, donor_index=donor_index, donor_weight=donor_weight, state=state, time_step=time_step, flux_jacobian=flux_jacobian)


SEGMENT_COEF = (0.25, 1.0 / 3.0, 0.5, 1.0)
DISSIP = 0.2


def make_basis(harmonic_list, blade_count, ncells, start, count):
    cells = start + jnp.arange(count, dtype=jnp.int32)
    waves = harmonic_list.astype(jnp.int32) * blade_count[0].astype(jnp.int32)
    phase = (waves[:, None] * cells[None, :]) % ncells
    angle = (2.0 * jnp.pi) * phase.astype(jnp.float32) / ncells
    return jnp.concatenate([jnp.cos(angle), jnp.sin(angle)], axis=0)


def apply_jac(matrix, field):
    return jnp.einsum("uv,vsat->usat", matrix, field, precision=lax.Precision.HIGHEST)


def operate(field, ghost, flux_jacobian):
    zero_span = jnp.zeros_like(field[:, :1])
    span_plus = jnp.concatenate([field[:, 1:], zero_span], axis=1)
    span_minus = jnp.concatenate([zero_span, field[:, :-1]], axis=1)
    zero_axial = jnp.zeros_like(field[:, :, :1])
    axial_plus = jnp.concatenate([field[:, :, 1:], zero_axial], axis=2)
    axial_minus = jnp.concatenate([ghost[:, :, None, :], field[:, :, :-1]], axis=2)
    theta_plus = jnp.roll(field, -1, axis=3)
    theta_minus = jnp.roll(field, 1, axis=3)
    total = apply_jac(flux_jacobian[0], (axial_plus - axial_minus) * 0.5)
    total = total + apply_jac(flux_jacobian[1], (span_plus - span_minus) * 0.5)
    total = total + apply_jac(flux_jacobian[2], (theta_plus - theta_minus) * 0.5)
    second = (axial_plus + axial_minus) + (span_plus + span_minus) + (theta_plus + theta_minus) - 6.0 * field
    return total - DISSIP * second


def reference(rotor_outlet, blade_count, harmonic_list, donor_index, donor_weight, state, time_step, flux_jacobian):
    ncells = rotor_outlet.shape[2]
    basis = make_basis(harmonic_list, blade_count, ncells, 0, ncells)
    coef = (2.0 / ncells) * jnp.einsum("vrj,kj->vrk", rotor_outlet, basis, precision=lax.Precision.HIGHEST)
    lower = jnp.take(coef, donor_index.astype(jnp.int32), axis=1)
    upper = jnp.take(coef, donor_index.astype(jnp.int32) + 1, axis=1)
    weight = donor_weight[None, :, None]
    inter = (1.0 - weight) * lower + weight * upper
    ghost = jnp.einsum("vsk,kj->vsj", inter, basis, precision=lax.Precision.HIGHEST)
    residual = operate(state, ghost, flux_jacobian)
    field = state - SEGMENT_COEF[0] * time_step[None] * residual
    for segment in range(1, SEGMENTS):
        field = state - SEGMENT_COEF[segment] * time_step[None] * operate(field, ghost, flux_jacobian)
    return field, residual
```

```python
import functools

import jax
import jax.numpy as jnp
import numpy as np
from jax import lax
from jax.experimental import pallas as pl
from jax.experimental.pallas import tpu as pltpu
from jax.sharding import PartitionSpec as P

SEGMENT_COEF = (0.25, 1.0 / 3.0, 0.5, 1.0)
DISSIP = 0.2
W = 4
HIGH = lax.Precision.HIGHEST
VMEM = pl.BlockSpec(memory_space=pltpu.VMEM)
SMEM = pl.BlockSpec(memory_space=pltpu.SMEM)
HBM = pl.BlockSpec(memory_space=pltpu.HBM)
ANY = pl.BlockSpec(memory_space=pl.ANY)
AXES = ("circ", "span", "axial")


def make_basis(harm, blade, nh, cells, ncells):
    width = cells.shape[1]
    row = lax.broadcasted_iota(jnp.int32, (nh, width), 0)
    waves = jnp.zeros((nh, width), jnp.int32)
    for k in range(nh):
        waves = jnp.where(row == k, harm[k] * blade[0], waves)
    phase = waves * cells
    phase = phase & (ncells - 1) if ncells & (ncells - 1) == 0 else phase % ncells
    angle = (2.0 * np.pi) * phase.astype(jnp.float32) / ncells
    return jnp.concatenate([jnp.cos(angle), jnp.sin(angle)], axis=0)


def dot(a, b, dims):
    return lax.dot_general(a, b, (dims, ((), ())), precision=HIGH, preferred_element_type=jnp.float32)


def axial_kernel(dims, state, dt, rotor, blade, harm, edge, bulk, part, *scratch):
    nv, sl, al, cl, nh = (dims[k] for k in ("nv", "sl", "al", "cl", "nh"))
    cells, dt_cells, rotor_v, blade_s, harm_s, sems = scratch
    axial = lax.axis_index("axial")
    circ = lax.axis_index("circ")
    swap = dims["n_axial"] == 2
    size = cells.shape[2]
    at = pl.multiple_of(jnp.where(axial == 0, al - size, 0), 8) if swap else 0
    copies = [
        pltpu.make_async_copy(state.at[:, :, pl.ds(at, size), :], cells, sems.at[0]),
        pltpu.make_async_copy(dt.at[:, pl.ds(at, size), :], dt_cells, sems.at[1]),
        pltpu.make_async_copy(rotor, rotor_v, sems.at[2]),
        pltpu.make_async_copy(blade, blade_s, sems.at[3]),
        pltpu.make_async_copy(harm, harm_s, sems.at[4]),
    ]
    for copy in copies:
        copy.start()
    for copy in copies[2:]:
        copy.wait()
    ncells = cl * dims["n_circ"]
    here = circ * cl + lax.broadcasted_iota(jnp.int32, (1, cl), 1)
    basis = make_basis(harm_s, blade_s, nh, here, ncells)
    rl = rotor_v.shape[1]
    flat = rotor_v[...].reshape(nv * rl, cl)
    part[...] = jnp.zeros_like(part)
    part[:, : nv * rl] = dot(basis, flat, ((1,), (1,))) * (2.0 / ncells)
    for copy in copies[:2]:
        copy.wait()

    def put(side, base):
        for f in range(nv + 1):
            for i in range(W):
                ref = cells.at[f] if f < nv else dt_cells
                rows = ref[:, base + i, :]
                edge[side, f, i, 0:W] = rows[0:W]
                edge[side, f, i, W:] = rows[sl - W :]
                bulk[side, f, i] = rows[W : sl - W]

    if swap:

        @pl.when(axial == 0)
        def _():
            put(0, size - W)

        @pl.when(axial != 0)
        def _():
            put(0, 0)

    else:
        put(0, size - W)
        put(1, 0)


def inter_rows(dims, parts, firsts, donor, weight):
    nv = dims["nv"]
    rl = dims["rl"]
    table = jnp.concatenate([p[:, : nv * rl] for p in parts], axis=1)
    rows = table.shape[1]
    row = lax.broadcasted_iota(jnp.int32, (rows, 128), 0)
    station = row % rl
    for i, first in enumerate(firsts):
        station = station + jnp.where(row // (nv * rl) == i, first, 0)
    mix = jnp.where(station == donor, 1.0 - weight, jnp.where(station == donor + 1, weight, 0.0))
    var = row // rl % nv
    return [dot(table, jnp.where(var == v, mix, 0.0), ((1,), (0,))) for v in range(nv)]


def span_kernel(dims, s_head, s_tail, d_head, d_tail, lo, hi, part, other, before, donor, weight, down, up, inter):
    nv, sl, al, cl, br, nh = (dims[k] for k in ("nv", "sl", "al", "cl", "br", "nh"))
    span = lax.axis_index("span")
    faces = (lo,) if dims["n_axial"] == 2 else (lo, hi)
    rows_of = (nv + 1) * W * (al + W * len(faces))
    for out, s_ref, d_ref, at in ((down, s_head, d_head, 0), (up, s_tail, d_tail, W)):
        for f in range(nv + 1):
            rows = slice(f * W * al, (f + 1) * W * al)
            out[rows, :] = s_ref[f] if f < nv else d_ref[...]
            for side, src in enumerate(faces):
                for i in range(W):
                    to = (nv + 1) * W * al + ((side * (nv + 1) + f) * W + i) * W
                    out[to : to + W, :] = src[f, i, at : at + W, :]

    if not dims["ride"]:
        return
    rl = dims["rl"]
    first = span * 2 * rl
    shares = inter_rows(
        dims, [part[...], other[...], before[...]], [first, first + rl, first - rl], donor[...], weight[...]
    )
    lane = lax.broadcasted_iota(jnp.int32, (2 * nh, 128), 1)
    head = tail = jnp.zeros((2 * nh, 128), jnp.float32)
    for v in range(nv):
        inter[v] = shares[v]
        mine = lane // W == v
        head = jnp.where(mine, pltpu.roll(shares[v], W * v, 1), head)
        tail = jnp.where(mine, pltpu.roll(shares[v], (W * v - (sl - W)) % 128, 1), tail)
    down[rows_of:, :] = head
    up[rows_of:, :] = tail


def lane_ids(rows=8):
    return lax.broadcasted_iota(jnp.int32, (rows, 128), 1)


def gather_strips(dims, load, store, tiles):
    nb, ng, br = dims["nb"], dims["ng"], dims["br"]
    group = lane_ids() // 8
    for g in range(ng):
        for t in tiles:
            acc = jnp.zeros((8, 128), jnp.float32)
            for r in range((nb - 1 - g) // ng + 1):
                part = pltpu.roll(load((ng * r + g) * br + 8 * t), (8 * r + 4) % 128, 1)
                acc = jnp.where(group == r, part, acc)
            store(g * br + 8 * t, acc)


def circ_kernel(
    dims, state, dt, lo_edge, hi_edge, lo, hi, below, above, inter, ext, left, right, share, strips
):
    nv, sl, al, cl, br, nb, ng, nh = (dims[k] for k in ("nv", "sl", "al", "cl", "br", "nb", "ng", "nh"))
    axial = lax.axis_index("axial")
    zero = jnp.zeros((8, cl), jnp.float32)
    for f in range(nv + 1):
        ext[f, 0:8, :] = zero
        ext[f, nb * br - br : nb * br - br + 8, :] = zero
        for s in range(sl):
            rows = slice(s * al, (s + 1) * al)
            at = (s + W) * br + 8
            ext[f, at : at + al, :] = state[f, rows, :] if f < nv else dt[rows, :]

    swap = dims["n_axial"] == 2
    for side, (edge, bulk, valid) in enumerate(
        ((lo_edge, lo, axial > 0), (hi_edge, hi, axial < dims["n_axial"] - 1))
    ):
        base = br if side else W

        def fill(edge, bulk, side, base):
            for f in range(nv + 1):
                for i in range(W):
                    part = (nv + 1) * W * al + (((0 if swap else side) * (nv + 1) + f) * W + i) * W
                    pieces = (
                        (0, W, lambda: below[part : part + W, :]),
                        (W, W, lambda: edge[f, i, 0:W]),
                        (2 * W, sl - 2 * W, lambda: bulk[f, i]),
                        (sl, W, lambda: edge[f, i, W:]),
                        (sl + W, W, lambda: above[part : part + W, :]),
                    )
                    for at, n, read in pieces:
                        val = jnp.zeros((n, cl), jnp.float32) if edge is None else read()
                        ext[f, pl.ds(base + at * br + i, n, stride=br), :] = val

        @pl.when(valid)
        def _(edge=edge, bulk=bulk, side=side, base=base):
            fill(edge, bulk, side, base)

        @pl.when(jnp.logical_not(valid))
        def _(side=side, base=base):
            fill(None, None, side, base)

    for f in range(nv + 1):
        for j in range(W):
            rows = slice((f * W + j) * al, (f * W + j + 1) * al)
            for src, b in ((below, j), (above, sl + W + j)):
                ext[f, b * br + 8 : b * br + 8 + al, :] = src[rows, :]

    def each(f, carry):
        def store(row, val):
            strips[f, row : row + 8, :] = val

        gather_strips(dims, lambda row: ext[f, row : row + 8, :], store, range(br // 8))
        return carry

    lax.fori_loop(0, nv + 1, each, 0)
    half = (nv + 1) // 2
    low = lane_ids(ng * br) % 8 < 4
    for f in range(half):
        one, two = strips[f], strips[f + half]
        rows = slice(f * ng * br, (f + 1) * ng * br)
        right[rows, :] = jnp.where(low, one, pltpu.roll(two, 4, 1))
        left[rows, :] = jnp.where(low, pltpu.roll(one, 124, 1), two)

    if not dims["ride"]:
        return
    wide = sl + 2 * W
    lane = lax.broadcasted_iota(jnp.int32, (2 * nh, 128), 1)
    rows = slice((nv + 1) * W * (al + W * (1 if swap else 2)), None)
    packed = [jnp.zeros((2 * nh, 128), jnp.float32)] * dims["packs"]
    for v in range(nv):
        whole = pltpu.roll(inter[v], W, 1)
        whole = jnp.where(lane < W, pltpu.roll(below[rows, :], (-W * v) % 128, 1), whole)
        whole = jnp.where(lane >= sl + W, pltpu.roll(above[rows, :], sl + W - W * v, 1), whole)
        pack, first = divmod(v, 128 // wide)
        first = first * wide
        packed[pack] = jnp.where(
            (lane >= first) & (lane < first + wide), pltpu.roll(whole, first, 1), packed[pack]
        )
    for i in range(dims["packs"]):
        at = half * ng * br + i * 2 * nh
        left[at : at + 2 * nh, :] = packed[i]
        right[at : at + 2 * nh, :] = packed[i]
        share[i * 2 * nh : (i + 1) * 2 * nh, :] = packed[i]


def ghost_table(dims, table, span):
    nv, sl, nh = (dims[k] for k in ("nv", "sl", "nh"))
    rows, width = table.shape
    donors = pltpu.roll(table[rows - 8 :, :], lax.rem(width - span * sl + W, width), 1)[:, :128]
    lane = lax.broadcasted_iota(jnp.int32, (1, 128), 1)
    where = span * sl - W + lane
    inside = (where >= 0) & (where < sl * dims["n_span"]) & (lane < sl + 2 * W)
    station = lax.broadcasted_iota(jnp.int32, (width, 128), 0)
    donor = (donors[0:1, :] + 0.5).astype(jnp.int32)
    weight = donors[1:2, :]
    mix = jnp.where(station == donor, 1.0 - weight, jnp.where(station == donor + 1, weight, 0.0))
    mix = jnp.where(inside, mix, 0.0)
    inter = dot(table[0 : rows - 8, :], mix, ((1,), (0,)))
    return [inter[v * 2 * nh : (v + 1) * 2 * nh, :] for v in range(nv)]


def step_kernel(
    dims, jac, harm, blade, shares, _, from_left, from_right, new, res, ext, new_v, res_v, q_a, q_b, p_0, p_a, p_b, edge, coef, sem
):
    nv, sl, al, cl, br, nb, ng, nh = (dims[k] for k in ("nv", "sl", "al", "cl", "br", "nb", "ng", "nh"))
    axial = lax.axis_index("axial")
    span = lax.axis_index("span")
    circ = lax.axis_index("circ")
    spare = (W - 1) * al
    parts = 4 if sl % 8 == 0 else 1
    for d in range(3):
        for u in range(nv):
            for v in range(nv):
                value = jac[d, u, v] * 0.5 - (DISSIP if u == v else 0.0)
                coef[(d * nv + u) * nv + v] = jnp.full((8, 128), value, jnp.float32)

    half = (nv + 1) // 2
    low = lane_ids(ng * br) % 8 < 4
    for f in range(half):
        rows = slice(f * ng * br, (f + 1) * ng * br)
        one, two = from_left[rows, :], from_right[rows, :]
        p_0[f, br : (ng + 1) * br, :] = jnp.where(low, one, pltpu.roll(two, 4, 1))
        p_0[f + half, br : (ng + 1) * br, :] = jnp.where(low, pltpu.roll(one, 124, 1), two)

    ncells = cl * dims["n_circ"]
    lane = lax.broadcasted_iota(jnp.int32, (1, 128), 1)
    wide = sl + 2 * W
    if dims["ride"]:
        rows = slice(half * ng * br, None)
        packed = from_left[rows, :] + from_right[rows, :] + shares[0][...] + shares[1][...]
        inter = []
        for v in range(nv):
            pack, first = divmod(v, 128 // wide)
            part = pltpu.roll(packed[pack * 2 * nh : (pack + 1) * 2 * nh, :], (-first * wide) % 128, 1)
            inter.append(jnp.where(lane < wide, part, 0.0))
    else:
        inter = ghost_table(dims, shares, span)
    start = circ * cl
    own = make_basis(harm, blade, nh, start + lax.broadcasted_iota(jnp.int32, (1, cl), 1), ncells)
    pos = lane % 8
    halo_cells = lax.rem(start + jnp.where(pos < 4, pos - 4, pos + cl - 4) + ncells, ncells)
    halo = make_basis(harm, blade, nh, halo_cells, ncells)
    s_id = lax.broadcasted_iota(jnp.int32, (128, 128), 0)
    r_id = lax.broadcasted_iota(jnp.int32, (128, 128), 1) // 8

    @pl.when(axial == 0)
    def _():
        for v in range(nv):
            part = inter[v]
            ghost = dot(part, own, ((0,), (0,)))
            ext[v, pl.ds(7, sl + 2 * W, stride=br), :] = ghost[: sl + 2 * W, :]
            ghost = dot(part, halo, ((0,), (0,)))
            for g in range(ng):
                picked = jnp.where(s_id == ng * r_id + g, ghost, 0.0)
                at = (g + 1) * br + 7
                p_0[v, at : at + 1, :] = jnp.sum(picked, axis=0, keepdims=True)

    lanes = lane_ids()
    first_lane, last_lane = lanes == 0, lanes == 127
    pos3, pos4 = lanes % 8 == 3, lanes % 8 == 4
    last = (ng + 1) * br

    def apply(cells):
        for c in cells:
            c["diff"] = [
                [plus - minus for plus, minus in zip(c[d + "+"], c[d + "-"])] for d in ("axial", "span", "theta")
            ]
            c["rest"] = [
                (2.0 * DISSIP) * (3.0 * q - (x + y + z))
                for q, x, y, z in zip(c["q"], c["axial-"], c["span-"], c["theta-"])
            ]
        out = [[] for _ in cells]
        for u in range(nv):
            acc = [c["rest"][u] for c in cells]
            for d in range(3):
                for v in range(nv):
                    k = coef[(d * nv + u) * nv + v]
                    for i, c in enumerate(cells):
                        acc[i] = acc[i] + k * c["diff"][d][v]
            for i in range(len(cells)):
                out[i].append(acc[i])
        return out

    def gather(view, at):
        def load(off):
            return [view[v, at + off : at + off + 8, :] for v in range(nv)]

        return {"q": load(0), "axial-": load(-1), "axial+": load(1), "span-": load(-br), "span+": load(br)}

    def turn(cell, beyond, at_plus, at_minus):
        cell["theta+"] = [
            pltpu.roll(jnp.where(at_plus, z, q), 127, 1) for z, q in zip(beyond, cell["q"])
        ]
        cell["theta-"] = [pltpu.roll(jnp.where(at_minus, z, q), 1, 1) for z, q in zip(beyond, cell["q"])]

    writes = [pltpu.make_async_copy(res_v.at[:, pl.ds(spare, sl * al), :], res, sem.at[0])]

    def stage(number, src, p_src, dst, p_dst):
        width = W - 1 - number
        factor = SEGMENT_COEF[number]
        final = number == len(SEGMENT_COEF) - 1
        for v in range(nv):
            p_src[v, 0:br, :] = pltpu.roll(p_src[v, last - br : last, :], 8, 1)
            p_src[v, last : last + br, :] = pltpu.roll(p_src[v, br : 2 * br, :], 120, 1)

        def blocks(b, count, tiles):
            around = pl.multiple_of((b - 1) * br, 8)
            rows = (count + 1) * br + (8 if tiles == [0] else br)
            view = src.at[:, pl.ds(around, rows), :]
            for t in tiles:
                cells = []
                for i in range(count):
                    r = (b + i) // ng
                    g = b + i - r * ng
                    p_row = pl.multiple_of((g + 1) * br, 8) + 8 * t
                    cell = gather(view, (i + 1) * br + 8 * t)
                    beyond = [pltpu.roll(p_src[v, pl.ds(p_row, 8), :], 124 - 8 * r, 1) for v in range(nv)]
                    turn(cell, beyond, first_lane, last_lane)
                    cells.append(cell)
                for i, result in enumerate(apply(cells)):
                    row = pl.multiple_of((b + i) * br, 8) + 8 * t
                    step = factor * ext[nv, pl.ds(row, 8), :]
                    out = pl.multiple_of((b + i - W) * al, 8) + 8 * (t - 1)
                    for u in range(nv):
                        value = ext[u, pl.ds(row, 8), :] - step * result[u]
                        if final:
                            new_v[u, pl.ds(out, 8), :] = value
                        else:
                            dst[u, pl.ds(row, 8), :] = value
                            if t > 0 and number == 0:
                                res_v[u, pl.ds(out + spare, 8), :] = result[u]

        def run(first, count, tiles):
            def loop(j, carry):
                blocks(first + 2 * j, 2, tiles)
                return carry

            lax.fori_loop(0, count // 2, loop, 0)
            if count % 2:
                blocks(first + count - 1, 1, tiles)

        if final:
            tiles = list(range(1, br // 8))
            for i in range(parts):
                run(W + i * (sl // parts), sl // parts, tiles)
                rows = pl.ds(i * (sl // parts) * al, sl // parts * al)
                copy = pltpu.make_async_copy(new_v.at[:, rows, :], new.at[:, rows, :], sem.at[i + 1])
                copy.start()
                writes.append(copy)
        else:
            run(W - width, sl + 2 * width, list(range(br // 8)))
            blocks(sl + W + width, 1, [0])
        if number == 0:
            writes[0].start()
        if final:
            return

        def edges(v, carry):
            def store(row, val):
                edge[v, row : row + 8, :] = val

            gather_strips(dims, lambda row: src[v, row : row + 8, :], store, range(br // 8))
            return carry

        lax.fori_loop(0, nv, edges, 0)

        def strip(g, carry):
            base = pl.multiple_of((g + 1) * br, 8)
            around = pl.multiple_of(g * br, 8)
            view = p_src.at[:, pl.ds(around, 3 * br), :]

            for t in range(br // 8):
                cell = gather(view, br + 8 * t)
                turn(cell, [edge[v, pl.ds(around + 8 * t, 8), :] for v in range(nv)], pos4, pos3)
                (result,) = apply([cell])
                step = factor * p_0[nv, pl.ds(base + 8 * t, 8), :]
                for u in range(nv):
                    p_dst[u, pl.ds(base + 8 * t, 8), :] = p_0[u, pl.ds(base + 8 * t, 8), :] - step * result[u]
            return carry

        lax.fori_loop(0, ng, strip, 0)

    stage(0, ext, p_0, q_a, p_a)
    stage(1, q_a, p_a, q_b, p_b)
    stage(2, q_b, p_b, q_a, p_a)
    stage(3, q_a, p_a, None, None)
    for copy in writes:
        copy.wait()


def shift_pairs(count, step, closed):
    return [(i, (i + step) % count) for i in range(count) if closed or 0 <= i + step < count]


def coef_table(part, donor_index, donor_weight, rl, nv, sizes):
    n_circ, n_span, n_axial = sizes
    modes, sl = part.shape[0], donor_index.shape[0]
    width = -(-max(rl * n_span * n_axial, sl * n_span) // 128) * 128
    circ, span, axial = (lax.axis_index(a) for a in AXES)
    rows = part[:, : nv * rl].reshape(modes, nv, rl).transpose(1, 0, 2).reshape(nv * modes, rl)
    table = jnp.zeros((nv * modes + 8, width), jnp.float32)
    table = lax.dynamic_update_slice(table, rows, (0, (span * n_axial + axial) * rl))
    donors = jnp.stack([donor_index.astype(jnp.float32), donor_weight])
    donors = jnp.where((circ == 0) & (axial == 0), donors, 0.0)
    table = lax.dynamic_update_slice(table, donors, (nv * modes, span * sl))
    return lax.psum(table, AXES)


def local(rotor_outlet, blade_count, harmonic_list, donor_index, donor_weight, state, time_step, flux_jacobian):
    f32 = jnp.float32
    n_circ, n_span, n_axial = (lax.axis_size(a) for a in AXES)
    nv, sl, al, cl = state.shape
    br = al + 2 * W
    nb = sl + 2 * W + 1
    ng = -(-nb // 16)
    nh = harmonic_list.shape[0]
    dims = dict(
        nv=nv, sl=sl, al=al, cl=cl, br=br, nb=nb, ng=ng, nh=nh, n_circ=n_circ, n_span=n_span, n_axial=n_axial
    )
    rl = rotor_outlet.shape[1]
    packs = -(-nv // (128 // (sl + 2 * W)))
    ride = n_axial == 2 and n_circ == 4 and nv * rl <= 128
    dims.update(rl=rl, packs=packs, ride=ride)
    params = pltpu.CompilerParams(vmem_limit_bytes=48 * 2**20)
    sides = 1 if n_axial == 2 else 2
    deep = 8 if n_axial == 2 else al

    edge, bulk, part = pl.pallas_call(
        functools.partial(axial_kernel, dims),
        out_shape=[
            jax.ShapeDtypeStruct((sides, nv + 1, W, 2 * W, cl), f32),
            jax.ShapeDtypeStruct((sides, nv + 1, W, sl - 2 * W, cl), f32),
            jax.ShapeDtypeStruct((2 * nh, -(-nv * rl // 128) * 128), f32),
        ],
        in_specs=[HBM] * 5,
        out_specs=[VMEM] * 3,
        scratch_shapes=[
            pltpu.VMEM((nv, sl, deep, cl), f32),
            pltpu.VMEM((sl, deep, cl), f32),
            pltpu.VMEM(rotor_outlet.shape, f32),
            pltpu.SMEM(blade_count.shape, jnp.int32),
            pltpu.SMEM(harmonic_list.shape, jnp.int32),
            pltpu.SemaphoreType.DMA((5,)),
        ],
        compiler_params=pltpu.CompilerParams(vmem_limit_bytes=63 * 2**20),
        name="axial_faces",
    )(state, time_step, rotor_outlet, blade_count, harmonic_list)
    state = state.reshape(nv, sl * al, cl)
    time_step = time_step.reshape(sl * al, cl)

    def axial_move(faces):
        if n_axial == 2:
            moved = lax.ppermute(faces[0], "axial", [(0, 1), (1, 0)])
            return moved, moved
        lo = lax.ppermute(faces[0], "axial", shift_pairs(n_axial, 1, False))
        hi = lax.ppermute(faces[1], "axial", shift_pairs(n_axial, -1, False))
        return lo, hi

    lo_edge, hi_edge = axial_move(edge)
    if ride:
        other = lax.ppermute(part, "axial", [(0, 1), (1, 0)])
        before = lax.ppermute(part, ("span", "axial"), shift_pairs(n_span * n_axial, 1, False))
        shares = None
    else:
        other = before = part
        shares = coef_table(part, donor_index, donor_weight, rl, nv, (n_circ, n_span, n_axial))
    lo, hi = axial_move(bulk)

    def spec(shape, *index):
        index = index or (0,) * len(shape)
        return pl.BlockSpec(shape, lambda i: index)

    faces = (nv + 1, W, 2 * W, cl)
    message = ((nv + 1) * W * (al + W * sides) + (2 * nh if ride else 0), cl)
    end = sl // W - 1
    pad = lambda x: jnp.pad(x, (0, 128 - sl))[None]
    down, up, inter = pl.pallas_call(
        functools.partial(span_kernel, dims),
        grid=(1,),
        out_shape=[jax.ShapeDtypeStruct(message, f32)] * 2 + [jax.ShapeDtypeStruct((nv, 2 * nh, 128), f32)],
        in_specs=[
            spec((nv, W * al, cl)),
            spec((nv, W * al, cl), 0, end, 0),
            spec((W * al, cl)),
            spec((W * al, cl), end, 0),
            spec(faces),
            spec(faces),
            spec(part.shape),
            spec(part.shape),
            spec(part.shape),
            spec((1, 128)),
            spec((1, 128)),
        ],
        out_specs=[spec(message), spec(message), spec((nv, 2 * nh, 128))],
        compiler_params=params,
        name="span_faces",
    )(
        state, state, time_step, time_step, lo_edge, hi_edge, part, other, before, pad(donor_index), pad(donor_weight)
    )
    below = lax.ppermute(up, "span", shift_pairs(n_span, 1, False))
    above = lax.ppermute(down, "span", shift_pairs(n_span, -1, False))

    strip = jax.ShapeDtypeStruct(((nv + 1) // 2 * ng * br + (packs * 2 * nh if ride else 0), 128), f32)
    ext, left, right, share = pl.pallas_call(
        functools.partial(circ_kernel, dims),
        out_shape=[
            jax.ShapeDtypeStruct((nv + 1, nb * br, cl), f32),
            strip,
            strip,
            jax.ShapeDtypeStruct((packs * 2 * nh, 128), f32),
        ],
        in_specs=[VMEM] * 9,
        out_specs=[VMEM] * 4,
        scratch_shapes=[pltpu.VMEM((nv + 1, ng * br, 128), f32)],
        compiler_params=params,
        name="circ_faces",
    )(state, time_step, lo_edge, hi_edge, lo, hi, below, above, inter)
    from_left = lax.ppermute(right, "circ", shift_pairs(n_circ, 1, True))
    from_right = lax.ppermute(left, "circ", shift_pairs(n_circ, -1, True))
    if ride:
        shares = [share, lax.ppermute(share, "circ", shift_pairs(n_circ, 2, True))]

    block = jax.ShapeDtypeStruct((nv, sl * al, cl), f32)
    field = pltpu.VMEM((nv, nb * br, cl), f32)
    strips = pltpu.VMEM((nv, (ng + 2) * br, 128), f32)
    new, res, _ = pl.pallas_call(
        functools.partial(step_kernel, dims),
        out_shape=[block, block, jax.ShapeDtypeStruct(ext.shape, f32)],
        in_specs=[SMEM, SMEM, SMEM, [VMEM, VMEM] if ride else VMEM, VMEM, VMEM, VMEM],
        out_specs=[HBM, HBM, VMEM],
        input_output_aliases={(5 if ride else 4): 2},
        scratch_shapes=[
            pltpu.VMEM((nv, sl * al, cl), f32),
            pltpu.VMEM((nv, (sl + 2 * W - 2) * al, cl), f32),
            field,
            field,
            pltpu.VMEM((nv + 1, (ng + 2) * br, 128), f32),
            strips,
            strips,
            pltpu.VMEM((nv, ng * br, 128), f32),
            pltpu.VMEM((3 * nv * nv, 8, 128), f32),
            pltpu.SemaphoreType.DMA((5,)),
        ],
        compiler_params=params,
        name="segments",
    )(flux_jacobian, harmonic_list, blade_count, shares, ext, from_left, from_right)
    return new.reshape(nv, sl, al, cl), res.reshape(nv, sl, al, cl)


def solution(mesh):
    return jax.shard_map(
        local,
        mesh=mesh,
        in_specs=(
            P(None, ("span", "axial"), "circ"),
            P(),
            P(),
            P("span"),
            P("span"),
            P(None, "span", "axial", "circ"),
            P("span", "axial", "circ"),
            P(),
        ),
        out_specs=(P(None, "span", "axial", "circ"), P(None, "span", "axial", "circ")),
        check_vma=False,
    )
```

```python
import functools

import jax
import jax.numpy as jnp
import numpy as np
from jax import lax
from jax.experimental import pallas as pl
from jax.experimental.pallas import tpu as pltpu
from jax.sharding import PartitionSpec as P

SEGMENT_COEF = (0.25, 1.0 / 3.0, 0.5, 1.0)
DISSIP = 0.2
W = 4
HIGH = lax.Precision.HIGHEST
VMEM = pl.BlockSpec(memory_space=pltpu.VMEM)
SMEM = pl.BlockSpec(memory_space=pltpu.SMEM)
HBM = pl.BlockSpec(memory_space=pltpu.HBM)
ANY = pl.BlockSpec(memory_space=pl.ANY)
AXES = ("circ", "span", "axial")


def make_basis(harm, blade, nh, cells, ncells):
    width = cells.shape[1]
    row = lax.broadcasted_iota(jnp.int32, (nh, width), 0)
    waves = jnp.zeros((nh, width), jnp.int32)
    for k in range(nh):
        waves = jnp.where(row == k, harm[k] * blade[0], waves)
    phase = waves * cells
    phase = phase & (ncells - 1) if ncells & (ncells - 1) == 0 else phase % ncells
    angle = (2.0 * np.pi) * phase.astype(jnp.float32) / ncells
    return jnp.concatenate([jnp.cos(angle), jnp.sin(angle)], axis=0)


def dot(a, b, dims):
    return lax.dot_general(a, b, (dims, ((), ())), precision=HIGH, preferred_element_type=jnp.float32)


def axial_kernel(dims, state, dt, rotor, blade, harm, edge, bulk, part, *scratch):
    nv, sl, al, cl, nh = (dims[k] for k in ("nv", "sl", "al", "cl", "nh"))
    cells, dt_cells, rotor_v, blade_s, harm_s, sems = scratch
    axial = lax.axis_index("axial")
    circ = lax.axis_index("circ")
    swap = dims["n_axial"] == 2
    size = cells.shape[2]
    at = pl.multiple_of(jnp.where(axial == 0, al - size, 0), 8) if swap else 0
    copies = [
        pltpu.make_async_copy(state.at[:, :, pl.ds(at, size), :], cells, sems.at[0]),
        pltpu.make_async_copy(dt.at[:, pl.ds(at, size), :], dt_cells, sems.at[1]),
        pltpu.make_async_copy(rotor, rotor_v, sems.at[2]),
        pltpu.make_async_copy(blade, blade_s, sems.at[3]),
        pltpu.make_async_copy(harm, harm_s, sems.at[4]),
    ]
    for copy in copies:
        copy.start()
    for copy in copies[2:]:
        copy.wait()
    ncells = cl * dims["n_circ"]
    here = circ * cl + lax.broadcasted_iota(jnp.int32, (1, cl), 1)
    basis = make_basis(harm_s, blade_s, nh, here, ncells)
    rl = rotor_v.shape[1]
    flat = rotor_v[...].reshape(nv * rl, cl)
    part[...] = jnp.zeros_like(part)
    part[:, : nv * rl] = dot(basis, flat, ((1,), (1,))) * (2.0 / ncells)
    for copy in copies[:2]:
        copy.wait()

    def put(side, base):
        for f in range(nv + 1):
            for i in range(W):
                ref = cells.at[f] if f < nv else dt_cells
                rows = ref[:, base + i, :]
                edge[side, f, i, 0:W] = rows[0:W]
                edge[side, f, i, W:] = rows[sl - W :]
                bulk[side, f, i] = rows[W : sl - W]

    if swap:

        @pl.when(axial == 0)
        def _():
            put(0, size - W)

        @pl.when(axial != 0)
        def _():
            put(0, 0)

    else:
        put(0, size - W)
        put(1, 0)


def inter_rows(dims, parts, firsts, donor, weight):
    nv = dims["nv"]
    rl = dims["rl"]
    table = jnp.concatenate([p[:, : nv * rl] for p in parts], axis=1)
    rows = table.shape[1]
    row = lax.broadcasted_iota(jnp.int32, (rows, 128), 0)
    station = row % rl
    for i, first in enumerate(firsts):
        station = station + jnp.where(row // (nv * rl) == i, first, 0)
    mix = jnp.where(station == donor, 1.0 - weight, jnp.where(station == donor + 1, weight, 0.0))
    var = row // rl % nv
    return [dot(table, jnp.where(var == v, mix, 0.0), ((1,), (0,))) for v in range(nv)]


def span_kernel(dims, s_head, s_tail, d_head, d_tail, lo, hi, part, other, before, donor, weight, down, up, inter):
    nv, sl, al, cl, br, nh = (dims[k] for k in ("nv", "sl", "al", "cl", "br", "nh"))
    span = lax.axis_index("span")
    faces = (lo,) if dims["n_axial"] == 2 else (lo, hi)
    rows_of = (nv + 1) * W * (al + W * len(faces))
    for out, s_ref, d_ref, at in ((down, s_head, d_head, 0), (up, s_tail, d_tail, W)):
        for f in range(nv + 1):
            rows = slice(f * W * al, (f + 1) * W * al)
            out[rows, :] = s_ref[f] if f < nv else d_ref[...]
            for side, src in enumerate(faces):
                for i in range(W):
                    to = (nv + 1) * W * al + ((side * (nv + 1) + f) * W + i) * W
                    out[to : to + W, :] = src[f, i, at : at + W, :]

    if not dims["ride"]:
        return
    rl = dims["rl"]
    first = span * 2 * rl
    shares = inter_rows(
        dims, [part[...], other[...], before[...]], [first, first + rl, first - rl], donor[...], weight[...]
    )
    lane = lax.broadcasted_iota(jnp.int32, (2 * nh, 128), 1)
    head = tail = jnp.zeros((2 * nh, 128), jnp.float32)
    for v in range(nv):
        inter[v] = shares[v]
        mine = lane // W == v
        head = jnp.where(mine, pltpu.roll(shares[v], W * v, 1), head)
        tail = jnp.where(mine, pltpu.roll(shares[v], (W * v - (sl - W)) % 128, 1), tail)
    down[rows_of:, :] = head
    up[rows_of:, :] = tail


def lane_ids(rows=8):
    return lax.broadcasted_iota(jnp.int32, (rows, 128), 1)


def gather_strips(dims, load, store, tiles):
    nb, ng, br = dims["nb"], dims["ng"], dims["br"]
    group = lane_ids() // 8
    for g in range(ng):
        for t in tiles:
            acc = jnp.zeros((8, 128), jnp.float32)
            for r in range((nb - 1 - g) // ng + 1):
                part = pltpu.roll(load((ng * r + g) * br + 8 * t), (8 * r + 4) % 128, 1)
                acc = jnp.where(group == r, part, acc)
            store(g * br + 8 * t, acc)


def circ_kernel(
    dims, state, dt, lo_edge, hi_edge, lo, hi, below, above, inter, ext, left, right, share, strips
):
    nv, sl, al, cl, br, nb, ng, nh = (dims[k] for k in ("nv", "sl", "al", "cl", "br", "nb", "ng", "nh"))
    axial = lax.axis_index("axial")
    turns = al // 8
    for f in range(nv + 1):
        for s in range(sl):
            for t in range(turns):
                rows = pl.ds(s * al + t, 8, stride=turns)
                at = (s + W) * br + 8 * (t + 1)
                ext[f, at : at + 8, :] = state[f, rows, :] if f < nv else dt[rows, :]

    swap = dims["n_axial"] == 2
    for side, (edge, bulk, valid) in enumerate(
        ((lo_edge, lo, axial > 0), (hi_edge, hi, axial < dims["n_axial"] - 1))
    ):
        base = 0 if side else W

        def fill(edge, bulk, side, base):
            for f in range(nv + 1):
                for i in range(W):
                    part = (nv + 1) * W * al + (((0 if swap else side) * (nv + 1) + f) * W + i) * W
                    pieces = (
                        (0, W, lambda: below[part : part + W, :]),
                        (W, W, lambda: edge[f, i, 0:W]),
                        (2 * W, sl - 2 * W, lambda: bulk[f, i]),
                        (sl, W, lambda: edge[f, i, W:]),
                        (sl + W, W, lambda: above[part : part + W, :]),
                    )
                    for at, n, read in pieces:
                        val = jnp.zeros((n, cl), jnp.float32) if edge is None else read()
                        ext[f, pl.ds(base + at * br + i, n, stride=br), :] = val

        @pl.when(valid)
        def _(edge=edge, bulk=bulk, side=side, base=base):
            fill(edge, bulk, side, base)

        @pl.when(jnp.logical_not(valid))
        def _(side=side, base=base):
            fill(None, None, side, base)

    for f in range(nv + 1):
        for j in range(W):
            for src, b in ((below, j), (above, sl + W + j)):
                for t in range(turns):
                    at = b * br + 8 * (t + 1)
                    ext[f, at : at + 8, :] = src[pl.ds((f * W + j) * al + t, 8, stride=turns), :]

    def each(f, carry):
        def store(row, val):
            strips[f, row : row + 8, :] = val

        gather_strips(dims, lambda row: ext[f, row : row + 8, :], store, range(br // 8))
        return carry

    lax.fori_loop(0, nv + 1, each, 0)
    half = (nv + 1) // 2
    low = lane_ids(ng * br) % 8 < 4
    for f in range(half):
        one, two = strips[f], strips[f + half]
        rows = slice(f * ng * br, (f + 1) * ng * br)
        right[rows, :] = jnp.where(low, one, pltpu.roll(two, 4, 1))
        left[rows, :] = jnp.where(low, pltpu.roll(one, 124, 1), two)

    if not dims["ride"]:
        return
    wide = sl + 2 * W
    lane = lax.broadcasted_iota(jnp.int32, (2 * nh, 128), 1)
    rows = slice((nv + 1) * W * (al + W * (1 if swap else 2)), None)
    packed = [jnp.zeros((2 * nh, 128), jnp.float32)] * dims["packs"]
    for v in range(nv):
        whole = pltpu.roll(inter[v], W, 1)
        whole = jnp.where(lane < W, pltpu.roll(below[rows, :], (-W * v) % 128, 1), whole)
        whole = jnp.where(lane >= sl + W, pltpu.roll(above[rows, :], sl + W - W * v, 1), whole)
        pack, first = divmod(v, 128 // wide)
        first = first * wide
        packed[pack] = jnp.where(
            (lane >= first) & (lane < first + wide), pltpu.roll(whole, first, 1), packed[pack]
        )
    for i in range(dims["packs"]):
        at = half * ng * br + i * 2 * nh
        left[at : at + 2 * nh, :] = packed[i]
        right[at : at + 2 * nh, :] = packed[i]
        share[i * 2 * nh : (i + 1) * 2 * nh, :] = packed[i]


def ghost_table(dims, table, span):
    nv, sl, nh = (dims[k] for k in ("nv", "sl", "nh"))
    rows, width = table.shape
    donors = pltpu.roll(table[rows - 8 :, :], lax.rem(width - span * sl + W, width), 1)[:, :128]
    lane = lax.broadcasted_iota(jnp.int32, (1, 128), 1)
    where = span * sl - W + lane
    inside = (where >= 0) & (where < sl * dims["n_span"]) & (lane < sl + 2 * W)
    station = lax.broadcasted_iota(jnp.int32, (width, 128), 0)
    donor = (donors[0:1, :] + 0.5).astype(jnp.int32)
    weight = donors[1:2, :]
    mix = jnp.where(station == donor, 1.0 - weight, jnp.where(station == donor + 1, weight, 0.0))
    mix = jnp.where(inside, mix, 0.0)
    inter = dot(table[0 : rows - 8, :], mix, ((1,), (0,)))
    return [inter[v * 2 * nh : (v + 1) * 2 * nh, :] for v in range(nv)]


def step_kernel(
    dims, jac, harm, blade, shares, _, from_left, from_right, new, res, ext, new_v, res_v, q_a, q_b, p_0, p_a, p_b, edge, coef, sem
):
    nv, sl, al, cl, br, nb, ng, nh = (dims[k] for k in ("nv", "sl", "al", "cl", "br", "nb", "ng", "nh"))
    axial = lax.axis_index("axial")
    span = lax.axis_index("span")
    circ = lax.axis_index("circ")
    spare = (W - 1) * al
    parts = 4 if sl % 8 == 0 else 1
    for d in range(3):
        for u in range(nv):
            for v in range(nv):
                value = jac[d, u, v] * 0.5 - (DISSIP if u == v else 0.0)
                coef[(d * nv + u) * nv + v] = jnp.full((8, 128), value, jnp.float32)

    half = (nv + 1) // 2
    low = lane_ids(ng * br) % 8 < 4
    for f in range(half):
        rows = slice(f * ng * br, (f + 1) * ng * br)
        one, two = from_left[rows, :], from_right[rows, :]
        p_0[f, br : (ng + 1) * br, :] = jnp.where(low, one, pltpu.roll(two, 4, 1))
        p_0[f + half, br : (ng + 1) * br, :] = jnp.where(low, pltpu.roll(one, 124, 1), two)

    ncells = cl * dims["n_circ"]
    lane = lax.broadcasted_iota(jnp.int32, (1, 128), 1)
    wide = sl + 2 * W
    if dims["ride"]:
        rows = slice(half * ng * br, None)
        packed = from_left[rows, :] + from_right[rows, :] + shares[0][...] + shares[1][...]
        inter = []
        for v in range(nv):
            pack, first = divmod(v, 128 // wide)
            part = pltpu.roll(packed[pack * 2 * nh : (pack + 1) * 2 * nh, :], (-first * wide) % 128, 1)
            inter.append(jnp.where(lane < wide, part, 0.0))
    else:
        inter = ghost_table(dims, shares, span)
    start = circ * cl
    own = make_basis(harm, blade, nh, start + lax.broadcasted_iota(jnp.int32, (1, cl), 1), ncells)
    pos = lane % 8
    halo_cells = lax.rem(start + jnp.where(pos < 4, pos - 4, pos + cl - 4) + ncells, ncells)
    halo = make_basis(harm, blade, nh, halo_cells, ncells)
    s_id = lax.broadcasted_iota(jnp.int32, (128, 128), 0)
    r_id = lax.broadcasted_iota(jnp.int32, (128, 128), 1) // 8

    @pl.when(axial == 0)
    def _():
        for v in range(nv):
            part = inter[v]
            ghost = dot(part, own, ((0,), (0,)))
            ext[v, pl.ds(7, sl + 2 * W, stride=br), :] = ghost[: sl + 2 * W, :]
            ghost = dot(part, halo, ((0,), (0,)))
            for g in range(ng):
                picked = jnp.where(s_id == ng * r_id + g, ghost, 0.0)
                at = (g + 1) * br + 7
                p_0[v, at : at + 1, :] = jnp.sum(picked, axis=0, keepdims=True)

    lanes = lane_ids()
    first_lane, last_lane = lanes == 0, lanes == 127
    pos3, pos4 = lanes % 8 == 3, lanes % 8 == 4
    last = (ng + 1) * br

    def apply(cells):
        for c in cells:
            c["diff"] = [
                [plus - minus for plus, minus in zip(c[d + "+"], c[d + "-"])] for d in ("axial", "span", "theta")
            ]
            c["rest"] = [
                (2.0 * DISSIP) * (3.0 * q - (x + y + z))
                for q, x, y, z in zip(c["q"], c["axial-"], c["span-"], c["theta-"])
            ]
        out = [[] for _ in cells]
        for u in range(nv):
            acc = [c["rest"][u] for c in cells]
            for d in range(3):
                for v in range(nv):
                    k = coef[(d * nv + u) * nv + v]
                    for i, c in enumerate(cells):
                        acc[i] = acc[i] + k * c["diff"][d][v]
            for i in range(len(cells)):
                out[i].append(acc[i])
        return out

    turns = al // 8
    sub = lax.broadcasted_iota(jnp.int32, (8, 128), 0)
    top, bottom = sub == 0, sub == 7

    def block_cells(view, at):
        memo = {}

        def load(t, off=0):
            if (t, off) not in memo:
                row = at + off + 8 * t
                memo[t, off] = [view[v, row : row + 8, :] for v in range(nv)]
            return memo[t, off]

        def rolled(t, amount):
            if (t, "roll", amount) not in memo:
                memo[t, "roll", amount] = [pltpu.roll(x, amount, 0) for x in load(t)]
            return memo[t, "roll", amount]

        def choose(mask, one, two):
            return [jnp.where(mask, x, y) for x, y in zip(one, two)]

        def values(t):
            if t == 0:
                plus = choose(bottom, rolled(1, 7), rolled(0, 7))
                minus = choose(top, rolled(turns, 1), rolled(0, 1))
            else:
                plus = load(t + 1) if t < turns else choose(bottom, rolled(0, 7), rolled(1, 7))
                minus = load(t - 1) if t > 1 else choose(top, rolled(0, 1), rolled(turns, 1))
            return {"q": load(t), "axial-": minus, "axial+": plus, "span-": load(t, -br), "span+": load(t, br)}

        return values

    def turn(cell, beyond, at_plus, at_minus):
        cell["theta+"] = [
            pltpu.roll(jnp.where(at_plus, z, q), 127, 1) for z, q in zip(beyond, cell["q"])
        ]
        cell["theta-"] = [pltpu.roll(jnp.where(at_minus, z, q), 1, 1) for z, q in zip(beyond, cell["q"])]

    writes = [pltpu.make_async_copy(res_v.at[:, pl.ds(spare, sl * al), :], res, sem.at[0])]

    def stage(number, src, p_src, dst, p_dst):
        width = W - 1 - number
        factor = SEGMENT_COEF[number]
        final = number == len(SEGMENT_COEF) - 1
        for v in range(nv):
            p_src[v, 0:br, :] = pltpu.roll(p_src[v, last - br : last, :], 8, 1)
            p_src[v, last : last + br, :] = pltpu.roll(p_src[v, br : 2 * br, :], 120, 1)

        def blocks(b, count, first):
            around = pl.multiple_of((b - 1) * br, 8)
            view = src.at[:, pl.ds(around, (count + 2) * br), :]
            values = [block_cells(view, (i + 1) * br) for i in range(count)]
            groups = [[(i, t) for t in range(1, turns + 1)] for i in range(count)]
            if first == 0:
                groups.append([(i, 0) for i in range(count)])
            for group in groups:
                cells = []
                for i, t in group:
                    r = (b + i) // ng
                    g = b + i - r * ng
                    p_row = pl.multiple_of((g + 1) * br, 8) + 8 * t
                    cell = values[i](t)
                    beyond = [pltpu.roll(p_src[v, pl.ds(p_row, 8), :], 124 - 8 * r, 1) for v in range(nv)]
                    turn(cell, beyond, first_lane, last_lane)
                    cells.append(cell)
                for (i, t), result in zip(group, apply(cells)):
                    row = pl.multiple_of((b + i) * br, 8) + 8 * t
                    step = factor * ext[nv, pl.ds(row, 8), :]
                    for u in range(nv):
                        value = ext[u, pl.ds(row, 8), :] - step * result[u]
                        if final:
                            rows = pl.ds(pl.multiple_of((b + i - W) * al, 8) + t - 1, 8, stride=turns)
                            new_v[u, rows, :] = value
                        else:
                            dst[u, pl.ds(row, 8), :] = value
                            if t > 0 and number == 0:
                                rows = pl.ds(pl.multiple_of((b + i - 1) * al, 8) + t - 1, 8, stride=turns)
                                res_v[u, rows, :] = result[u]

        def run(start, count, first):
            def loop(j, carry):
                blocks(start + 2 * j, 2, first)
                return carry

            lax.fori_loop(0, count // 2, loop, 0)
            if count % 2:
                blocks(start + count - 1, 1, first)

        if final:
            for i in range(parts):
                run(W + i * (sl // parts), sl // parts, 1)
                rows = pl.ds(i * (sl // parts) * al, sl // parts * al)
                copy = pltpu.make_async_copy(new_v.at[:, rows, :], new.at[:, rows, :], sem.at[i + 1])
                copy.start()
                writes.append(copy)
        else:
            run(W - width, sl + 2 * width, 0)
        if number == 0:
            writes[0].start()
        if final:
            return

        def edges(v, carry):
            def store(row, val):
                edge[v, row : row + 8, :] = val

            gather_strips(dims, lambda row: src[v, row : row + 8, :], store, range(br // 8))
            return carry

        lax.fori_loop(0, nv, edges, 0)

        def strip(g, carry):
            base = pl.multiple_of((g + 1) * br, 8)
            around = pl.multiple_of(g * br, 8)
            view = p_src.at[:, pl.ds(around, 3 * br), :]

            values = block_cells(view, br)
            for t in range(br // 8):
                cell = values(t)
                turn(cell, [edge[v, pl.ds(around + 8 * t, 8), :] for v in range(nv)], pos4, pos3)
                (result,) = apply([cell])
                step = factor * p_0[nv, pl.ds(base + 8 * t, 8), :]
                for u in range(nv):
                    p_dst[u, pl.ds(base + 8 * t, 8), :] = p_0[u, pl.ds(base + 8 * t, 8), :] - step * result[u]
            return carry

        lax.fori_loop(0, ng, strip, 0)

    stage(0, ext, p_0, q_a, p_a)
    stage(1, q_a, p_a, q_b, p_b)
    stage(2, q_b, p_b, q_a, p_a)
    stage(3, q_a, p_a, None, None)
    for copy in writes:
        copy.wait()


def shift_pairs(count, step, closed):
    return [(i, (i + step) % count) for i in range(count) if closed or 0 <= i + step < count]


def coef_table(part, donor_index, donor_weight, rl, nv, sizes):
    n_circ, n_span, n_axial = sizes
    modes, sl = part.shape[0], donor_index.shape[0]
    width = -(-max(rl * n_span * n_axial, sl * n_span) // 128) * 128
    circ, span, axial = (lax.axis_index(a) for a in AXES)
    rows = part[:, : nv * rl].reshape(modes, nv, rl).transpose(1, 0, 2).reshape(nv * modes, rl)
    table = jnp.zeros((nv * modes + 8, width), jnp.float32)
    table = lax.dynamic_update_slice(table, rows, (0, (span * n_axial + axial) * rl))
    donors = jnp.stack([donor_index.astype(jnp.float32), donor_weight])
    donors = jnp.where((circ == 0) & (axial == 0), donors, 0.0)
    table = lax.dynamic_update_slice(table, donors, (nv * modes, span * sl))
    return lax.psum(table, AXES)


def local(rotor_outlet, blade_count, harmonic_list, donor_index, donor_weight, state, time_step, flux_jacobian):
    f32 = jnp.float32
    n_circ, n_span, n_axial = (lax.axis_size(a) for a in AXES)
    nv, sl, al, cl = state.shape
    br = al + 2 * W
    nb = sl + 2 * W
    ng = -(-nb // 16)
    nh = harmonic_list.shape[0]
    dims = dict(
        nv=nv, sl=sl, al=al, cl=cl, br=br, nb=nb, ng=ng, nh=nh, n_circ=n_circ, n_span=n_span, n_axial=n_axial
    )
    rl = rotor_outlet.shape[1]
    packs = -(-nv // (128 // (sl + 2 * W)))
    ride = n_axial == 2 and n_circ == 4 and nv * rl <= 128
    dims.update(rl=rl, packs=packs, ride=ride)
    params = pltpu.CompilerParams(vmem_limit_bytes=48 * 2**20)
    sides = 1 if n_axial == 2 else 2
    deep = 8 if n_axial == 2 else al

    edge, bulk, part = pl.pallas_call(
        functools.partial(axial_kernel, dims),
        out_shape=[
            jax.ShapeDtypeStruct((sides, nv + 1, W, 2 * W, cl), f32),
            jax.ShapeDtypeStruct((sides, nv + 1, W, sl - 2 * W, cl), f32),
            jax.ShapeDtypeStruct((2 * nh, -(-nv * rl // 128) * 128), f32),
        ],
        in_specs=[HBM] * 5,
        out_specs=[VMEM] * 3,
        scratch_shapes=[
            pltpu.VMEM((nv, sl, deep, cl), f32),
            pltpu.VMEM((sl, deep, cl), f32),
            pltpu.VMEM(rotor_outlet.shape, f32),
            pltpu.SMEM(blade_count.shape, jnp.int32),
            pltpu.SMEM(harmonic_list.shape, jnp.int32),
            pltpu.SemaphoreType.DMA((5,)),
        ],
        compiler_params=pltpu.CompilerParams(vmem_limit_bytes=63 * 2**20),
        name="axial_faces",
    )(state, time_step, rotor_outlet, blade_count, harmonic_list)
    state = state.reshape(nv, sl * al, cl)
    time_step = time_step.reshape(sl * al, cl)

    def axial_move(faces):
        if n_axial == 2:
            moved = lax.ppermute(faces[0], "axial", [(0, 1), (1, 0)])
            return moved, moved
        lo = lax.ppermute(faces[0], "axial", shift_pairs(n_axial, 1, False))
        hi = lax.ppermute(faces[1], "axial", shift_pairs(n_axial, -1, False))
        return lo, hi

    lo_edge, hi_edge = axial_move(edge)
    if ride:
        other = lax.ppermute(part, "axial", [(0, 1), (1, 0)])
        before = lax.ppermute(part, ("span", "axial"), shift_pairs(n_span * n_axial, 1, False))
        shares = None
    else:
        other = before = part
        shares = coef_table(part, donor_index, donor_weight, rl, nv, (n_circ, n_span, n_axial))
    lo, hi = axial_move(bulk)

    def spec(shape, *index):
        index = index or (0,) * len(shape)
        return pl.BlockSpec(shape, lambda i: index)

    faces = (nv + 1, W, 2 * W, cl)
    message = ((nv + 1) * W * (al + W * sides) + (2 * nh if ride else 0), cl)
    end = sl // W - 1
    pad = lambda x: jnp.pad(x, (0, 128 - sl))[None]
    down, up, inter = pl.pallas_call(
        functools.partial(span_kernel, dims),
        grid=(1,),
        out_shape=[jax.ShapeDtypeStruct(message, f32)] * 2 + [jax.ShapeDtypeStruct((nv, 2 * nh, 128), f32)],
        in_specs=[
            spec((nv, W * al, cl)),
            spec((nv, W * al, cl), 0, end, 0),
            spec((W * al, cl)),
            spec((W * al, cl), end, 0),
            spec(faces),
            spec(faces),
            spec(part.shape),
            spec(part.shape),
            spec(part.shape),
            spec((1, 128)),
            spec((1, 128)),
        ],
        out_specs=[spec(message), spec(message), spec((nv, 2 * nh, 128))],
        compiler_params=params,
        name="span_faces",
    )(
        state, state, time_step, time_step, lo_edge, hi_edge, part, other, before, pad(donor_index), pad(donor_weight)
    )
    below = lax.ppermute(up, "span", shift_pairs(n_span, 1, False))
    above = lax.ppermute(down, "span", shift_pairs(n_span, -1, False))

    strip = jax.ShapeDtypeStruct(((nv + 1) // 2 * ng * br + (packs * 2 * nh if ride else 0), 128), f32)
    ext, left, right, share = pl.pallas_call(
        functools.partial(circ_kernel, dims),
        out_shape=[
            jax.ShapeDtypeStruct((nv + 1, nb * br, cl), f32),
            strip,
            strip,
            jax.ShapeDtypeStruct((packs * 2 * nh, 128), f32),
        ],
        in_specs=[VMEM] * 9,
        out_specs=[VMEM] * 4,
        scratch_shapes=[pltpu.VMEM((nv + 1, ng * br, 128), f32)],
        compiler_params=params,
        name="circ_faces",
    )(state, time_step, lo_edge, hi_edge, lo, hi, below, above, inter)
    from_left = lax.ppermute(right, "circ", shift_pairs(n_circ, 1, True))
    from_right = lax.ppermute(left, "circ", shift_pairs(n_circ, -1, True))
    if ride:
        shares = [share, lax.ppermute(share, "circ", shift_pairs(n_circ, 2, True))]

    block = jax.ShapeDtypeStruct((nv, sl * al, cl), f32)
    field = pltpu.VMEM((nv, nb * br, cl), f32)
    strips = pltpu.VMEM((nv, (ng + 2) * br, 128), f32)
    new, res, _ = pl.pallas_call(
        functools.partial(step_kernel, dims),
        out_shape=[block, block, jax.ShapeDtypeStruct(ext.shape, f32)],
        in_specs=[SMEM, SMEM, SMEM, [VMEM, VMEM] if ride else VMEM, VMEM, VMEM, VMEM],
        out_specs=[HBM, HBM, VMEM],
        input_output_aliases={(5 if ride else 4): 2},
        scratch_shapes=[
            pltpu.VMEM((nv, sl * al, cl), f32),
            pltpu.VMEM((nv, (sl + 2 * W - 2) * al, cl), f32),
            field,
            field,
            pltpu.VMEM((nv + 1, (ng + 2) * br, 128), f32),
            strips,
            strips,
            pltpu.VMEM((nv, ng * br, 128), f32),
            pltpu.VMEM((3 * nv * nv, 8, 128), f32),
            pltpu.SemaphoreType.DMA((5,)),
        ],
        compiler_params=params,
        name="segments",
    )(flux_jacobian, harmonic_list, blade_count, shares, ext, from_left, from_right)
    return new.reshape(nv, sl, al, cl), res.reshape(nv, sl, al, cl)


def solution(mesh):
    return jax.shard_map(
        local,
        mesh=mesh,
        in_specs=(
            P(None, ("span", "axial"), "circ"),
            P(),
            P(),
            P("span"),
            P("span"),
            P(None, "span", "axial", "circ"),
            P("span", "axial", "circ"),
            P(),
        ),
        out_specs=(P(None, "span", "axial", "circ"), P(None, "span", "axial", "circ")),
        check_vma=False,
    )
```

```python
import functools

import jax
import jax.numpy as jnp
import numpy as np
from jax import lax
from jax.experimental import pallas as pl
from jax.experimental.pallas import tpu as pltpu
from jax.sharding import PartitionSpec as P

SEGMENT_COEF = (0.25, 1.0 / 3.0, 0.5, 1.0)
DISSIP = 0.2
W = 4
HIGH = lax.Precision.HIGHEST
VMEM = pl.BlockSpec(memory_space=pltpu.VMEM)
SMEM = pl.BlockSpec(memory_space=pltpu.SMEM)
HBM = pl.BlockSpec(memory_space=pltpu.HBM)
ANY = pl.BlockSpec(memory_space=pl.ANY)
AXES = ("circ", "span", "axial")


def make_basis(harm, blade, nh, cells, ncells):
    width = cells.shape[1]
    row = lax.broadcasted_iota(jnp.int32, (nh, width), 0)
    waves = jnp.zeros((nh, width), jnp.int32)
    for k in range(nh):
        waves = jnp.where(row == k, harm[k] * blade[0], waves)
    phase = waves * cells
    phase = phase & (ncells - 1) if ncells & (ncells - 1) == 0 else phase % ncells
    angle = (2.0 * np.pi) * phase.astype(jnp.float32) / ncells
    return jnp.concatenate([jnp.cos(angle), jnp.sin(angle)], axis=0)


def dot(a, b, dims):
    return lax.dot_general(a, b, (dims, ((), ())), precision=HIGH, preferred_element_type=jnp.float32)


def axial_kernel(dims, state, dt, rotor, blade, harm, edge, bulk, part, *scratch):
    nv, sl, al, cl, nh = (dims[k] for k in ("nv", "sl", "al", "cl", "nh"))
    cells, dt_cells, rotor_v, blade_s, harm_s, sems = scratch
    axial = lax.axis_index("axial")
    circ = lax.axis_index("circ")
    swap = dims["n_axial"] == 2
    size = cells.shape[2]
    at = pl.multiple_of(jnp.where(axial == 0, al - size, 0), 8) if swap else 0
    copies = [
        pltpu.make_async_copy(state.at[:, :, pl.ds(at, size), :], cells, sems.at[0]),
        pltpu.make_async_copy(dt.at[:, pl.ds(at, size), :], dt_cells, sems.at[1]),
        pltpu.make_async_copy(rotor, rotor_v, sems.at[2]),
        pltpu.make_async_copy(blade, blade_s, sems.at[3]),
        pltpu.make_async_copy(harm, harm_s, sems.at[4]),
    ]
    for copy in copies:
        copy.start()
    for copy in copies[2:]:
        copy.wait()
    ncells = cl * dims["n_circ"]
    here = circ * cl + lax.broadcasted_iota(jnp.int32, (1, cl), 1)
    basis = make_basis(harm_s, blade_s, nh, here, ncells)
    rl = rotor_v.shape[1]
    flat = rotor_v[...].reshape(nv * rl, cl)
    part[...] = jnp.zeros_like(part)
    part[:, : nv * rl] = dot(basis, flat, ((1,), (1,))) * (2.0 / ncells)
    for copy in copies[:2]:
        copy.wait()

    def put(side, base):
        for f in range(nv + 1):
            for i in range(W):
                ref = cells.at[f] if f < nv else dt_cells
                rows = ref[:, base + i, :]
                edge[side, f, i, 0:W] = rows[0:W]
                edge[side, f, i, W:] = rows[sl - W :]
                bulk[side, f, i] = rows[W : sl - W]

    if swap:

        @pl.when(axial == 0)
        def _():
            put(0, size - W)

        @pl.when(axial != 0)
        def _():
            put(0, 0)

    else:
        put(0, size - W)
        put(1, 0)


def inter_rows(dims, parts, firsts, donor, weight):
    nv = dims["nv"]
    rl = dims["rl"]
    table = jnp.concatenate([p[:, : nv * rl] for p in parts], axis=1)
    rows = table.shape[1]
    row = lax.broadcasted_iota(jnp.int32, (rows, 128), 0)
    station = row % rl
    for i, first in enumerate(firsts):
        station = station + jnp.where(row // (nv * rl) == i, first, 0)
    mix = jnp.where(station == donor, 1.0 - weight, jnp.where(station == donor + 1, weight, 0.0))
    var = row // rl % nv
    return [dot(table, jnp.where(var == v, mix, 0.0), ((1,), (0,))) for v in range(nv)]


def span_kernel(dims, s_head, s_tail, d_head, d_tail, lo, hi, part, other, before, donor, weight, down, up, inter):
    nv, sl, al, cl, br, nh = (dims[k] for k in ("nv", "sl", "al", "cl", "br", "nh"))
    span = lax.axis_index("span")
    faces = (lo,) if dims["n_axial"] == 2 else (lo, hi)
    rows_of = (nv + 1) * W * (al + W * len(faces))
    for out, s_ref, d_ref, at in ((down, s_head, d_head, 0), (up, s_tail, d_tail, W)):
        for f in range(nv + 1):
            rows = slice(f * W * al, (f + 1) * W * al)
            out[rows, :] = s_ref[f] if f < nv else d_ref[...]
            for side, src in enumerate(faces):
                for i in range(W):
                    to = (nv + 1) * W * al + ((side * (nv + 1) + f) * W + i) * W
                    out[to : to + W, :] = src[f, i, at : at + W, :]

    if not dims["ride"]:
        return
    rl = dims["rl"]
    first = span * 2 * rl
    shares = inter_rows(
        dims, [part[...], other[...], before[...]], [first, first + rl, first - rl], donor[...], weight[...]
    )
    lane = lax.broadcasted_iota(jnp.int32, (2 * nh, 128), 1)
    head = tail = jnp.zeros((2 * nh, 128), jnp.float32)
    for v in range(nv):
        inter[v] = shares[v]
        mine = lane // W == v
        head = jnp.where(mine, pltpu.roll(shares[v], W * v, 1), head)
        tail = jnp.where(mine, pltpu.roll(shares[v], (W * v - (sl - W)) % 128, 1), tail)
    down[rows_of:, :] = head
    up[rows_of:, :] = tail


def lane_ids(rows=8):
    return lax.broadcasted_iota(jnp.int32, (rows, 128), 1)


def gather_strips(dims, load, store, tiles):
    nb, ng, br = dims["nb"], dims["ng"], dims["br"]
    group = lane_ids() // 8
    for g in range(ng):
        for t in tiles:
            acc = jnp.zeros((8, 128), jnp.float32)
            for r in range((nb - 1 - g) // ng + 1):
                part = pltpu.roll(load((ng * r + g) * br + 8 * t), (8 * r + 4) % 128, 1)
                acc = jnp.where(group == r, part, acc)
            store(g * br + 8 * t, acc)


def circ_kernel(
    dims, state, dt, lo_edge, hi_edge, lo, hi, below, above, inter, ext, left, right, share, strips
):
    nv, sl, al, cl, br, nb, ng, nh = (dims[k] for k in ("nv", "sl", "al", "cl", "br", "nb", "ng", "nh"))
    axial = lax.axis_index("axial")
    turns = al // 8
    for f in range(nv + 1):
        for s in range(sl):
            for t in range(turns):
                rows = pl.ds(s * al + t, 8, stride=turns)
                at = (s + W) * br + 8 * (t + 1)
                ext[f, at : at + 8, :] = state[f, rows, :] if f < nv else dt[rows, :]

    swap = dims["n_axial"] == 2
    for side, (edge, bulk, valid) in enumerate(
        ((lo_edge, lo, axial > 0), (hi_edge, hi, axial < dims["n_axial"] - 1))
    ):
        base = 0 if side else W

        def fill(edge, bulk, side, base):
            for f in range(nv + 1):
                for i in range(W):
                    part = (nv + 1) * W * al + (((0 if swap else side) * (nv + 1) + f) * W + i) * W
                    pieces = (
                        (0, W, lambda: below[part : part + W, :]),
                        (W, W, lambda: edge[f, i, 0:W]),
                        (2 * W, sl - 2 * W, lambda: bulk[f, i]),
                        (sl, W, lambda: edge[f, i, W:]),
                        (sl + W, W, lambda: above[part : part + W, :]),
                    )
                    for at, n, read in pieces:
                        val = jnp.zeros((n, cl), jnp.float32) if edge is None else read()
                        ext[f, pl.ds(base + at * br + i, n, stride=br), :] = val

        @pl.when(valid)
        def _(edge=edge, bulk=bulk, side=side, base=base):
            fill(edge, bulk, side, base)

        @pl.when(jnp.logical_not(valid))
        def _(side=side, base=base):
            fill(None, None, side, base)

    for f in range(nv + 1):
        for j in range(W):
            for src, b in ((below, j), (above, sl + W + j)):
                for t in range(turns):
                    at = b * br + 8 * (t + 1)
                    ext[f, at : at + 8, :] = src[pl.ds((f * W + j) * al + t, 8, stride=turns), :]

    def each(f, carry):
        def store(row, val):
            strips[f, row : row + 8, :] = val

        gather_strips(dims, lambda row: ext[f, row : row + 8, :], store, range(br // 8))
        return carry

    lax.fori_loop(0, nv + 1, each, 0)
    half = (nv + 1) // 2
    low = lane_ids(ng * br) % 8 < 4
    for f in range(half):
        one, two = strips[f], strips[f + half]
        rows = slice(f * ng * br, (f + 1) * ng * br)
        right[rows, :] = jnp.where(low, one, pltpu.roll(two, 4, 1))
        left[rows, :] = jnp.where(low, pltpu.roll(one, 124, 1), two)

    if not dims["ride"]:
        return
    wide = sl + 2 * W
    lane = lax.broadcasted_iota(jnp.int32, (2 * nh, 128), 1)
    rows = slice((nv + 1) * W * (al + W * (1 if swap else 2)), None)
    packed = [jnp.zeros((2 * nh, 128), jnp.float32)] * dims["packs"]
    for v in range(nv):
        whole = pltpu.roll(inter[v], W, 1)
        whole = jnp.where(lane < W, pltpu.roll(below[rows, :], (-W * v) % 128, 1), whole)
        whole = jnp.where(lane >= sl + W, pltpu.roll(above[rows, :], sl + W - W * v, 1), whole)
        pack, first = divmod(v, 128 // wide)
        first = first * wide
        packed[pack] = jnp.where(
            (lane >= first) & (lane < first + wide), pltpu.roll(whole, first, 1), packed[pack]
        )
    for i in range(dims["packs"]):
        at = half * ng * br + i * 2 * nh
        left[at : at + 2 * nh, :] = packed[i]
        right[at : at + 2 * nh, :] = packed[i]
        share[i * 2 * nh : (i + 1) * 2 * nh, :] = packed[i]


def ghost_table(dims, table, span):
    nv, sl, nh = (dims[k] for k in ("nv", "sl", "nh"))
    rows, width = table.shape
    donors = pltpu.roll(table[rows - 8 :, :], lax.rem(width - span * sl + W, width), 1)[:, :128]
    lane = lax.broadcasted_iota(jnp.int32, (1, 128), 1)
    where = span * sl - W + lane
    inside = (where >= 0) & (where < sl * dims["n_span"]) & (lane < sl + 2 * W)
    station = lax.broadcasted_iota(jnp.int32, (width, 128), 0)
    donor = (donors[0:1, :] + 0.5).astype(jnp.int32)
    weight = donors[1:2, :]
    mix = jnp.where(station == donor, 1.0 - weight, jnp.where(station == donor + 1, weight, 0.0))
    mix = jnp.where(inside, mix, 0.0)
    inter = dot(table[0 : rows - 8, :], mix, ((1,), (0,)))
    return [inter[v * 2 * nh : (v + 1) * 2 * nh, :] for v in range(nv)]


def step_kernel(
    dims, jac, harm, blade, shares, _, from_left, from_right, new, res, ext, new_v, res_v, q_a, q_b, p_0, p_a, p_b, edge, coef, sem
):
    nv, sl, al, cl, br, nb, ng, nh = (dims[k] for k in ("nv", "sl", "al", "cl", "br", "nb", "ng", "nh"))
    axial = lax.axis_index("axial")
    span = lax.axis_index("span")
    circ = lax.axis_index("circ")
    spare = (W - 1) * al
    parts = 4 if sl % 8 == 0 else 1
    for d in range(3):
        for u in range(nv):
            for v in range(nv):
                value = jac[d, u, v] * 0.5 - (DISSIP if u == v else 0.0)
                coef[(d * nv + u) * nv + v] = jnp.full((8, 128), value, jnp.float32)

    half = (nv + 1) // 2
    low = lane_ids(ng * br) % 8 < 4
    for f in range(half):
        rows = slice(f * ng * br, (f + 1) * ng * br)
        one, two = from_left[rows, :], from_right[rows, :]
        p_0[f, br : (ng + 1) * br, :] = jnp.where(low, one, pltpu.roll(two, 4, 1))
        p_0[f + half, br : (ng + 1) * br, :] = jnp.where(low, pltpu.roll(one, 124, 1), two)

    ncells = cl * dims["n_circ"]
    lane = lax.broadcasted_iota(jnp.int32, (1, 128), 1)
    wide = sl + 2 * W
    if dims["ride"]:
        rows = slice(half * ng * br, None)
        packed = from_left[rows, :] + from_right[rows, :] + shares[0][...] + shares[1][...]
        inter = []
        for v in range(nv):
            pack, first = divmod(v, 128 // wide)
            part = pltpu.roll(packed[pack * 2 * nh : (pack + 1) * 2 * nh, :], (-first * wide) % 128, 1)
            inter.append(jnp.where(lane < wide, part, 0.0))
    else:
        inter = ghost_table(dims, shares, span)
    start = circ * cl
    own = make_basis(harm, blade, nh, start + lax.broadcasted_iota(jnp.int32, (1, cl), 1), ncells)
    pos = lane % 8
    halo_cells = lax.rem(start + jnp.where(pos < 4, pos - 4, pos + cl - 4) + ncells, ncells)
    halo = make_basis(harm, blade, nh, halo_cells, ncells)
    s_id = lax.broadcasted_iota(jnp.int32, (128, 128), 0)
    r_id = lax.broadcasted_iota(jnp.int32, (128, 128), 1) // 8

    @pl.when(axial == 0)
    def _():
        for v in range(nv):
            part = inter[v]
            ghost = dot(part, own, ((0,), (0,)))
            ext[v, pl.ds(7, sl + 2 * W, stride=br), :] = ghost[: sl + 2 * W, :]
            ghost = dot(part, halo, ((0,), (0,)))
            for g in range(ng):
                picked = jnp.where(s_id == ng * r_id + g, ghost, 0.0)
                at = (g + 1) * br + 7
                p_0[v, at : at + 1, :] = jnp.sum(picked, axis=0, keepdims=True)

    lanes = lane_ids()
    first_lane, last_lane = lanes == 0, lanes == 127
    pos3, pos4 = lanes % 8 == 3, lanes % 8 == 4
    last = (ng + 1) * br

    def apply(cells):
        for c in cells:
            c["diff"] = [
                [plus - minus for plus, minus in zip(c[d + "+"], c[d + "-"])] for d in ("axial", "span", "theta")
            ]
            c["rest"] = [
                (2.0 * DISSIP) * (3.0 * q - (x + y + z))
                for q, x, y, z in zip(c["q"], c["axial-"], c["span-"], c["theta-"])
            ]
        out = [[None] * nv for _ in cells]
        for first in range(0, nv, 2):
            some = range(first, min(first + 2, nv))
            sums = {}
            for v in range(nv):
                for d in range(3):
                    for u in some:
                        k = coef[(d * nv + u) * nv + v]
                        for i, c in enumerate(cells):
                            term = k * c["diff"][d][v]
                            sums[i, u, d] = sums[i, u, d] + term if v else term
            for u in some:
                for i, c in enumerate(cells):
                    out[i][u] = (sums[i, u, 0] + sums[i, u, 1]) + (sums[i, u, 2] + c["rest"][u])
        return out

    turns = al // 8
    sub = lax.broadcasted_iota(jnp.int32, (8, 128), 0)
    top, bottom = sub == 0, sub == 7

    def block_cells(view, at):
        memo = {}

        def load(t, off=0):
            if (t, off) not in memo:
                row = at + off + 8 * t
                memo[t, off] = [view[v, row : row + 8, :] for v in range(nv)]
            return memo[t, off]

        def rolled(t, amount):
            if (t, "roll", amount) not in memo:
                memo[t, "roll", amount] = [pltpu.roll(x, amount, 0) for x in load(t)]
            return memo[t, "roll", amount]

        def choose(mask, one, two):
            return [jnp.where(mask, x, y) for x, y in zip(one, two)]

        def values(t):
            if t == 0:
                plus = choose(bottom, rolled(1, 7), rolled(0, 7))
                minus = choose(top, rolled(turns, 1), rolled(0, 1))
            else:
                plus = load(t + 1) if t < turns else choose(bottom, rolled(0, 7), rolled(1, 7))
                minus = load(t - 1) if t > 1 else choose(top, rolled(0, 1), rolled(turns, 1))
            return {"q": load(t), "axial-": minus, "axial+": plus, "span-": load(t, -br), "span+": load(t, br)}

        return values

    def turn(cell, beyond, at_plus, at_minus):
        cell["theta+"] = [
            pltpu.roll(jnp.where(at_plus, z, q), 127, 1) for z, q in zip(beyond, cell["q"])
        ]
        cell["theta-"] = [pltpu.roll(jnp.where(at_minus, z, q), 1, 1) for z, q in zip(beyond, cell["q"])]

    writes = [pltpu.make_async_copy(res_v.at[:, pl.ds(spare, sl * al), :], res, sem.at[0])]

    def stage(number, src, p_src, dst, p_dst):
        width = W - 1 - number
        factor = SEGMENT_COEF[number]
        final = number == len(SEGMENT_COEF) - 1
        for v in range(nv):
            p_src[v, 0:br, :] = pltpu.roll(p_src[v, last - br : last, :], 8, 1)
            p_src[v, last : last + br, :] = pltpu.roll(p_src[v, br : 2 * br, :], 120, 1)

        def blocks(b, count, first):
            around = pl.multiple_of((b - 1) * br, 8)
            view = src.at[:, pl.ds(around, (count + 2) * br), :]
            values = [block_cells(view, (i + 1) * br) for i in range(count)]
            groups = [[(i, t) for t in range(1, turns + 1)] for i in range(count)]
            if first == 0:
                groups.append([(i, 0) for i in range(count)])

            def prepare(group):
                cells = []
                for i, t in group:
                    r = (b + i) // ng
                    g = b + i - r * ng
                    p_row = pl.multiple_of((g + 1) * br, 8) + 8 * t
                    row = pl.multiple_of((b + i) * br, 8) + 8 * t
                    cell = values[i](t)
                    beyond = [pltpu.roll(p_src[v, pl.ds(p_row, 8), :], 124 - 8 * r, 1) for v in range(nv)]
                    turn(cell, beyond, first_lane, last_lane)
                    cell["base"] = [ext[u, pl.ds(row, 8), :] for u in range(nv)] if number else cell["q"]
                    cell["step"] = factor * ext[nv, pl.ds(row, 8), :]
                    cells.append(cell)
                return cells

            cells = prepare(groups[0])
            for n, group in enumerate(groups):
                following = prepare(groups[n + 1]) if n + 1 < len(groups) else None
                results = apply(cells)
                for (i, t), cell, result in zip(group, cells, results):
                    row = pl.multiple_of((b + i) * br, 8) + 8 * t
                    for u in range(nv):
                        value = cell["base"][u] - cell["step"] * result[u]
                        if final:
                            rows = pl.ds(pl.multiple_of((b + i - W) * al, 8) + t - 1, 8, stride=turns)
                            new_v[u, rows, :] = value
                        else:
                            dst[u, pl.ds(row, 8), :] = value
                            if t > 0 and number == 0:
                                rows = pl.ds(pl.multiple_of((b + i - 1) * al, 8) + t - 1, 8, stride=turns)
                                res_v[u, rows, :] = result[u]
                cells = following

        def run(start, count, first):
            def loop(j, carry):
                blocks(start + 2 * j, 2, first)
                return carry

            lax.fori_loop(0, count // 2, loop, 0)
            if count % 2:
                blocks(start + count - 1, 1, first)

        if final:
            for i in range(parts):
                run(W + i * (sl // parts), sl // parts, 1)
                rows = pl.ds(i * (sl // parts) * al, sl // parts * al)
                copy = pltpu.make_async_copy(new_v.at[:, rows, :], new.at[:, rows, :], sem.at[i + 1])
                copy.start()
                writes.append(copy)
        else:
            run(W - width, sl + 2 * width, 0)
        if number == 0:
            writes[0].start()
        if final:
            return

        def edges(v, carry):
            def store(row, val):
                edge[v, row : row + 8, :] = val

            gather_strips(dims, lambda row: src[v, row : row + 8, :], store, range(br // 8))
            return carry

        lax.fori_loop(0, nv, edges, 0)

        def strip(g, carry):
            base = pl.multiple_of((g + 1) * br, 8)
            around = pl.multiple_of(g * br, 8)
            view = p_src.at[:, pl.ds(around, 3 * br), :]

            values = block_cells(view, br)
            for t in range(br // 8):
                cell = values(t)
                turn(cell, [edge[v, pl.ds(around + 8 * t, 8), :] for v in range(nv)], pos4, pos3)
                (result,) = apply([cell])
                step = factor * p_0[nv, pl.ds(base + 8 * t, 8), :]
                for u in range(nv):
                    p_dst[u, pl.ds(base + 8 * t, 8), :] = p_0[u, pl.ds(base + 8 * t, 8), :] - step * result[u]
            return carry

        lax.fori_loop(0, ng, strip, 0)

    stage(0, ext, p_0, q_a, p_a)
    stage(1, q_a, p_a, q_b, p_b)
    stage(2, q_b, p_b, q_a, p_a)
    stage(3, q_a, p_a, None, None)
    for copy in writes:
        copy.wait()


def shift_pairs(count, step, closed):
    return [(i, (i + step) % count) for i in range(count) if closed or 0 <= i + step < count]


def coef_table(part, donor_index, donor_weight, rl, nv, sizes):
    n_circ, n_span, n_axial = sizes
    modes, sl = part.shape[0], donor_index.shape[0]
    width = -(-max(rl * n_span * n_axial, sl * n_span) // 128) * 128
    circ, span, axial = (lax.axis_index(a) for a in AXES)
    rows = part[:, : nv * rl].reshape(modes, nv, rl).transpose(1, 0, 2).reshape(nv * modes, rl)
    table = jnp.zeros((nv * modes + 8, width), jnp.float32)
    table = lax.dynamic_update_slice(table, rows, (0, (span * n_axial + axial) * rl))
    donors = jnp.stack([donor_index.astype(jnp.float32), donor_weight])
    donors = jnp.where((circ == 0) & (axial == 0), donors, 0.0)
    table = lax.dynamic_update_slice(table, donors, (nv * modes, span * sl))
    return lax.psum(table, AXES)


def local(rotor_outlet, blade_count, harmonic_list, donor_index, donor_weight, state, time_step, flux_jacobian):
    f32 = jnp.float32
    n_circ, n_span, n_axial = (lax.axis_size(a) for a in AXES)
    nv, sl, al, cl = state.shape
    br = al + 2 * W
    nb = sl + 2 * W
    ng = -(-nb // 16)
    nh = harmonic_list.shape[0]
    dims = dict(
        nv=nv, sl=sl, al=al, cl=cl, br=br, nb=nb, ng=ng, nh=nh, n_circ=n_circ, n_span=n_span, n_axial=n_axial
    )
    rl = rotor_outlet.shape[1]
    packs = -(-nv // (128 // (sl + 2 * W)))
    ride = n_axial == 2 and n_circ == 4 and nv * rl <= 128
    dims.update(rl=rl, packs=packs, ride=ride)
    params = pltpu.CompilerParams(vmem_limit_bytes=48 * 2**20)
    sides = 1 if n_axial == 2 else 2
    deep = 8 if n_axial == 2 else al

    edge, bulk, part = pl.pallas_call(
        functools.partial(axial_kernel, dims),
        out_shape=[
            jax.ShapeDtypeStruct((sides, nv + 1, W, 2 * W, cl), f32),
            jax.ShapeDtypeStruct((sides, nv + 1, W, sl - 2 * W, cl), f32),
            jax.ShapeDtypeStruct((2 * nh, -(-nv * rl // 128) * 128), f32),
        ],
        in_specs=[HBM] * 5,
        out_specs=[VMEM] * 3,
        scratch_shapes=[
            pltpu.VMEM((nv, sl, deep, cl), f32),
            pltpu.VMEM((sl, deep, cl), f32),
            pltpu.VMEM(rotor_outlet.shape, f32),
            pltpu.SMEM(blade_count.shape, jnp.int32),
            pltpu.SMEM(harmonic_list.shape, jnp.int32),
            pltpu.SemaphoreType.DMA((5,)),
        ],
        compiler_params=pltpu.CompilerParams(vmem_limit_bytes=63 * 2**20),
        name="axial_faces",
    )(state, time_step, rotor_outlet, blade_count, harmonic_list)
    state = state.reshape(nv, sl * al, cl)
    time_step = time_step.reshape(sl * al, cl)

    def axial_move(faces):
        if n_axial == 2:
            moved = lax.ppermute(faces[0], "axial", [(0, 1), (1, 0)])
            return moved, moved
        lo = lax.ppermute(faces[0], "axial", shift_pairs(n_axial, 1, False))
        hi = lax.ppermute(faces[1], "axial", shift_pairs(n_axial, -1, False))
        return lo, hi

    lo_edge, hi_edge = axial_move(edge)
    if ride:
        other = lax.ppermute(part, "axial", [(0, 1), (1, 0)])
        before = lax.ppermute(part, ("span", "axial"), shift_pairs(n_span * n_axial, 1, False))
        shares = None
    else:
        other = before = part
        shares = coef_table(part, donor_index, donor_weight, rl, nv, (n_circ, n_span, n_axial))
    lo, hi = axial_move(bulk)

    def spec(shape, *index):
        index = index or (0,) * len(shape)
        return pl.BlockSpec(shape, lambda i: index)

    faces = (nv + 1, W, 2 * W, cl)
    message = ((nv + 1) * W * (al + W * sides) + (2 * nh if ride else 0), cl)
    end = sl // W - 1
    pad = lambda x: jnp.pad(x, (0, 128 - sl))[None]
    down, up, inter = pl.pallas_call(
        functools.partial(span_kernel, dims),
        grid=(1,),
        out_shape=[jax.ShapeDtypeStruct(message, f32)] * 2 + [jax.ShapeDtypeStruct((nv, 2 * nh, 128), f32)],
        in_specs=[
            spec((nv, W * al, cl)),
            spec((nv, W * al, cl), 0, end, 0),
            spec((W * al, cl)),
            spec((W * al, cl), end, 0),
            spec(faces),
            spec(faces),
            spec(part.shape),
            spec(part.shape),
            spec(part.shape),
            spec((1, 128)),
            spec((1, 128)),
        ],
        out_specs=[spec(message), spec(message), spec((nv, 2 * nh, 128))],
        compiler_params=params,
        name="span_faces",
    )(
        state, state, time_step, time_step, lo_edge, hi_edge, part, other, before, pad(donor_index), pad(donor_weight)
    )
    below = lax.ppermute(up, "span", shift_pairs(n_span, 1, False))
    above = lax.ppermute(down, "span", shift_pairs(n_span, -1, False))

    strip = jax.ShapeDtypeStruct(((nv + 1) // 2 * ng * br + (packs * 2 * nh if ride else 0), 128), f32)
    ext, left, right, share = pl.pallas_call(
        functools.partial(circ_kernel, dims),
        out_shape=[
            jax.ShapeDtypeStruct((nv + 1, nb * br, cl), f32),
            strip,
            strip,
            jax.ShapeDtypeStruct((packs * 2 * nh, 128), f32),
        ],
        in_specs=[VMEM] * 9,
        out_specs=[VMEM] * 4,
        scratch_shapes=[pltpu.VMEM((nv + 1, ng * br, 128), f32)],
        compiler_params=params,
        name="circ_faces",
    )(state, time_step, lo_edge, hi_edge, lo, hi, below, above, inter)
    from_left = lax.ppermute(right, "circ", shift_pairs(n_circ, 1, True))
    from_right = lax.ppermute(left, "circ", shift_pairs(n_circ, -1, True))
    if ride:
        shares = [share, lax.ppermute(share, "circ", shift_pairs(n_circ, 2, True))]

    block = jax.ShapeDtypeStruct((nv, sl * al, cl), f32)
    field = pltpu.VMEM((nv, nb * br, cl), f32)
    strips = pltpu.VMEM((nv, (ng + 2) * br, 128), f32)
    new, res, _ = pl.pallas_call(
        functools.partial(step_kernel, dims),
        out_shape=[block, block, jax.ShapeDtypeStruct(ext.shape, f32)],
        in_specs=[SMEM, SMEM, SMEM, [VMEM, VMEM] if ride else VMEM, VMEM, VMEM, VMEM],
        out_specs=[HBM, HBM, VMEM],
        input_output_aliases={(5 if ride else 4): 2},
        scratch_shapes=[
            pltpu.VMEM((nv, sl * al, cl), f32),
            pltpu.VMEM((nv, (sl + 2 * W - 2) * al, cl), f32),
            field,
            field,
            pltpu.VMEM((nv + 1, (ng + 2) * br, 128), f32),
            strips,
            strips,
            pltpu.VMEM((nv, ng * br, 128), f32),
            pltpu.VMEM((3 * nv * nv, 8, 128), f32),
            pltpu.SemaphoreType.DMA((5,)),
        ],
        compiler_params=params,
        name="segments",
    )(flux_jacobian, harmonic_list, blade_count, shares, ext, from_left, from_right)
    return new.reshape(nv, sl, al, cl), res.reshape(nv, sl, al, cl)


def solution(mesh):
    return jax.shard_map(
        local,
        mesh=mesh,
        in_specs=(
            P(None, ("span", "axial"), "circ"),
            P(),
            P(),
            P("span"),
            P("span"),
            P(None, "span", "axial", "circ"),
            P("span", "axial", "circ"),
            P(),
        ),
        out_specs=(P(None, "span", "axial", "circ"), P(None, "span", "axial", "circ")),
        check_vma=False,
    )
```

```python
import functools

import jax
import jax.numpy as jnp
import numpy as np
from jax import lax
from jax.experimental import pallas as pl
from jax.experimental.pallas import tpu as pltpu
from jax.sharding import PartitionSpec as P

SEGMENT_COEF = (0.25, 1.0 / 3.0, 0.5, 1.0)
DISSIP = 0.2
W = 4
HIGH = lax.Precision.HIGHEST
VMEM = pl.BlockSpec(memory_space=pltpu.VMEM)
SMEM = pl.BlockSpec(memory_space=pltpu.SMEM)
HBM = pl.BlockSpec(memory_space=pltpu.HBM)
ANY = pl.BlockSpec(memory_space=pl.ANY)
AXES = ("circ", "span", "axial")


def make_basis(harm, blade, nh, cells, ncells):
    width = cells.shape[1]
    row = lax.broadcasted_iota(jnp.int32, (nh, width), 0)
    waves = jnp.zeros((nh, width), jnp.int32)
    for k in range(nh):
        waves = jnp.where(row == k, harm[k] * blade[0], waves)
    phase = waves * cells
    phase = phase & (ncells - 1) if ncells & (ncells - 1) == 0 else phase % ncells
    angle = (2.0 * np.pi) * phase.astype(jnp.float32) / ncells
    return jnp.concatenate([jnp.cos(angle), jnp.sin(angle)], axis=0)


def dot(a, b, dims):
    return lax.dot_general(a, b, (dims, ((), ())), precision=HIGH, preferred_element_type=jnp.float32)


def axial_kernel(dims, state, dt, rotor, blade, harm, edge, bulk, part, *scratch):
    nv, sl, al, cl, nh = (dims[k] for k in ("nv", "sl", "al", "cl", "nh"))
    cells, dt_cells, rotor_v, blade_s, harm_s, sems = scratch
    axial = lax.axis_index("axial")
    circ = lax.axis_index("circ")
    swap = dims["n_axial"] == 2
    size = cells.shape[2]
    at = pl.multiple_of(jnp.where(axial == 0, al - size, 0), 8) if swap else 0
    copies = [
        pltpu.make_async_copy(state.at[:, :, pl.ds(at, size), :], cells, sems.at[0]),
        pltpu.make_async_copy(dt.at[:, pl.ds(at, size), :], dt_cells, sems.at[1]),
        pltpu.make_async_copy(rotor, rotor_v, sems.at[2]),
        pltpu.make_async_copy(blade, blade_s, sems.at[3]),
        pltpu.make_async_copy(harm, harm_s, sems.at[4]),
    ]
    for copy in copies:
        copy.start()
    for copy in copies[2:]:
        copy.wait()
    ncells = cl * dims["n_circ"]
    here = circ * cl + lax.broadcasted_iota(jnp.int32, (1, cl), 1)
    basis = make_basis(harm_s, blade_s, nh, here, ncells)
    rl = rotor_v.shape[1]
    flat = rotor_v[...].reshape(nv * rl, cl)
    part[...] = jnp.zeros_like(part)
    part[:, : nv * rl] = dot(basis, flat, ((1,), (1,))) * (2.0 / ncells)
    for copy in copies[:2]:
        copy.wait()

    def put(side, base):
        for f in range(nv + 1):
            for i in range(W):
                ref = cells.at[f] if f < nv else dt_cells
                rows = ref[:, base + i, :]
                edge[side, f, i, 0:W] = rows[0:W]
                edge[side, f, i, W:] = rows[sl - W :]
                bulk[side, f, i] = rows[W : sl - W]

    if swap:

        @pl.when(axial == 0)
        def _():
            put(0, size - W)

        @pl.when(axial != 0)
        def _():
            put(0, 0)

    else:
        put(0, size - W)
        put(1, 0)


def inter_rows(dims, parts, firsts, donor, weight):
    nv = dims["nv"]
    rl = dims["rl"]
    table = jnp.concatenate([p[:, : nv * rl] for p in parts], axis=1)
    rows = table.shape[1]
    row = lax.broadcasted_iota(jnp.int32, (rows, 128), 0)
    station = row % rl
    for i, first in enumerate(firsts):
        station = station + jnp.where(row // (nv * rl) == i, first, 0)
    mix = jnp.where(station == donor, 1.0 - weight, jnp.where(station == donor + 1, weight, 0.0))
    var = row // rl % nv
    return [dot(table, jnp.where(var == v, mix, 0.0), ((1,), (0,))) for v in range(nv)]


def span_kernel(dims, s_head, s_tail, d_head, d_tail, lo, hi, part, other, before, donor, weight, down, up, inter):
    nv, sl, al, cl, br, nh = (dims[k] for k in ("nv", "sl", "al", "cl", "br", "nh"))
    span = lax.axis_index("span")
    faces = (lo,) if dims["n_axial"] == 2 else (lo, hi)
    rows_of = (nv + 1) * W * (al + W * len(faces))
    for out, s_ref, d_ref, at in ((down, s_head, d_head, 0), (up, s_tail, d_tail, W)):
        for f in range(nv + 1):
            rows = slice(f * W * al, (f + 1) * W * al)
            out[rows, :] = s_ref[f] if f < nv else d_ref[...]
            for side, src in enumerate(faces):
                for i in range(W):
                    to = (nv + 1) * W * al + ((side * (nv + 1) + f) * W + i) * W
                    out[to : to + W, :] = src[f, i, at : at + W, :]

    if not dims["ride"]:
        return
    rl = dims["rl"]
    first = span * 2 * rl
    shares = inter_rows(
        dims, [part[...], other[...], before[...]], [first, first + rl, first - rl], donor[...], weight[...]
    )
    lane = lax.broadcasted_iota(jnp.int32, (2 * nh, 128), 1)
    head = tail = jnp.zeros((2 * nh, 128), jnp.float32)
    for v in range(nv):
        inter[v] = shares[v]
        mine = lane // W == v
        head = jnp.where(mine, pltpu.roll(shares[v], W * v, 1), head)
        tail = jnp.where(mine, pltpu.roll(shares[v], (W * v - (sl - W)) % 128, 1), tail)
    down[rows_of:, :] = head
    up[rows_of:, :] = tail


def lane_ids(rows=8):
    return lax.broadcasted_iota(jnp.int32, (rows, 128), 1)


def gather_strips(dims, load, store, tiles):
    nb, ng, br = dims["nb"], dims["ng"], dims["br"]
    group = lane_ids() // 8
    for g in range(ng):
        for t in tiles:
            acc = jnp.zeros((8, 128), jnp.float32)
            for r in range((nb - 1 - g) // ng + 1):
                part = pltpu.roll(load((ng * r + g) * br + 8 * t), (8 * r + 4) % 128, 1)
                acc = jnp.where(group == r, part, acc)
            store(g * br + 8 * t, acc)


def circ_kernel(
    dims, state, dt, lo_edge, hi_edge, lo, hi, below, above, inter, ext, left, right, share, strips
):
    nv, sl, al, cl, br, nb, ng, nh = (dims[k] for k in ("nv", "sl", "al", "cl", "br", "nb", "ng", "nh"))
    axial = lax.axis_index("axial")
    turns = al // 8
    for f in range(nv + 1):
        for s in range(sl):
            for t in range(turns):
                rows = pl.ds(s * al + t, 8, stride=turns)
                at = (s + W) * br + 8 * (t + 1)
                ext[f, at : at + 8, :] = state[f, rows, :] if f < nv else dt[rows, :]

    swap = dims["n_axial"] == 2
    for side, (edge, bulk, valid) in enumerate(
        ((lo_edge, lo, axial > 0), (hi_edge, hi, axial < dims["n_axial"] - 1))
    ):
        base = 0 if side else W

        def fill(edge, bulk, side, base):
            for f in range(nv + 1):
                for i in range(W):
                    part = (nv + 1) * W * al + (((0 if swap else side) * (nv + 1) + f) * W + i) * W
                    pieces = (
                        (0, W, lambda: below[part : part + W, :]),
                        (W, W, lambda: edge[f, i, 0:W]),
                        (2 * W, sl - 2 * W, lambda: bulk[f, i]),
                        (sl, W, lambda: edge[f, i, W:]),
                        (sl + W, W, lambda: above[part : part + W, :]),
                    )
                    for at, n, read in pieces:
                        val = jnp.zeros((n, cl), jnp.float32) if edge is None else read()
                        ext[f, pl.ds(base + at * br + i, n, stride=br), :] = val

        @pl.when(valid)
        def _(edge=edge, bulk=bulk, side=side, base=base):
            fill(edge, bulk, side, base)

        @pl.when(jnp.logical_not(valid))
        def _(side=side, base=base):
            fill(None, None, side, base)

    for f in range(nv + 1):
        for j in range(W):
            for src, b in ((below, j), (above, sl + W + j)):
                for t in range(turns):
                    at = b * br + 8 * (t + 1)
                    ext[f, at : at + 8, :] = src[pl.ds((f * W + j) * al + t, 8, stride=turns), :]

    def each(f, carry):
        def store(row, val):
            strips[f, row : row + 8, :] = val

        gather_strips(dims, lambda row: ext[f, row : row + 8, :], store, range(br // 8))
        return carry

    lax.fori_loop(0, nv + 1, each, 0)
    half = (nv + 1) // 2
    low = lane_ids(ng * br) % 8 < 4
    for f in range(half):
        one, two = strips[f], strips[f + half]
        rows = slice(f * ng * br, (f + 1) * ng * br)
        right[rows, :] = jnp.where(low, one, pltpu.roll(two, 4, 1))
        left[rows, :] = jnp.where(low, pltpu.roll(one, 124, 1), two)

    if not dims["ride"]:
        return
    wide = sl + 2 * W
    lane = lax.broadcasted_iota(jnp.int32, (2 * nh, 128), 1)
    rows = slice((nv + 1) * W * (al + W * (1 if swap else 2)), None)
    packed = [jnp.zeros((2 * nh, 128), jnp.float32)] * dims["packs"]
    for v in range(nv):
        whole = pltpu.roll(inter[v], W, 1)
        whole = jnp.where(lane < W, pltpu.roll(below[rows, :], (-W * v) % 128, 1), whole)
        whole = jnp.where(lane >= sl + W, pltpu.roll(above[rows, :], sl + W - W * v, 1), whole)
        pack, first = divmod(v, 128 // wide)
        first = first * wide
        packed[pack] = jnp.where(
            (lane >= first) & (lane < first + wide), pltpu.roll(whole, first, 1), packed[pack]
        )
    for i in range(dims["packs"]):
        at = half * ng * br + i * 2 * nh
        left[at : at + 2 * nh, :] = packed[i]
        right[at : at + 2 * nh, :] = packed[i]
        share[i * 2 * nh : (i + 1) * 2 * nh, :] = packed[i]


def ghost_table(dims, table, span):
    nv, sl, nh = (dims[k] for k in ("nv", "sl", "nh"))
    rows, width = table.shape
    donors = pltpu.roll(table[rows - 8 :, :], lax.rem(width - span * sl + W, width), 1)[:, :128]
    lane = lax.broadcasted_iota(jnp.int32, (1, 128), 1)
    where = span * sl - W + lane
    inside = (where >= 0) & (where < sl * dims["n_span"]) & (lane < sl + 2 * W)
    station = lax.broadcasted_iota(jnp.int32, (width, 128), 0)
    donor = (donors[0:1, :] + 0.5).astype(jnp.int32)
    weight = donors[1:2, :]
    mix = jnp.where(station == donor, 1.0 - weight, jnp.where(station == donor + 1, weight, 0.0))
    mix = jnp.where(inside, mix, 0.0)
    inter = dot(table[0 : rows - 8, :], mix, ((1,), (0,)))
    return [inter[v * 2 * nh : (v + 1) * 2 * nh, :] for v in range(nv)]


def step_kernel(
    dims, jac, harm, blade, shares, _, from_left, from_right, new, res, ext, new_v, res_v, q_a, q_b, p_0, p_a, p_b, edge, coef, sem
):
    nv, sl, al, cl, br, nb, ng, nh = (dims[k] for k in ("nv", "sl", "al", "cl", "br", "nb", "ng", "nh"))
    axial = lax.axis_index("axial")
    span = lax.axis_index("span")
    circ = lax.axis_index("circ")
    spare = (W - 1) * al
    parts = 4 if sl % 8 == 0 else 1
    blocks_of = -(-3 * nv // 16) * 16
    lane = lax.broadcasted_iota(jnp.int32, (8, 8 * blocks_of), 1)
    row = lax.broadcasted_iota(jnp.int32, (8, 8 * blocks_of), 0)
    matrix = []
    for u in range(nv):
        part = jnp.zeros((8, 8 * blocks_of), jnp.float32)
        for d in range(3):
            for v in range(nv):
                value = (jac[d, u, v] * 0.5 - (DISSIP if u == v else 0.0)) * (0.5 / DISSIP)
                part = jnp.where(lane == row + 8 * (d * nv + v), value, part)
        matrix.append(part)
    matrix = jnp.concatenate(matrix, axis=0)
    high = matrix.astype(jnp.bfloat16).astype(jnp.float32)
    again = jnp.concatenate([matrix - high, jnp.zeros_like(high)], axis=1)
    coef[...] = jnp.concatenate([jnp.concatenate([high, high], axis=1), again], axis=0).astype(jnp.bfloat16)

    half = (nv + 1) // 2
    low = lane_ids(ng * br) % 8 < 4
    for f in range(half):
        rows = slice(f * ng * br, (f + 1) * ng * br)
        one, two = from_left[rows, :], from_right[rows, :]
        p_0[f, br : (ng + 1) * br, :] = jnp.where(low, one, pltpu.roll(two, 4, 1))
        p_0[f + half, br : (ng + 1) * br, :] = jnp.where(low, pltpu.roll(one, 124, 1), two)

    ncells = cl * dims["n_circ"]
    lane = lax.broadcasted_iota(jnp.int32, (1, 128), 1)
    wide = sl + 2 * W
    if dims["ride"]:
        rows = slice(half * ng * br, None)
        packed = from_left[rows, :] + from_right[rows, :] + shares[0][...] + shares[1][...]
        inter = []
        for v in range(nv):
            pack, first = divmod(v, 128 // wide)
            part = pltpu.roll(packed[pack * 2 * nh : (pack + 1) * 2 * nh, :], (-first * wide) % 128, 1)
            inter.append(jnp.where(lane < wide, part, 0.0))
    else:
        inter = ghost_table(dims, shares, span)
    start = circ * cl
    own = make_basis(harm, blade, nh, start + lax.broadcasted_iota(jnp.int32, (1, cl), 1), ncells)
    pos = lane % 8
    halo_cells = lax.rem(start + jnp.where(pos < 4, pos - 4, pos + cl - 4) + ncells, ncells)
    halo = make_basis(harm, blade, nh, halo_cells, ncells)
    s_id = lax.broadcasted_iota(jnp.int32, (128, 128), 0)
    r_id = lax.broadcasted_iota(jnp.int32, (128, 128), 1) // 8

    @pl.when(axial == 0)
    def _():
        for v in range(nv):
            part = inter[v]
            ghost = dot(part, own, ((0,), (0,)))
            ext[v, pl.ds(7, sl + 2 * W, stride=br), :] = ghost[: sl + 2 * W, :]
            ghost = dot(part, halo, ((0,), (0,)))
            for g in range(ng):
                picked = jnp.where(s_id == ng * r_id + g, ghost, 0.0)
                at = (g + 1) * br + 7
                p_0[v, at : at + 1, :] = jnp.sum(picked, axis=0, keepdims=True)

    lanes = lane_ids()
    first_lane, last_lane = lanes == 0, lanes == 127
    pos3, pos4 = lanes % 8 == 3, lanes % 8 == 4
    last = (ng + 1) * br

    def apply(cells):
        def beside(name):
            return [jnp.concatenate(parts, axis=1) for parts in zip(*(c[name] for c in cells))]

        both = {name: beside(name) for name in cells[0] if name[-1] in "+-q"}
        diff = [p - m for d in ("axial", "span", "theta") for p, m in zip(both[d + "+"], both[d + "-"])]
        diff += [jnp.zeros_like(diff[0])] * (blocks_of - len(diff))
        diff = jnp.concatenate(diff, axis=0)
        high = diff.astype(jnp.bfloat16)
        low = (diff - high.astype(jnp.float32)).astype(jnp.bfloat16)
        product = jnp.dot(
            coef[...], jnp.concatenate([high, low], axis=0), preferred_element_type=jnp.float32
        )
        out = [[None] * nv for _ in cells]
        for u in range(nv):
            rest = 3.0 * both["q"][u] - (both["axial-"][u] + both["span-"][u] + both["theta-"][u])
            total = product[8 * u : 8 * u + 8] + (product[8 * (nv + u) : 8 * (nv + u) + 8] + rest)
            for i in range(len(cells)):
                out[i][u] = total[:, 128 * i : 128 * i + 128]
        return out

    turns = al // 8
    sub = lax.broadcasted_iota(jnp.int32, (8, 128), 0)
    top, bottom = sub == 0, sub == 7

    def block_cells(view, at):
        memo = {}

        def load(t, off=0):
            if (t, off) not in memo:
                row = at + off + 8 * t
                memo[t, off] = [view[v, row : row + 8, :] for v in range(nv)]
            return memo[t, off]

        def rolled(t, amount):
            if (t, "roll", amount) not in memo:
                memo[t, "roll", amount] = [pltpu.roll(x, amount, 0) for x in load(t)]
            return memo[t, "roll", amount]

        def choose(mask, one, two):
            return [jnp.where(mask, x, y) for x, y in zip(one, two)]

        def values(t):
            if t == 0:
                plus = choose(bottom, rolled(1, 7), rolled(0, 7))
                minus = choose(top, rolled(turns, 1), rolled(0, 1))
            else:
                plus = load(t + 1) if t < turns else choose(bottom, rolled(0, 7), rolled(1, 7))
                minus = load(t - 1) if t > 1 else choose(top, rolled(0, 1), rolled(turns, 1))
            return {"q": load(t), "axial-": minus, "axial+": plus, "span-": load(t, -br), "span+": load(t, br)}

        return values

    def turn(cell, beyond, at_plus, at_minus):
        cell["theta+"] = [
            pltpu.roll(jnp.where(at_plus, z, q), 127, 1) for z, q in zip(beyond, cell["q"])
        ]
        cell["theta-"] = [pltpu.roll(jnp.where(at_minus, z, q), 1, 1) for z, q in zip(beyond, cell["q"])]

    writes = [pltpu.make_async_copy(res_v.at[:, pl.ds(spare, sl * al), :], res, sem.at[0])]

    def stage(number, src, p_src, dst, p_dst):
        width = W - 1 - number
        factor = SEGMENT_COEF[number]
        final = number == len(SEGMENT_COEF) - 1
        for v in range(nv):
            p_src[v, 0:br, :] = pltpu.roll(p_src[v, last - br : last, :], 8, 1)
            p_src[v, last : last + br, :] = pltpu.roll(p_src[v, br : 2 * br, :], 120, 1)

        def blocks(b, count, first):
            around = pl.multiple_of((b - 1) * br, 8)
            view = src.at[:, pl.ds(around, (count + 2) * br), :]
            values = [block_cells(view, (i + 1) * br) for i in range(count)]
            groups = [[(i, t) for t in range(1, turns + 1)] for i in range(count)]
            if first == 0:
                groups.append([(i, 0) for i in range(count)])

            def prepare(group):
                cells = []
                for i, t in group:
                    r = (b + i) // ng
                    g = b + i - r * ng
                    p_row = pl.multiple_of((g + 1) * br, 8) + 8 * t
                    row = pl.multiple_of((b + i) * br, 8) + 8 * t
                    cell = values[i](t)
                    beyond = [pltpu.roll(p_src[v, pl.ds(p_row, 8), :], 124 - 8 * r, 1) for v in range(nv)]
                    turn(cell, beyond, first_lane, last_lane)
                    cell["base"] = [ext[u, pl.ds(row, 8), :] for u in range(nv)] if number else cell["q"]
                    cell["step"] = (2.0 * DISSIP * factor) * ext[nv, pl.ds(row, 8), :]
                    cells.append(cell)
                return cells

            cells = prepare(groups[0])
            for n, group in enumerate(groups):
                following = prepare(groups[n + 1]) if n + 1 < len(groups) else None
                results = apply(cells)
                for (i, t), cell, result in zip(group, cells, results):
                    row = pl.multiple_of((b + i) * br, 8) + 8 * t
                    for u in range(nv):
                        value = cell["base"][u] - cell["step"] * result[u]
                        if final:
                            rows = pl.ds(pl.multiple_of((b + i - W) * al, 8) + t - 1, 8, stride=turns)
                            new_v[u, rows, :] = value
                        else:
                            dst[u, pl.ds(row, 8), :] = value
                            if t > 0 and number == 0:
                                rows = pl.ds(pl.multiple_of((b + i - 1) * al, 8) + t - 1, 8, stride=turns)
                                res_v[u, rows, :] = (2.0 * DISSIP) * result[u]
                cells = following

        def run(start, count, first):
            def loop(j, carry):
                blocks(start + 2 * j, 2, first)
                return carry

            lax.fori_loop(0, count // 2, loop, 0)
            if count % 2:
                blocks(start + count - 1, 1, first)

        if final:
            for i in range(parts):
                run(W + i * (sl // parts), sl // parts, 1)
                rows = pl.ds(i * (sl // parts) * al, sl // parts * al)
                copy = pltpu.make_async_copy(new_v.at[:, rows, :], new.at[:, rows, :], sem.at[i + 1])
                copy.start()
                writes.append(copy)
        else:
            run(W - width, sl + 2 * width, 0)
        if number == 0:
            writes[0].start()
        if final:
            return

        def edges(v, carry):
            def store(row, val):
                edge[v, row : row + 8, :] = val

            gather_strips(dims, lambda row: src[v, row : row + 8, :], store, range(br // 8))
            return carry

        lax.fori_loop(0, nv, edges, 0)

        def strip(g, carry):
            base = pl.multiple_of((g + 1) * br, 8)
            around = pl.multiple_of(g * br, 8)
            view = p_src.at[:, pl.ds(around, 3 * br), :]

            values = block_cells(view, br)
            for t in range(br // 8):
                cell = values(t)
                turn(cell, [edge[v, pl.ds(around + 8 * t, 8), :] for v in range(nv)], pos4, pos3)
                (result,) = apply([cell])
                step = (2.0 * DISSIP * factor) * p_0[nv, pl.ds(base + 8 * t, 8), :]
                for u in range(nv):
                    p_dst[u, pl.ds(base + 8 * t, 8), :] = p_0[u, pl.ds(base + 8 * t, 8), :] - step * result[u]
            return carry

        lax.fori_loop(0, ng, strip, 0)

    stage(0, ext, p_0, q_a, p_a)
    stage(1, q_a, p_a, q_b, p_b)
    stage(2, q_b, p_b, q_a, p_a)
    stage(3, q_a, p_a, None, None)
    for copy in writes:
        copy.wait()


def shift_pairs(count, step, closed):
    return [(i, (i + step) % count) for i in range(count) if closed or 0 <= i + step < count]


def coef_table(part, donor_index, donor_weight, rl, nv, sizes):
    n_circ, n_span, n_axial = sizes
    modes, sl = part.shape[0], donor_index.shape[0]
    width = -(-max(rl * n_span * n_axial, sl * n_span) // 128) * 128
    circ, span, axial = (lax.axis_index(a) for a in AXES)
    rows = part[:, : nv * rl].reshape(modes, nv, rl).transpose(1, 0, 2).reshape(nv * modes, rl)
    table = jnp.zeros((nv * modes + 8, width), jnp.float32)
    table = lax.dynamic_update_slice(table, rows, (0, (span * n_axial + axial) * rl))
    donors = jnp.stack([donor_index.astype(jnp.float32), donor_weight])
    donors = jnp.where((circ == 0) & (axial == 0), donors, 0.0)
    table = lax.dynamic_update_slice(table, donors, (nv * modes, span * sl))
    return lax.psum(table, AXES)


def local(rotor_outlet, blade_count, harmonic_list, donor_index, donor_weight, state, time_step, flux_jacobian):
    f32 = jnp.float32
    n_circ, n_span, n_axial = (lax.axis_size(a) for a in AXES)
    nv, sl, al, cl = state.shape
    br = al + 2 * W
    nb = sl + 2 * W
    ng = -(-nb // 16)
    nh = harmonic_list.shape[0]
    dims = dict(
        nv=nv, sl=sl, al=al, cl=cl, br=br, nb=nb, ng=ng, nh=nh, n_circ=n_circ, n_span=n_span, n_axial=n_axial
    )
    rl = rotor_outlet.shape[1]
    packs = -(-nv // (128 // (sl + 2 * W)))
    ride = n_axial == 2 and n_circ == 4 and nv * rl <= 128
    dims.update(rl=rl, packs=packs, ride=ride)
    params = pltpu.CompilerParams(vmem_limit_bytes=48 * 2**20)
    sides = 1 if n_axial == 2 else 2
    deep = 8 if n_axial == 2 else al

    edge, bulk, part = pl.pallas_call(
        functools.partial(axial_kernel, dims),
        out_shape=[
            jax.ShapeDtypeStruct((sides, nv + 1, W, 2 * W, cl), f32),
            jax.ShapeDtypeStruct((sides, nv + 1, W, sl - 2 * W, cl), f32),
            jax.ShapeDtypeStruct((2 * nh, -(-nv * rl // 128) * 128), f32),
        ],
        in_specs=[HBM] * 5,
        out_specs=[VMEM] * 3,
        scratch_shapes=[
            pltpu.VMEM((nv, sl, deep, cl), f32),
            pltpu.VMEM((sl, deep, cl), f32),
            pltpu.VMEM(rotor_outlet.shape, f32),
            pltpu.SMEM(blade_count.shape, jnp.int32),
            pltpu.SMEM(harmonic_list.shape, jnp.int32),
            pltpu.SemaphoreType.DMA((5,)),
        ],
        compiler_params=pltpu.CompilerParams(vmem_limit_bytes=63 * 2**20),
        name="axial_faces",
    )(state, time_step, rotor_outlet, blade_count, harmonic_list)
    state = state.reshape(nv, sl * al, cl)
    time_step = time_step.reshape(sl * al, cl)

    def axial_move(faces):
        if n_axial == 2:
            moved = lax.ppermute(faces[0], "axial", [(0, 1), (1, 0)])
            return moved, moved
        lo = lax.ppermute(faces[0], "axial", shift_pairs(n_axial, 1, False))
        hi = lax.ppermute(faces[1], "axial", shift_pairs(n_axial, -1, False))
        return lo, hi

    lo_edge, hi_edge = axial_move(edge)
    if ride:
        other = lax.ppermute(part, "axial", [(0, 1), (1, 0)])
        before = lax.ppermute(part, ("span", "axial"), shift_pairs(n_span * n_axial, 1, False))
        shares = None
    else:
        other = before = part
        shares = coef_table(part, donor_index, donor_weight, rl, nv, (n_circ, n_span, n_axial))
    lo, hi = axial_move(bulk)

    def spec(shape, *index):
        index = index or (0,) * len(shape)
        return pl.BlockSpec(shape, lambda i: index)

    faces = (nv + 1, W, 2 * W, cl)
    message = ((nv + 1) * W * (al + W * sides) + (2 * nh if ride else 0), cl)
    end = sl // W - 1
    pad = lambda x: jnp.pad(x, (0, 128 - sl))[None]
    down, up, inter = pl.pallas_call(
        functools.partial(span_kernel, dims),
        grid=(1,),
        out_shape=[jax.ShapeDtypeStruct(message, f32)] * 2 + [jax.ShapeDtypeStruct((nv, 2 * nh, 128), f32)],
        in_specs=[
            spec((nv, W * al, cl)),
            spec((nv, W * al, cl), 0, end, 0),
            spec((W * al, cl)),
            spec((W * al, cl), end, 0),
            spec(faces),
            spec(faces),
            spec(part.shape),
            spec(part.shape),
            spec(part.shape),
            spec((1, 128)),
            spec((1, 128)),
        ],
        out_specs=[spec(message), spec(message), spec((nv, 2 * nh, 128))],
        compiler_params=params,
        name="span_faces",
    )(
        state, state, time_step, time_step, lo_edge, hi_edge, part, other, before, pad(donor_index), pad(donor_weight)
    )
    below = lax.ppermute(up, "span", shift_pairs(n_span, 1, False))
    above = lax.ppermute(down, "span", shift_pairs(n_span, -1, False))

    strip = jax.ShapeDtypeStruct(((nv + 1) // 2 * ng * br + (packs * 2 * nh if ride else 0), 128), f32)
    ext, left, right, share = pl.pallas_call(
        functools.partial(circ_kernel, dims),
        out_shape=[
            jax.ShapeDtypeStruct((nv + 1, nb * br, cl), f32),
            strip,
            strip,
            jax.ShapeDtypeStruct((packs * 2 * nh, 128), f32),
        ],
        in_specs=[VMEM] * 9,
        out_specs=[VMEM] * 4,
        scratch_shapes=[pltpu.VMEM((nv + 1, ng * br, 128), f32)],
        compiler_params=params,
        name="circ_faces",
    )(state, time_step, lo_edge, hi_edge, lo, hi, below, above, inter)
    from_left = lax.ppermute(right, "circ", shift_pairs(n_circ, 1, True))
    from_right = lax.ppermute(left, "circ", shift_pairs(n_circ, -1, True))
    if ride:
        shares = [share, lax.ppermute(share, "circ", shift_pairs(n_circ, 2, True))]

    block = jax.ShapeDtypeStruct((nv, sl * al, cl), f32)
    field = pltpu.VMEM((nv, nb * br, cl), f32)
    strips = pltpu.VMEM((nv, (ng + 2) * br, 128), f32)
    new, res, _ = pl.pallas_call(
        functools.partial(step_kernel, dims),
        out_shape=[block, block, jax.ShapeDtypeStruct(ext.shape, f32)],
        in_specs=[SMEM, SMEM, SMEM, [VMEM, VMEM] if ride else VMEM, VMEM, VMEM, VMEM],
        out_specs=[HBM, HBM, VMEM],
        input_output_aliases={(5 if ride else 4): 2},
        scratch_shapes=[
            pltpu.VMEM((nv, sl * al, cl), f32),
            pltpu.VMEM((nv, (sl + 2 * W - 2) * al, cl), f32),
            field,
            field,
            pltpu.VMEM((nv + 1, (ng + 2) * br, 128), f32),
            strips,
            strips,
            pltpu.VMEM((nv, ng * br, 128), f32),
            pltpu.VMEM((16 * nv, 16 * (-(-3 * nv // 16) * 16)), jnp.bfloat16),
            pltpu.SemaphoreType.DMA((5,)),
        ],
        compiler_params=params,
        name="segments",
    )(flux_jacobian, harmonic_list, blade_count, shares, ext, from_left, from_right)
    return new.reshape(nv, sl, al, cl), res.reshape(nv, sl, al, cl)


def solution(mesh):
    return jax.shard_map(
        local,
        mesh=mesh,
        in_specs=(
            P(None, ("span", "axial"), "circ"),
            P(),
            P(),
            P("span"),
            P("span"),
            P(None, "span", "axial", "circ"),
            P("span", "axial", "circ"),
            P(),
        ),
        out_specs=(P(None, "span", "axial", "circ"), P(None, "span", "axial", "circ")),
        check_vma=False,
    )
```

```python
import functools

import jax
import jax.numpy as jnp
import numpy as np
from jax import lax
from jax.experimental import pallas as pl
from jax.experimental.pallas import tpu as pltpu
from jax.sharding import PartitionSpec as P

SEGMENT_COEF = (0.25, 1.0 / 3.0, 0.5, 1.0)
DISSIP = 0.2
W = 4
SHARE = 8
HIGH = lax.Precision.HIGHEST
VMEM = pl.BlockSpec(memory_space=pltpu.VMEM)
SMEM = pl.BlockSpec(memory_space=pltpu.SMEM)
HBM = pl.BlockSpec(memory_space=pltpu.HBM)
ANY = pl.BlockSpec(memory_space=pl.ANY)
AXES = ("circ", "span", "axial")


def make_basis(harm, blade, nh, cells, ncells):
    width = cells.shape[1]
    row = lax.broadcasted_iota(jnp.int32, (nh, width), 0)
    waves = jnp.zeros((nh, width), jnp.int32)
    for k in range(nh):
        waves = jnp.where(row == k, harm[k] * blade[0], waves)
    phase = waves * cells
    phase = phase & (ncells - 1) if ncells & (ncells - 1) == 0 else phase % ncells
    angle = (2.0 * np.pi) * phase.astype(jnp.float32) / ncells
    return jnp.concatenate([jnp.cos(angle), jnp.sin(angle)], axis=0)


def dot(a, b, dims):
    return lax.dot_general(a, b, (dims, ((), ())), precision=HIGH, preferred_element_type=jnp.float32)


def axial_kernel(dims, state, dt, rotor, blade, harm, edge, bulk, part, *scratch):
    nv, sl, al, cl, nh = (dims[k] for k in ("nv", "sl", "al", "cl", "nh"))
    cells, dt_cells, rotor_v, blade_s, harm_s, sems = scratch
    axial = lax.axis_index("axial")
    circ = lax.axis_index("circ")
    swap = dims["n_axial"] == 2
    size = cells.shape[2]
    at = pl.multiple_of(jnp.where(axial == 0, al - size, 0), 8) if swap else 0
    copies = [
        pltpu.make_async_copy(state.at[:, :, pl.ds(at, size), :], cells, sems.at[0]),
        pltpu.make_async_copy(dt.at[:, pl.ds(at, size), :], dt_cells, sems.at[1]),
        pltpu.make_async_copy(rotor, rotor_v, sems.at[2]),
        pltpu.make_async_copy(blade, blade_s, sems.at[3]),
        pltpu.make_async_copy(harm, harm_s, sems.at[4]),
    ]
    for copy in copies:
        copy.start()
    for copy in copies[2:]:
        copy.wait()
    ncells = cl * dims["n_circ"]
    here = circ * cl + lax.broadcasted_iota(jnp.int32, (1, cl), 1)
    basis = make_basis(harm_s, blade_s, nh, here, ncells)
    rl = rotor_v.shape[1]
    flat = rotor_v[...].reshape(nv * rl, cl)
    part[...] = jnp.zeros_like(part)
    part[:, : nv * rl] = dot(basis, flat, ((1,), (1,))) * (2.0 / ncells)
    for copy in copies[:2]:
        copy.wait()

    def put(side, base):
        for f in range(nv + 1):
            for i in range(W):
                ref = cells.at[f] if f < nv else dt_cells
                rows = ref[:, base + i, :]
                edge[side, f, i, 0:W] = rows[0:W]
                edge[side, f, i, W:] = rows[sl - W :]
                bulk[side, f, i] = rows[W : sl - W]

    if swap:

        @pl.when(axial == 0)
        def _():
            put(0, size - W)

        @pl.when(axial != 0)
        def _():
            put(0, 0)

    else:
        put(0, size - W)
        put(1, 0)


def inter_rows(dims, parts, firsts, donor, weight):
    nv = dims["nv"]
    rl = dims["rl"]
    table = jnp.concatenate([p[:, : nv * rl] for p in parts], axis=1)
    rows = table.shape[1]
    row = lax.broadcasted_iota(jnp.int32, (rows, 128), 0)
    station = row % rl
    for i, first in enumerate(firsts):
        station = station + jnp.where(row // (nv * rl) == i, first, 0)
    mix = jnp.where(station == donor, 1.0 - weight, jnp.where(station == donor + 1, weight, 0.0))
    var = row // rl % nv
    return [dot(table, jnp.where(var == v, mix, 0.0), ((1,), (0,))) for v in range(nv)]


def span_kernel(dims, s_head, s_tail, d_head, d_tail, lo, hi, part, other, before, donor, weight, down, up, inter):
    nv, sl, al, cl, br, nh = (dims[k] for k in ("nv", "sl", "al", "cl", "br", "nh"))
    span = lax.axis_index("span")
    faces = (lo,) if dims["n_axial"] == 2 else (lo, hi)
    rows_of = (nv + 1) * W * (al + W * len(faces))
    for out, s_ref, d_ref, at in ((down, s_head, d_head, 0), (up, s_tail, d_tail, W)):
        for f in range(nv + 1):
            rows = slice(f * W * al, (f + 1) * W * al)
            out[rows, :] = s_ref[f] if f < nv else d_ref[...]
            for side, src in enumerate(faces):
                for i in range(W):
                    to = (nv + 1) * W * al + ((side * (nv + 1) + f) * W + i) * W
                    out[to : to + W, :] = src[f, i, at : at + W, :]

    if not dims["ride"]:
        return
    rl = dims["rl"]
    first = span * 2 * rl
    shares = inter_rows(
        dims, [part[...], other[...], before[...]], [first, first + rl, first - rl], donor[...], weight[...]
    )
    lane = lax.broadcasted_iota(jnp.int32, (2 * nh, 128), 1)
    head = tail = jnp.zeros((2 * nh, 128), jnp.float32)
    for v in range(nv):
        inter[v] = shares[v]
        mine = lane // W == v
        head = jnp.where(mine, pltpu.roll(shares[v], W * v, 1), head)
        tail = jnp.where(mine, pltpu.roll(shares[v], (W * v - (sl - W)) % 128, 1), tail)
    down[rows_of:, :] = head
    up[rows_of:, :] = tail


def lane_ids(rows=8):
    return lax.broadcasted_iota(jnp.int32, (rows, 128), 1)


def gather_strips(dims, load, store, tiles):
    nb, ng, br = dims["nb"], dims["ng"], dims["br"]
    group = lane_ids() // 8
    for g in range(ng):
        for t in tiles:
            acc = jnp.zeros((8, 128), jnp.float32)
            for r in range((nb - 1 - g) // ng + 1):
                part = pltpu.roll(load((ng * r + g) * br + 8 * t), (8 * r + 4) % 128, 1)
                acc = jnp.where(group == r, part, acc)
            store(g * br + 8 * t, acc)


def circ_kernel(
    dims, state, dt, lo_edge, hi_edge, lo, hi, below, above, inter, ext, left, right, share, strips
):
    nv, sl, al, cl, br, nb, ng, nh = (dims[k] for k in ("nv", "sl", "al", "cl", "br", "nb", "ng", "nh"))
    axial = lax.axis_index("axial")
    turns = al // 8
    for f in range(nv + 1):
        for s in range(sl):
            for t in range(turns):
                rows = pl.ds(s * al + t, 8, stride=turns)
                at = (s + W) * br + 8 * (t + 1)
                ext[f, at : at + 8, :] = state[f, rows, :] if f < nv else dt[rows, :]

    swap = dims["n_axial"] == 2
    for side, (edge, bulk, valid) in enumerate(
        ((lo_edge, lo, axial > 0), (hi_edge, hi, axial < dims["n_axial"] - 1))
    ):
        base = 0 if side else W

        def fill(edge, bulk, side, base):
            for f in range(nv + 1):
                for i in range(W):
                    part = (nv + 1) * W * al + (((0 if swap else side) * (nv + 1) + f) * W + i) * W
                    pieces = (
                        (0, W, lambda: below[part : part + W, :]),
                        (W, W, lambda: edge[f, i, 0:W]),
                        (2 * W, sl - 2 * W, lambda: bulk[f, i]),
                        (sl, W, lambda: edge[f, i, W:]),
                        (sl + W, W, lambda: above[part : part + W, :]),
                    )
                    for at, n, read in pieces:
                        val = jnp.zeros((n, cl), jnp.float32) if edge is None else read()
                        ext[f, pl.ds(base + at * br + i, n, stride=br), :] = val

        @pl.when(valid)
        def _(edge=edge, bulk=bulk, side=side, base=base):
            fill(edge, bulk, side, base)

        @pl.when(jnp.logical_not(valid))
        def _(side=side, base=base):
            fill(None, None, side, base)

    for f in range(nv + 1):
        for j in range(W):
            for src, b in ((below, j), (above, sl + W + j)):
                for t in range(turns):
                    at = b * br + 8 * (t + 1)
                    ext[f, at : at + 8, :] = src[pl.ds((f * W + j) * al + t, 8, stride=turns), :]

    def each(f, carry):
        def store(row, val):
            strips[f, row : row + 8, :] = val

        gather_strips(dims, lambda row: ext[f, row : row + 8, :], store, range(br // 8))
        return carry

    lax.fori_loop(0, nv + 1, each, 0)
    half = (nv + 1) // 2
    low = lane_ids(ng * br) % 8 < 4
    for f in range(half):
        one, two = strips[f], strips[f + half]
        rows = slice(f * ng * br, (f + 1) * ng * br)
        right[rows, :] = jnp.where(low, one, pltpu.roll(two, 4, 1))
        left[rows, :] = jnp.where(low, pltpu.roll(one, 124, 1), two)

    if not dims["ride"]:
        return
    wide = sl + 2 * W
    lane = lax.broadcasted_iota(jnp.int32, (2 * nh, 128), 1)
    rows = slice((nv + 1) * W * (al + W * (1 if swap else 2)), None)
    packed = [jnp.zeros((2 * nh, 128), jnp.float32)] * dims["packs"]
    for v in range(nv):
        whole = pltpu.roll(inter[v], W, 1)
        whole = jnp.where(lane < W, pltpu.roll(below[rows, :], (-W * v) % 128, 1), whole)
        whole = jnp.where(lane >= sl + W, pltpu.roll(above[rows, :], sl + W - W * v, 1), whole)
        pack, first = divmod(v, 128 // wide)
        first = first * wide
        packed[pack] = jnp.where(
            (lane >= first) & (lane < first + wide), pltpu.roll(whole, first, 1), packed[pack]
        )
    for i in range(dims["packs"]):
        at = half * ng * br + i * 2 * nh
        left[at : at + 2 * nh, :] = packed[i]
        right[at : at + 2 * nh, :] = packed[i]
        share[i * 2 * nh : (i + 1) * 2 * nh, :] = packed[i]


def ghost_table(dims, table, span):
    nv, sl, nh = (dims[k] for k in ("nv", "sl", "nh"))
    rows, width = table.shape
    donors = pltpu.roll(table[rows - 8 :, :], lax.rem(width - span * sl + W, width), 1)[:, :128]
    lane = lax.broadcasted_iota(jnp.int32, (1, 128), 1)
    where = span * sl - W + lane
    inside = (where >= 0) & (where < sl * dims["n_span"]) & (lane < sl + 2 * W)
    station = lax.broadcasted_iota(jnp.int32, (width, 128), 0)
    donor = (donors[0:1, :] + 0.5).astype(jnp.int32)
    weight = donors[1:2, :]
    mix = jnp.where(station == donor, 1.0 - weight, jnp.where(station == donor + 1, weight, 0.0))
    mix = jnp.where(inside, mix, 0.0)
    inter = dot(table[0 : rows - 8, :], mix, ((1,), (0,)))
    return [inter[v * 2 * nh : (v + 1) * 2 * nh, :] for v in range(nv)]


def step_kernel(
    dims, jac, harm, blade, shares, _, from_left, from_right, new, res, ext, new_v, res_v, q_a, q_b, p_0, p_a, p_b, edge, coef, matrix, sem
):
    nv, sl, al, cl, br, nb, ng, nh = (dims[k] for k in ("nv", "sl", "al", "cl", "br", "nb", "ng", "nh"))
    axial = lax.axis_index("axial")
    span = lax.axis_index("span")
    circ = lax.axis_index("circ")
    spare = (W - 1) * al
    chunks = 4 if sl % 8 == 0 else 1
    lane = lax.broadcasted_iota(jnp.int32, (8, 8 * SHARE), 1)
    row = lax.broadcasted_iota(jnp.int32, (8, 8 * SHARE), 0)
    parts = []
    for u in range(nv):
        part = jnp.zeros((8, 8 * SHARE), jnp.float32)
        for k in range(3 * nv):
            d, v = 2 - k // nv if k // nv != 1 else 1, k % nv
            value = (jac[d, u, v] * 0.5 - (DISSIP if u == v else 0.0)) * (0.5 / DISSIP)
            if k < SHARE:
                part = jnp.where(lane == row + 8 * k, value, part)
            else:
                coef[u * 3 * nv + k] = jnp.full((8, 128), value, jnp.float32)
        parts.append(part)
    parts = jnp.concatenate(parts, axis=0)
    high = parts.astype(jnp.bfloat16).astype(jnp.float32)
    again = jnp.concatenate([parts - high, jnp.zeros_like(high)], axis=1)
    matrix[...] = jnp.concatenate([jnp.concatenate([high, high], axis=1), again], axis=0).astype(jnp.bfloat16)

    half = (nv + 1) // 2
    low = lane_ids(ng * br) % 8 < 4
    for f in range(half):
        rows = slice(f * ng * br, (f + 1) * ng * br)
        one, two = from_left[rows, :], from_right[rows, :]
        p_0[f, br : (ng + 1) * br, :] = jnp.where(low, one, pltpu.roll(two, 4, 1))
        p_0[f + half, br : (ng + 1) * br, :] = jnp.where(low, pltpu.roll(one, 124, 1), two)

    ncells = cl * dims["n_circ"]
    lane = lax.broadcasted_iota(jnp.int32, (1, 128), 1)
    wide = sl + 2 * W
    if dims["ride"]:
        rows = slice(half * ng * br, None)
        packed = from_left[rows, :] + from_right[rows, :] + shares[0][...] + shares[1][...]
        inter = []
        for v in range(nv):
            pack, first = divmod(v, 128 // wide)
            part = pltpu.roll(packed[pack * 2 * nh : (pack + 1) * 2 * nh, :], (-first * wide) % 128, 1)
            inter.append(jnp.where(lane < wide, part, 0.0))
    else:
        inter = ghost_table(dims, shares, span)
    start = circ * cl
    own = make_basis(harm, blade, nh, start + lax.broadcasted_iota(jnp.int32, (1, cl), 1), ncells)
    pos = lane % 8
    halo_cells = lax.rem(start + jnp.where(pos < 4, pos - 4, pos + cl - 4) + ncells, ncells)
    halo = make_basis(harm, blade, nh, halo_cells, ncells)
    s_id = lax.broadcasted_iota(jnp.int32, (128, 128), 0)
    r_id = lax.broadcasted_iota(jnp.int32, (128, 128), 1) // 8

    @pl.when(axial == 0)
    def _():
        for v in range(nv):
            part = inter[v]
            ghost = dot(part, own, ((0,), (0,)))
            ext[v, pl.ds(7, sl + 2 * W, stride=br), :] = ghost[: sl + 2 * W, :]
            ghost = dot(part, halo, ((0,), (0,)))
            for g in range(ng):
                picked = jnp.where(s_id == ng * r_id + g, ghost, 0.0)
                at = (g + 1) * br + 7
                p_0[v, at : at + 1, :] = jnp.sum(picked, axis=0, keepdims=True)

    lanes = lane_ids()
    first_lane, last_lane = lanes == 0, lanes == 127
    pos3, pos4 = lanes % 8 == 3, lanes % 8 == 4
    last = (ng + 1) * br

    def apply(cells):
        n = range(len(cells))
        for c in cells:
            c["diff"] = [p - m for d in ("theta", "span", "axial") for p, m in zip(c[d + "+"], c[d + "-"])]
        diff = jnp.concatenate(
            [jnp.concatenate([c["diff"][k] for c in cells], axis=1) for k in range(SHARE)], axis=0
        )
        high = diff.astype(jnp.bfloat16)
        low = (diff - high.astype(jnp.float32)).astype(jnp.bfloat16)
        product = jnp.dot(
            matrix[...], jnp.concatenate([high, low], axis=0), preferred_element_type=jnp.float32
        )
        out = [[None] * nv for _ in cells]
        for u in range(nv):
            odd = even = None
            for k in range(SHARE, 3 * nv):
                value = coef[u * 3 * nv + k]
                terms = [value * c["diff"][k] for c in cells]
                if (k - SHARE) % 2:
                    odd = [x + y for x, y in zip(odd, terms)] if odd else terms
                else:
                    even = [x + y for x, y in zip(even, terms)] if even else terms
            for i, c in enumerate(cells):
                lanes = slice(128 * i, 128 * i + 128)
                rest = 3.0 * c["q"][u] - (c["axial-"][u] + c["span-"][u] + c["theta-"][u])
                total = (odd[i] + even[i]) + rest
                out[i][u] = (
                    product[8 * u : 8 * u + 8, lanes] + product[8 * (nv + u) : 8 * (nv + u) + 8, lanes]
                ) + total
        return out

    turns = al // 8
    sub = lax.broadcasted_iota(jnp.int32, (8, 128), 0)
    top, bottom = sub == 0, sub == 7

    def block_cells(view, at):
        memo = {}

        def load(t, off=0):
            if (t, off) not in memo:
                row = at + off + 8 * t
                memo[t, off] = [view[v, row : row + 8, :] for v in range(nv)]
            return memo[t, off]

        def rolled(t, amount):
            if (t, "roll", amount) not in memo:
                memo[t, "roll", amount] = [pltpu.roll(x, amount, 0) for x in load(t)]
            return memo[t, "roll", amount]

        def choose(mask, one, two):
            return [jnp.where(mask, x, y) for x, y in zip(one, two)]

        def values(t):
            if t == 0:
                plus = choose(bottom, rolled(1, 7), rolled(0, 7))
                minus = choose(top, rolled(turns, 1), rolled(0, 1))
            else:
                plus = load(t + 1) if t < turns else choose(bottom, rolled(0, 7), rolled(1, 7))
                minus = load(t - 1) if t > 1 else choose(top, rolled(0, 1), rolled(turns, 1))
            return {"q": load(t), "axial-": minus, "axial+": plus, "span-": load(t, -br), "span+": load(t, br)}

        return values

    def turn(cell, beyond, at_plus, at_minus):
        cell["theta+"] = [
            pltpu.roll(jnp.where(at_plus, z, q), 127, 1) for z, q in zip(beyond, cell["q"])
        ]
        cell["theta-"] = [pltpu.roll(jnp.where(at_minus, z, q), 1, 1) for z, q in zip(beyond, cell["q"])]

    writes = [pltpu.make_async_copy(res_v.at[:, pl.ds(spare, sl * al), :], res, sem.at[0])]

    def stage(number, src, p_src, dst, p_dst):
        width = W - 1 - number
        factor = SEGMENT_COEF[number]
        final = number == len(SEGMENT_COEF) - 1
        for v in range(nv):
            p_src[v, 0:br, :] = pltpu.roll(p_src[v, last - br : last, :], 8, 1)
            p_src[v, last : last + br, :] = pltpu.roll(p_src[v, br : 2 * br, :], 120, 1)

        def blocks(b, count, first):
            around = pl.multiple_of((b - 1) * br, 8)
            view = src.at[:, pl.ds(around, (count + 2) * br), :]
            values = [block_cells(view, (i + 1) * br) for i in range(count)]
            groups = [[(i, t) for t in range(1, turns + 1)] for i in range(count)]
            if first == 0:
                groups.append([(i, 0) for i in range(count)])

            def prepare(group):
                cells = []
                for i, t in group:
                    r = (b + i) // ng
                    g = b + i - r * ng
                    p_row = pl.multiple_of((g + 1) * br, 8) + 8 * t
                    row = pl.multiple_of((b + i) * br, 8) + 8 * t
                    cell = values[i](t)
                    beyond = [pltpu.roll(p_src[v, pl.ds(p_row, 8), :], 124 - 8 * r, 1) for v in range(nv)]
                    turn(cell, beyond, first_lane, last_lane)
                    cell["base"] = [ext[u, pl.ds(row, 8), :] for u in range(nv)] if number else cell["q"]
                    cell["step"] = (2.0 * DISSIP * factor) * ext[nv, pl.ds(row, 8), :]
                    cells.append(cell)
                return cells

            cells = prepare(groups[0])
            for n, group in enumerate(groups):
                following = prepare(groups[n + 1]) if n + 1 < len(groups) else None
                results = apply(cells)
                for (i, t), cell, result in zip(group, cells, results):
                    row = pl.multiple_of((b + i) * br, 8) + 8 * t
                    for u in range(nv):
                        value = cell["base"][u] - cell["step"] * result[u]
                        if final:
                            rows = pl.ds(pl.multiple_of((b + i - W) * al, 8) + t - 1, 8, stride=turns)
                            new_v[u, rows, :] = value
                        else:
                            dst[u, pl.ds(row, 8), :] = value
                            if t > 0 and number == 0:
                                rows = pl.ds(pl.multiple_of((b + i - 1) * al, 8) + t - 1, 8, stride=turns)
                                res_v[u, rows, :] = (2.0 * DISSIP) * result[u]
                cells = following

        def run(start, count, first):
            def loop(j, carry):
                blocks(start + 2 * j, 2, first)
                return carry

            lax.fori_loop(0, count // 2, loop, 0)
            if count % 2:
                blocks(start + count - 1, 1, first)

        if final:
            for i in range(chunks):
                run(W + i * (sl // chunks), sl // chunks, 1)
                rows = pl.ds(i * (sl // chunks) * al, sl // chunks * al)
                copy = pltpu.make_async_copy(new_v.at[:, rows, :], new.at[:, rows, :], sem.at[i + 1])
                copy.start()
                writes.append(copy)
        else:
            run(W - width, sl + 2 * width, 0)
        if number == 0:
            writes[0].start()
        if final:
            return

        def edges(v, carry):
            def store(row, val):
                edge[v, row : row + 8, :] = val

            gather_strips(dims, lambda row: src[v, row : row + 8, :], store, range(br // 8))
            return carry

        lax.fori_loop(0, nv, edges, 0)

        def strip(g, carry):
            base = pl.multiple_of((g + 1) * br, 8)
            around = pl.multiple_of(g * br, 8)
            view = p_src.at[:, pl.ds(around, 3 * br), :]

            values = block_cells(view, br)
            for t in range(br // 8):
                cell = values(t)
                turn(cell, [edge[v, pl.ds(around + 8 * t, 8), :] for v in range(nv)], pos4, pos3)
                (result,) = apply([cell])
                step = (2.0 * DISSIP * factor) * p_0[nv, pl.ds(base + 8 * t, 8), :]
                for u in range(nv):
                    p_dst[u, pl.ds(base + 8 * t, 8), :] = p_0[u, pl.ds(base + 8 * t, 8), :] - step * result[u]
            return carry

        lax.fori_loop(0, ng, strip, 0)

    stage(0, ext, p_0, q_a, p_a)
    stage(1, q_a, p_a, q_b, p_b)
    stage(2, q_b, p_b, q_a, p_a)
    stage(3, q_a, p_a, None, None)
    for copy in writes:
        copy.wait()


def shift_pairs(count, step, closed):
    return [(i, (i + step) % count) for i in range(count) if closed or 0 <= i + step < count]


def coef_table(part, donor_index, donor_weight, rl, nv, sizes):
    n_circ, n_span, n_axial = sizes
    modes, sl = part.shape[0], donor_index.shape[0]
    width = -(-max(rl * n_span * n_axial, sl * n_span) // 128) * 128
    circ, span, axial = (lax.axis_index(a) for a in AXES)
    rows = part[:, : nv * rl].reshape(modes, nv, rl).transpose(1, 0, 2).reshape(nv * modes, rl)
    table = jnp.zeros((nv * modes + 8, width), jnp.float32)
    table = lax.dynamic_update_slice(table, rows, (0, (span * n_axial + axial) * rl))
    donors = jnp.stack([donor_index.astype(jnp.float32), donor_weight])
    donors = jnp.where((circ == 0) & (axial == 0), donors, 0.0)
    table = lax.dynamic_update_slice(table, donors, (nv * modes, span * sl))
    return lax.psum(table, AXES)


def local(rotor_outlet, blade_count, harmonic_list, donor_index, donor_weight, state, time_step, flux_jacobian):
    f32 = jnp.float32
    n_circ, n_span, n_axial = (lax.axis_size(a) for a in AXES)
    nv, sl, al, cl = state.shape
    br = al + 2 * W
    nb = sl + 2 * W
    ng = -(-nb // 16)
    nh = harmonic_list.shape[0]
    dims = dict(
        nv=nv, sl=sl, al=al, cl=cl, br=br, nb=nb, ng=ng, nh=nh, n_circ=n_circ, n_span=n_span, n_axial=n_axial
    )
    rl = rotor_outlet.shape[1]
    packs = -(-nv // (128 // (sl + 2 * W)))
    ride = n_axial == 2 and n_circ == 4 and nv * rl <= 128
    dims.update(rl=rl, packs=packs, ride=ride)
    params = pltpu.CompilerParams(vmem_limit_bytes=48 * 2**20)
    sides = 1 if n_axial == 2 else 2
    deep = 8 if n_axial == 2 else al

    edge, bulk, part = pl.pallas_call(
        functools.partial(axial_kernel, dims),
        out_shape=[
            jax.ShapeDtypeStruct((sides, nv + 1, W, 2 * W, cl), f32),
            jax.ShapeDtypeStruct((sides, nv + 1, W, sl - 2 * W, cl), f32),
            jax.ShapeDtypeStruct((2 * nh, -(-nv * rl // 128) * 128), f32),
        ],
        in_specs=[HBM] * 5,
        out_specs=[VMEM] * 3,
        scratch_shapes=[
            pltpu.VMEM((nv, sl, deep, cl), f32),
            pltpu.VMEM((sl, deep, cl), f32),
            pltpu.VMEM(rotor_outlet.shape, f32),
            pltpu.SMEM(blade_count.shape, jnp.int32),
            pltpu.SMEM(harmonic_list.shape, jnp.int32),
            pltpu.SemaphoreType.DMA((5,)),
        ],
        compiler_params=pltpu.CompilerParams(vmem_limit_bytes=63 * 2**20),
        name="axial_faces",
    )(state, time_step, rotor_outlet, blade_count, harmonic_list)
    state = state.reshape(nv, sl * al, cl)
    time_step = time_step.reshape(sl * al, cl)

    def axial_move(faces):
        if n_axial == 2:
            moved = lax.ppermute(faces[0], "axial", [(0, 1), (1, 0)])
            return moved, moved
        lo = lax.ppermute(faces[0], "axial", shift_pairs(n_axial, 1, False))
        hi = lax.ppermute(faces[1], "axial", shift_pairs(n_axial, -1, False))
        return lo, hi

    lo_edge, hi_edge = axial_move(edge)
    if ride:
        other = lax.ppermute(part, "axial", [(0, 1), (1, 0)])
        before = lax.ppermute(part, ("span", "axial"), shift_pairs(n_span * n_axial, 1, False))
        shares = None
    else:
        other = before = part
        shares = coef_table(part, donor_index, donor_weight, rl, nv, (n_circ, n_span, n_axial))
    lo, hi = axial_move(bulk)

    def spec(shape, *index):
        index = index or (0,) * len(shape)
        return pl.BlockSpec(shape, lambda i: index)

    faces = (nv + 1, W, 2 * W, cl)
    message = ((nv + 1) * W * (al + W * sides) + (2 * nh if ride else 0), cl)
    end = sl // W - 1
    pad = lambda x: jnp.pad(x, (0, 128 - sl))[None]
    down, up, inter = pl.pallas_call(
        functools.partial(span_kernel, dims),
        grid=(1,),
        out_shape=[jax.ShapeDtypeStruct(message, f32)] * 2 + [jax.ShapeDtypeStruct((nv, 2 * nh, 128), f32)],
        in_specs=[
            spec((nv, W * al, cl)),
            spec((nv, W * al, cl), 0, end, 0),
            spec((W * al, cl)),
            spec((W * al, cl), end, 0),
            spec(faces),
            spec(faces),
            spec(part.shape),
            spec(part.shape),
            spec(part.shape),
            spec((1, 128)),
            spec((1, 128)),
        ],
        out_specs=[spec(message), spec(message), spec((nv, 2 * nh, 128))],
        compiler_params=params,
        name="span_faces",
    )(
        state, state, time_step, time_step, lo_edge, hi_edge, part, other, before, pad(donor_index), pad(donor_weight)
    )
    below = lax.ppermute(up, "span", shift_pairs(n_span, 1, False))
    above = lax.ppermute(down, "span", shift_pairs(n_span, -1, False))

    strip = jax.ShapeDtypeStruct(((nv + 1) // 2 * ng * br + (packs * 2 * nh if ride else 0), 128), f32)
    ext, left, right, share = pl.pallas_call(
        functools.partial(circ_kernel, dims),
        out_shape=[
            jax.ShapeDtypeStruct((nv + 1, nb * br, cl), f32),
            strip,
            strip,
            jax.ShapeDtypeStruct((packs * 2 * nh, 128), f32),
        ],
        in_specs=[VMEM] * 9,
        out_specs=[VMEM] * 4,
        scratch_shapes=[pltpu.VMEM((nv + 1, ng * br, 128), f32)],
        compiler_params=params,
        name="circ_faces",
    )(state, time_step, lo_edge, hi_edge, lo, hi, below, above, inter)
    from_left = lax.ppermute(right, "circ", shift_pairs(n_circ, 1, True))
    from_right = lax.ppermute(left, "circ", shift_pairs(n_circ, -1, True))
    if ride:
        shares = [share, lax.ppermute(share, "circ", shift_pairs(n_circ, 2, True))]

    block = jax.ShapeDtypeStruct((nv, sl * al, cl), f32)
    field = pltpu.VMEM((nv, nb * br, cl), f32)
    strips = pltpu.VMEM((nv, (ng + 2) * br, 128), f32)
    new, res, _ = pl.pallas_call(
        functools.partial(step_kernel, dims),
        out_shape=[block, block, jax.ShapeDtypeStruct(ext.shape, f32)],
        in_specs=[SMEM, SMEM, SMEM, [VMEM, VMEM] if ride else VMEM, VMEM, VMEM, VMEM],
        out_specs=[HBM, HBM, VMEM],
        input_output_aliases={(5 if ride else 4): 2},
        scratch_shapes=[
            pltpu.VMEM((nv, sl * al, cl), f32),
            pltpu.VMEM((nv, (sl + 2 * W - 2) * al, cl), f32),
            field,
            field,
            pltpu.VMEM((nv + 1, (ng + 2) * br, 128), f32),
            strips,
            strips,
            pltpu.VMEM((nv, ng * br, 128), f32),
            pltpu.VMEM((3 * nv * nv, 8, 128), f32),
            pltpu.VMEM((16 * nv, 16 * SHARE), jnp.bfloat16),
            pltpu.SemaphoreType.DMA((5,)),
        ],
        compiler_params=params,
        name="segments",
    )(flux_jacobian, harmonic_list, blade_count, shares, ext, from_left, from_right)
    return new.reshape(nv, sl, al, cl), res.reshape(nv, sl, al, cl)


def solution(mesh):
    return jax.shard_map(
        local,
        mesh=mesh,
        in_specs=(
            P(None, ("span", "axial"), "circ"),
            P(),
            P(),
            P("span"),
            P("span"),
            P(None, "span", "axial", "circ"),
            P("span", "axial", "circ"),
            P(),
        ),
        out_specs=(P(None, "span", "axial", "circ"), P(None, "span", "axial", "circ")),
        check_vma=False,
    )
```

```python
import functools

import jax
import jax.numpy as jnp
import numpy as np
from jax import lax
from jax.experimental import pallas as pl
from jax.experimental.pallas import tpu as pltpu
from jax.sharding import PartitionSpec as P

SEGMENT_COEF = (0.25, 1.0 / 3.0, 0.5, 1.0)
DISSIP = 0.2
W = 4
HIGH = lax.Precision.HIGHEST
VMEM = pl.BlockSpec(memory_space=pltpu.VMEM)
SMEM = pl.BlockSpec(memory_space=pltpu.SMEM)
HBM = pl.BlockSpec(memory_space=pltpu.HBM)
ANY = pl.BlockSpec(memory_space=pl.ANY)
AXES = ("circ", "span", "axial")


def make_basis(harm, blade, nh, cells, ncells):
    width = cells.shape[1]
    row = lax.broadcasted_iota(jnp.int32, (nh, width), 0)
    waves = jnp.zeros((nh, width), jnp.int32)
    for k in range(nh):
        waves = jnp.where(row == k, harm[k] * blade[0], waves)
    phase = waves * cells
    phase = phase & (ncells - 1) if ncells & (ncells - 1) == 0 else phase % ncells
    angle = (2.0 * np.pi) * phase.astype(jnp.float32) / ncells
    return jnp.concatenate([jnp.cos(angle), jnp.sin(angle)], axis=0)


def dot(a, b, dims):
    return lax.dot_general(a, b, (dims, ((), ())), precision=HIGH, preferred_element_type=jnp.float32)


def axial_kernel(dims, state, dt, rotor, blade, harm, edge, bulk, part, *scratch):
    nv, sl, al, cl, nh = (dims[k] for k in ("nv", "sl", "al", "cl", "nh"))
    cells, dt_cells, rotor_v, blade_s, harm_s, sems = scratch
    axial = lax.axis_index("axial")
    circ = lax.axis_index("circ")
    swap = dims["n_axial"] == 2
    size = cells.shape[2]
    at = pl.multiple_of(jnp.where(axial == 0, al - size, 0), 8) if swap else 0
    copies = [
        pltpu.make_async_copy(state.at[:, :, pl.ds(at, size), :], cells, sems.at[0]),
        pltpu.make_async_copy(dt.at[:, pl.ds(at, size), :], dt_cells, sems.at[1]),
        pltpu.make_async_copy(rotor, rotor_v, sems.at[2]),
        pltpu.make_async_copy(blade, blade_s, sems.at[3]),
        pltpu.make_async_copy(harm, harm_s, sems.at[4]),
    ]
    for copy in copies:
        copy.start()
    for copy in copies[2:]:
        copy.wait()
    ncells = cl * dims["n_circ"]
    here = circ * cl + lax.broadcasted_iota(jnp.int32, (1, cl), 1)
    basis = make_basis(harm_s, blade_s, nh, here, ncells)
    rl = rotor_v.shape[1]
    flat = rotor_v[...].reshape(nv * rl, cl)
    part[...] = jnp.zeros_like(part)
    part[:, : nv * rl] = dot(basis, flat, ((1,), (1,))) * (2.0 / ncells)
    for copy in copies[:2]:
        copy.wait()

    def put(side, base):
        for f in range(nv + 1):
            for i in range(W):
                ref = cells.at[f] if f < nv else dt_cells
                rows = ref[:, base + i, :]
                edge[side, f, i, 0:W] = rows[0:W]
                edge[side, f, i, W:] = rows[sl - W :]
                bulk[side, f, i] = rows[W : sl - W]

    if swap:

        @pl.when(axial == 0)
        def _():
            put(0, size - W)

        @pl.when(axial != 0)
        def _():
            put(0, 0)

    else:
        put(0, size - W)
        put(1, 0)


def inter_rows(dims, parts, firsts, donor, weight):
    nv = dims["nv"]
    rl = dims["rl"]
    table = jnp.concatenate([p[:, : nv * rl] for p in parts], axis=1)
    rows = table.shape[1]
    row = lax.broadcasted_iota(jnp.int32, (rows, 128), 0)
    station = row % rl
    for i, first in enumerate(firsts):
        station = station + jnp.where(row // (nv * rl) == i, first, 0)
    mix = jnp.where(station == donor, 1.0 - weight, jnp.where(station == donor + 1, weight, 0.0))
    var = row // rl % nv
    return [dot(table, jnp.where(var == v, mix, 0.0), ((1,), (0,))) for v in range(nv)]


def span_kernel(dims, s_head, s_tail, d_head, d_tail, lo, hi, part, other, before, donor, weight, down, up, inter):
    nv, sl, al, cl, br, nh = (dims[k] for k in ("nv", "sl", "al", "cl", "br", "nh"))
    span = lax.axis_index("span")
    faces = (lo,) if dims["n_axial"] == 2 else (lo, hi)
    rows_of = (nv + 1) * W * (al + W * len(faces))
    for out, s_ref, d_ref, at in ((down, s_head, d_head, 0), (up, s_tail, d_tail, W)):
        for f in range(nv + 1):
            rows = slice(f * W * al, (f + 1) * W * al)
            out[rows, :] = s_ref[f] if f < nv else d_ref[...]
            for side, src in enumerate(faces):
                for i in range(W):
                    to = (nv + 1) * W * al + ((side * (nv + 1) + f) * W + i) * W
                    out[to : to + W, :] = src[f, i, at : at + W, :]

    if not dims["ride"]:
        return
    rl = dims["rl"]
    first = span * 2 * rl
    shares = inter_rows(
        dims, [part[...], other[...], before[...]], [first, first + rl, first - rl], donor[...], weight[...]
    )
    lane = lax.broadcasted_iota(jnp.int32, (2 * nh, 128), 1)
    head = tail = jnp.zeros((2 * nh, 128), jnp.float32)
    for v in range(nv):
        inter[v] = shares[v]
        mine = lane // W == v
        head = jnp.where(mine, pltpu.roll(shares[v], W * v, 1), head)
        tail = jnp.where(mine, pltpu.roll(shares[v], (W * v - (sl - W)) % 128, 1), tail)
    down[rows_of:, :] = head
    up[rows_of:, :] = tail


def lane_ids(rows=8):
    return lax.broadcasted_iota(jnp.int32, (rows, 128), 1)


def gather_strips(dims, load, store, tiles):
    nb, ng, br = dims["nb"], dims["ng"], dims["br"]
    group = lane_ids() // 8
    for g in range(ng):
        for t in tiles:
            acc = jnp.zeros((8, 128), jnp.float32)
            for r in range((nb - 1 - g) // ng + 1):
                part = pltpu.roll(load((ng * r + g) * br + 8 * t), (8 * r + 4) % 128, 1)
                acc = jnp.where(group == r, part, acc)
            store(g * br + 8 * t, acc)


def circ_kernel(
    dims, state, dt, lo_edge, hi_edge, lo, hi, below, above, inter, ext, left, right, share, strips
):
    nv, sl, al, cl, br, nb, ng, nh = (dims[k] for k in ("nv", "sl", "al", "cl", "br", "nb", "ng", "nh"))
    axial = lax.axis_index("axial")
    turns = al // 8
    for f in range(nv + 1):
        for s in range(sl):
            for t in range(turns):
                rows = pl.ds(s * al + t, 8, stride=turns)
                at = (s + W) * br + 8 * (t + 1)
                ext[f, at : at + 8, :] = state[f, rows, :] if f < nv else dt[rows, :]

    swap = dims["n_axial"] == 2
    for side, (edge, bulk, valid) in enumerate(
        ((lo_edge, lo, axial > 0), (hi_edge, hi, axial < dims["n_axial"] - 1))
    ):
        base = 0 if side else W

        def fill(edge, bulk, side, base):
            for f in range(nv + 1):
                for i in range(W):
                    part = (nv + 1) * W * al + (((0 if swap else side) * (nv + 1) + f) * W + i) * W
                    pieces = (
                        (0, W, lambda: below[part : part + W, :]),
                        (W, W, lambda: edge[f, i, 0:W]),
                        (2 * W, sl - 2 * W, lambda: bulk[f, i]),
                        (sl, W, lambda: edge[f, i, W:]),
                        (sl + W, W, lambda: above[part : part + W, :]),
                    )
                    for at, n, read in pieces:
                        val = jnp.zeros((n, cl), jnp.float32) if edge is None else read()
                        ext[f, pl.ds(base + at * br + i, n, stride=br), :] = val

        @pl.when(valid)
        def _(edge=edge, bulk=bulk, side=side, base=base):
            fill(edge, bulk, side, base)

        @pl.when(jnp.logical_not(valid))
        def _(side=side, base=base):
            fill(None, None, side, base)

    for f in range(nv + 1):
        for j in range(W):
            for src, b in ((below, j), (above, sl + W + j)):
                for t in range(turns):
                    at = b * br + 8 * (t + 1)
                    ext[f, at : at + 8, :] = src[pl.ds((f * W + j) * al + t, 8, stride=turns), :]

    def each(f, carry):
        def store(row, val):
            strips[f, row : row + 8, :] = val

        gather_strips(dims, lambda row: ext[f, row : row + 8, :], store, range(br // 8))
        return carry

    lax.fori_loop(0, nv + 1, each, 0)
    half = (nv + 1) // 2
    low = lane_ids(ng * br) % 8 < 4
    for f in range(half):
        one, two = strips[f], strips[f + half]
        rows = slice(f * ng * br, (f + 1) * ng * br)
        right[rows, :] = jnp.where(low, one, pltpu.roll(two, 4, 1))
        left[rows, :] = jnp.where(low, pltpu.roll(one, 124, 1), two)

    if not dims["ride"]:
        return
    wide = sl + 2 * W
    lane = lax.broadcasted_iota(jnp.int32, (2 * nh, 128), 1)
    rows = slice((nv + 1) * W * (al + W * (1 if swap else 2)), None)
    packed = [jnp.zeros((2 * nh, 128), jnp.float32)] * dims["packs"]
    for v in range(nv):
        whole = pltpu.roll(inter[v], W, 1)
        whole = jnp.where(lane < W, pltpu.roll(below[rows, :], (-W * v) % 128, 1), whole)
        whole = jnp.where(lane >= sl + W, pltpu.roll(above[rows, :], sl + W - W * v, 1), whole)
        pack, first = divmod(v, 128 // wide)
        first = first * wide
        packed[pack] = jnp.where(
            (lane >= first) & (lane < first + wide), pltpu.roll(whole, first, 1), packed[pack]
        )
    for i in range(dims["packs"]):
        at = half * ng * br + i * 2 * nh
        left[at : at + 2 * nh, :] = packed[i]
        right[at : at + 2 * nh, :] = packed[i]
        share[i * 2 * nh : (i + 1) * 2 * nh, :] = packed[i]


def ghost_table(dims, table, span):
    nv, sl, nh = (dims[k] for k in ("nv", "sl", "nh"))
    rows, width = table.shape
    donors = pltpu.roll(table[rows - 8 :, :], lax.rem(width - span * sl + W, width), 1)[:, :128]
    lane = lax.broadcasted_iota(jnp.int32, (1, 128), 1)
    where = span * sl - W + lane
    inside = (where >= 0) & (where < sl * dims["n_span"]) & (lane < sl + 2 * W)
    station = lax.broadcasted_iota(jnp.int32, (width, 128), 0)
    donor = (donors[0:1, :] + 0.5).astype(jnp.int32)
    weight = donors[1:2, :]
    mix = jnp.where(station == donor, 1.0 - weight, jnp.where(station == donor + 1, weight, 0.0))
    mix = jnp.where(inside, mix, 0.0)
    inter = dot(table[0 : rows - 8, :], mix, ((1,), (0,)))
    return [inter[v * 2 * nh : (v + 1) * 2 * nh, :] for v in range(nv)]


def step_kernel(
    dims, jac, harm, blade, shares, _, from_left, from_right, new, res, ext, new_v, res_v, q_a, q_b, p_0, p_a, p_b, edge, coef, sem
):
    nv, sl, al, cl, br, nb, ng, nh = (dims[k] for k in ("nv", "sl", "al", "cl", "br", "nb", "ng", "nh"))
    axial = lax.axis_index("axial")
    span = lax.axis_index("span")
    circ = lax.axis_index("circ")
    spare = (W - 1) * al
    parts = 4 if sl % 8 == 0 else 1
    for d in range(3):
        for u in range(nv):
            for v in range(nv):
                value = (jac[d, u, v] * 0.5 - (DISSIP if u == v else 0.0)) * (0.5 / DISSIP)
                coef[(d * nv + u) * nv + v] = jnp.full((8, 128), value, jnp.float32)

    half = (nv + 1) // 2
    low = lane_ids(ng * br) % 8 < 4
    for f in range(half):
        rows = slice(f * ng * br, (f + 1) * ng * br)
        one, two = from_left[rows, :], from_right[rows, :]
        p_0[f, br : (ng + 1) * br, :] = jnp.where(low, one, pltpu.roll(two, 4, 1))
        p_0[f + half, br : (ng + 1) * br, :] = jnp.where(low, pltpu.roll(one, 124, 1), two)

    ncells = cl * dims["n_circ"]
    lane = lax.broadcasted_iota(jnp.int32, (1, 128), 1)
    wide = sl + 2 * W
    if dims["ride"]:
        rows = slice(half * ng * br, None)
        packed = from_left[rows, :] + from_right[rows, :] + shares[0][...] + shares[1][...]
        inter = []
        for v in range(nv):
            pack, first = divmod(v, 128 // wide)
            part = pltpu.roll(packed[pack * 2 * nh : (pack + 1) * 2 * nh, :], (-first * wide) % 128, 1)
            inter.append(jnp.where(lane < wide, part, 0.0))
    else:
        inter = ghost_table(dims, shares, span)
    start = circ * cl
    own = make_basis(harm, blade, nh, start + lax.broadcasted_iota(jnp.int32, (1, cl), 1), ncells)
    pos = lane % 8
    halo_cells = lax.rem(start + jnp.where(pos < 4, pos - 4, pos + cl - 4) + ncells, ncells)
    halo = make_basis(harm, blade, nh, halo_cells, ncells)
    s_id = lax.broadcasted_iota(jnp.int32, (128, 128), 0)
    r_id = lax.broadcasted_iota(jnp.int32, (128, 128), 1) // 8

    @pl.when(axial == 0)
    def _():
        for v in range(nv):
            part = inter[v]
            ghost = dot(part, own, ((0,), (0,)))
            ext[v, pl.ds(7, sl + 2 * W, stride=br), :] = ghost[: sl + 2 * W, :]
            ghost = dot(part, halo, ((0,), (0,)))
            for g in range(ng):
                picked = jnp.where(s_id == ng * r_id + g, ghost, 0.0)
                at = (g + 1) * br + 7
                p_0[v, at : at + 1, :] = jnp.sum(picked, axis=0, keepdims=True)

    lanes = lane_ids()
    first_lane, last_lane = lanes == 0, lanes == 127
    pos3, pos4 = lanes % 8 == 3, lanes % 8 == 4
    last = (ng + 1) * br

    def apply(cells):
        sums = [[3.0 * q for q in c["q"]] for c in cells]
        for d, name in enumerate(("axial", "span", "theta")):
            diff = []
            for c, total in zip(cells, sums):
                diff.append([p - m for p, m in zip(c[name + "+"], c[name + "-"])])
                for u in range(nv):
                    total[u] = total[u] - c[name + "-"][u]
            for v in range(nv):
                for u in range(nv):
                    k = coef[(d * nv + u) * nv + v]
                    for i in range(len(cells)):
                        sums[i][u] = sums[i][u] + k * diff[i][v]
        return sums

    turns = al // 8
    sub = lax.broadcasted_iota(jnp.int32, (8, 128), 0)
    top, bottom = sub == 0, sub == 7

    def block_cells(view, at):
        memo = {}

        def load(t, off=0):
            if (t, off) not in memo:
                row = at + off + 8 * t
                memo[t, off] = [view[v, row : row + 8, :] for v in range(nv)]
            return memo[t, off]

        def rolled(t, amount):
            if (t, "roll", amount) not in memo:
                memo[t, "roll", amount] = [pltpu.roll(x, amount, 0) for x in load(t)]
            return memo[t, "roll", amount]

        def choose(mask, one, two):
            return [jnp.where(mask, x, y) for x, y in zip(one, two)]

        def values(t):
            if t == 0:
                plus = choose(bottom, rolled(1, 7), rolled(0, 7))
                minus = choose(top, rolled(turns, 1), rolled(0, 1))
            else:
                plus = load(t + 1) if t < turns else choose(bottom, rolled(0, 7), rolled(1, 7))
                minus = load(t - 1) if t > 1 else choose(top, rolled(0, 1), rolled(turns, 1))
            return {"q": load(t), "axial-": minus, "axial+": plus, "span-": load(t, -br), "span+": load(t, br)}

        return values

    def turn(cell, beyond, at_plus, at_minus):
        cell["theta+"] = [
            pltpu.roll(jnp.where(at_plus, z, q), 127, 1) for z, q in zip(beyond, cell["q"])
        ]
        cell["theta-"] = [pltpu.roll(jnp.where(at_minus, z, q), 1, 1) for z, q in zip(beyond, cell["q"])]

    writes = [pltpu.make_async_copy(res_v.at[:, pl.ds(spare, sl * al), :], res, sem.at[0])]

    def stage(number, src, p_src, dst, p_dst):
        width = W - 1 - number
        factor = SEGMENT_COEF[number]
        final = number == len(SEGMENT_COEF) - 1
        for v in range(nv):
            p_src[v, 0:br, :] = pltpu.roll(p_src[v, last - br : last, :], 8, 1)
            p_src[v, last : last + br, :] = pltpu.roll(p_src[v, br : 2 * br, :], 120, 1)

        def blocks(b, count, first):
            around = pl.multiple_of((b - 1) * br, 8)
            view = src.at[:, pl.ds(around, (count + 2) * br), :]
            values = [block_cells(view, (i + 1) * br) for i in range(count)]
            groups = [[(i, t) for i in range(count) for t in range(1, turns + 1)]]
            if first == 0:
                groups.append([(i, 0) for i in range(count)])

            def prepare(group):
                cells = []
                for i, t in group:
                    r = (b + i) // ng
                    g = b + i - r * ng
                    p_row = pl.multiple_of((g + 1) * br, 8) + 8 * t
                    row = pl.multiple_of((b + i) * br, 8) + 8 * t
                    cell = values[i](t)
                    beyond = [pltpu.roll(p_src[v, pl.ds(p_row, 8), :], 124 - 8 * r, 1) for v in range(nv)]
                    turn(cell, beyond, first_lane, last_lane)
                    cell["base"] = [ext[u, pl.ds(row, 8), :] for u in range(nv)] if number else cell["q"]
                    cell["step"] = (2.0 * DISSIP * factor) * ext[nv, pl.ds(row, 8), :]
                    cells.append(cell)
                return cells

            cells = prepare(groups[0])
            for n, group in enumerate(groups):
                following = prepare(groups[n + 1]) if n + 1 < len(groups) else None
                results = apply(cells)
                for (i, t), cell, result in zip(group, cells, results):
                    row = pl.multiple_of((b + i) * br, 8) + 8 * t
                    for u in range(nv):
                        value = cell["base"][u] - cell["step"] * result[u]
                        if final:
                            rows = pl.ds(pl.multiple_of((b + i - W) * al, 8) + t - 1, 8, stride=turns)
                            new_v[u, rows, :] = value
                        else:
                            dst[u, pl.ds(row, 8), :] = value
                            if t > 0 and number == 0:
                                rows = pl.ds(pl.multiple_of((b + i - 1) * al, 8) + t - 1, 8, stride=turns)
                                res_v[u, rows, :] = (2.0 * DISSIP) * result[u]
                cells = following

        def run(start, count, first):
            def loop(j, carry):
                blocks(start + 2 * j, 2, first)
                return carry

            lax.fori_loop(0, count // 2, loop, 0)
            if count % 2:
                blocks(start + count - 1, 1, first)

        if final:
            for i in range(parts):
                run(W + i * (sl // parts), sl // parts, 1)
                rows = pl.ds(i * (sl // parts) * al, sl // parts * al)
                copy = pltpu.make_async_copy(new_v.at[:, rows, :], new.at[:, rows, :], sem.at[i + 1])
                copy.start()
                writes.append(copy)
        else:
            run(W - width, sl + 2 * width, 0)
        if number == 0:
            writes[0].start()
        if final:
            return

        def edges(v, carry):
            def store(row, val):
                edge[v, row : row + 8, :] = val

            gather_strips(dims, lambda row: src[v, row : row + 8, :], store, range(br // 8))
            return carry

        lax.fori_loop(0, nv, edges, 0)

        def strip(g, carry):
            base = pl.multiple_of((g + 1) * br, 8)
            around = pl.multiple_of(g * br, 8)
            view = p_src.at[:, pl.ds(around, 3 * br), :]

            values = block_cells(view, br)
            for t in range(br // 8):
                cell = values(t)
                turn(cell, [edge[v, pl.ds(around + 8 * t, 8), :] for v in range(nv)], pos4, pos3)
                (result,) = apply([cell])
                step = (2.0 * DISSIP * factor) * p_0[nv, pl.ds(base + 8 * t, 8), :]
                for u in range(nv):
                    p_dst[u, pl.ds(base + 8 * t, 8), :] = p_0[u, pl.ds(base + 8 * t, 8), :] - step * result[u]
            return carry

        lax.fori_loop(0, ng, strip, 0)

    stage(0, ext, p_0, q_a, p_a)
    stage(1, q_a, p_a, q_b, p_b)
    stage(2, q_b, p_b, q_a, p_a)
    stage(3, q_a, p_a, None, None)
    for copy in writes:
        copy.wait()


def shift_pairs(count, step, closed):
    return [(i, (i + step) % count) for i in range(count) if closed or 0 <= i + step < count]


def coef_table(part, donor_index, donor_weight, rl, nv, sizes):
    n_circ, n_span, n_axial = sizes
    modes, sl = part.shape[0], donor_index.shape[0]
    width = -(-max(rl * n_span * n_axial, sl * n_span) // 128) * 128
    circ, span, axial = (lax.axis_index(a) for a in AXES)
    rows = part[:, : nv * rl].reshape(modes, nv, rl).transpose(1, 0, 2).reshape(nv * modes, rl)
    table = jnp.zeros((nv * modes + 8, width), jnp.float32)
    table = lax.dynamic_update_slice(table, rows, (0, (span * n_axial + axial) * rl))
    donors = jnp.stack([donor_index.astype(jnp.float32), donor_weight])
    donors = jnp.where((circ == 0) & (axial == 0), donors, 0.0)
    table = lax.dynamic_update_slice(table, donors, (nv * modes, span * sl))
    return lax.psum(table, AXES)


def local(rotor_outlet, blade_count, harmonic_list, donor_index, donor_weight, state, time_step, flux_jacobian):
    f32 = jnp.float32
    n_circ, n_span, n_axial = (lax.axis_size(a) for a in AXES)
    nv, sl, al, cl = state.shape
    br = al + 2 * W
    nb = sl + 2 * W
    ng = -(-nb // 16)
    nh = harmonic_list.shape[0]
    dims = dict(
        nv=nv, sl=sl, al=al, cl=cl, br=br, nb=nb, ng=ng, nh=nh, n_circ=n_circ, n_span=n_span, n_axial=n_axial
    )
    rl = rotor_outlet.shape[1]
    packs = -(-nv // (128 // (sl + 2 * W)))
    ride = n_axial == 2 and n_circ == 4 and nv * rl <= 128
    dims.update(rl=rl, packs=packs, ride=ride)
    params = pltpu.CompilerParams(vmem_limit_bytes=48 * 2**20)
    sides = 1 if n_axial == 2 else 2
    deep = 8 if n_axial == 2 else al

    edge, bulk, part = pl.pallas_call(
        functools.partial(axial_kernel, dims),
        out_shape=[
            jax.ShapeDtypeStruct((sides, nv + 1, W, 2 * W, cl), f32),
            jax.ShapeDtypeStruct((sides, nv + 1, W, sl - 2 * W, cl), f32),
            jax.ShapeDtypeStruct((2 * nh, -(-nv * rl // 128) * 128), f32),
        ],
        in_specs=[HBM] * 5,
        out_specs=[VMEM] * 3,
        scratch_shapes=[
            pltpu.VMEM((nv, sl, deep, cl), f32),
            pltpu.VMEM((sl, deep, cl), f32),
            pltpu.VMEM(rotor_outlet.shape, f32),
            pltpu.SMEM(blade_count.shape, jnp.int32),
            pltpu.SMEM(harmonic_list.shape, jnp.int32),
            pltpu.SemaphoreType.DMA((5,)),
        ],
        compiler_params=pltpu.CompilerParams(vmem_limit_bytes=63 * 2**20),
        name="axial_faces",
    )(state, time_step, rotor_outlet, blade_count, harmonic_list)
    state = state.reshape(nv, sl * al, cl)
    time_step = time_step.reshape(sl * al, cl)

    def axial_move(faces):
        if n_axial == 2:
            moved = lax.ppermute(faces[0], "axial", [(0, 1), (1, 0)])
            return moved, moved
        lo = lax.ppermute(faces[0], "axial", shift_pairs(n_axial, 1, False))
        hi = lax.ppermute(faces[1], "axial", shift_pairs(n_axial, -1, False))
        return lo, hi

    lo_edge, hi_edge = axial_move(edge)
    if ride:
        other = lax.ppermute(part, "axial", [(0, 1), (1, 0)])
        before = lax.ppermute(part, ("span", "axial"), shift_pairs(n_span * n_axial, 1, False))
        shares = None
    else:
        other = before = part
        shares = coef_table(part, donor_index, donor_weight, rl, nv, (n_circ, n_span, n_axial))
    lo, hi = axial_move(bulk)

    def spec(shape, *index):
        index = index or (0,) * len(shape)
        return pl.BlockSpec(shape, lambda i: index)

    faces = (nv + 1, W, 2 * W, cl)
    message = ((nv + 1) * W * (al + W * sides) + (2 * nh if ride else 0), cl)
    end = sl // W - 1
    pad = lambda x: jnp.pad(x, (0, 128 - sl))[None]
    down, up, inter = pl.pallas_call(
        functools.partial(span_kernel, dims),
        grid=(1,),
        out_shape=[jax.ShapeDtypeStruct(message, f32)] * 2 + [jax.ShapeDtypeStruct((nv, 2 * nh, 128), f32)],
        in_specs=[
            spec((nv, W * al, cl)),
            spec((nv, W * al, cl), 0, end, 0),
            spec((W * al, cl)),
            spec((W * al, cl), end, 0),
            spec(faces),
            spec(faces),
            spec(part.shape),
            spec(part.shape),
            spec(part.shape),
            spec((1, 128)),
            spec((1, 128)),
        ],
        out_specs=[spec(message), spec(message), spec((nv, 2 * nh, 128))],
        compiler_params=params,
        name="span_faces",
    )(
        state, state, time_step, time_step, lo_edge, hi_edge, part, other, before, pad(donor_index), pad(donor_weight)
    )
    below = lax.ppermute(up, "span", shift_pairs(n_span, 1, False))
    above = lax.ppermute(down, "span", shift_pairs(n_span, -1, False))

    strip = jax.ShapeDtypeStruct(((nv + 1) // 2 * ng * br + (packs * 2 * nh if ride else 0), 128), f32)
    ext, left, right, share = pl.pallas_call(
        functools.partial(circ_kernel, dims),
        out_shape=[
            jax.ShapeDtypeStruct((nv + 1, nb * br, cl), f32),
            strip,
            strip,
            jax.ShapeDtypeStruct((packs * 2 * nh, 128), f32),
        ],
        in_specs=[VMEM] * 9,
        out_specs=[VMEM] * 4,
        scratch_shapes=[pltpu.VMEM((nv + 1, ng * br, 128), f32)],
        compiler_params=params,
        name="circ_faces",
    )(state, time_step, lo_edge, hi_edge, lo, hi, below, above, inter)
    from_left = lax.ppermute(right, "circ", shift_pairs(n_circ, 1, True))
    from_right = lax.ppermute(left, "circ", shift_pairs(n_circ, -1, True))
    if ride:
        shares = [share, lax.ppermute(share, "circ", shift_pairs(n_circ, 2, True))]

    block = jax.ShapeDtypeStruct((nv, sl * al, cl), f32)
    field = pltpu.VMEM((nv, nb * br, cl), f32)
    strips = pltpu.VMEM((nv, (ng + 2) * br, 128), f32)
    new, res, _ = pl.pallas_call(
        functools.partial(step_kernel, dims),
        out_shape=[block, block, jax.ShapeDtypeStruct(ext.shape, f32)],
        in_specs=[SMEM, SMEM, SMEM, [VMEM, VMEM] if ride else VMEM, VMEM, VMEM, VMEM],
        out_specs=[HBM, HBM, VMEM],
        input_output_aliases={(5 if ride else 4): 2},
        scratch_shapes=[
            pltpu.VMEM((nv, sl * al, cl), f32),
            pltpu.VMEM((nv, (sl + 2 * W - 2) * al, cl), f32),
            field,
            field,
            pltpu.VMEM((nv + 1, (ng + 2) * br, 128), f32),
            strips,
            strips,
            pltpu.VMEM((nv, ng * br, 128), f32),
            pltpu.VMEM((3 * nv * nv, 8, 128), f32),
            pltpu.SemaphoreType.DMA((5,)),
        ],
        compiler_params=params,
        name="segments",
    )(flux_jacobian, harmonic_list, blade_count, shares, ext, from_left, from_right)
    return new.reshape(nv, sl, al, cl), res.reshape(nv, sl, al, cl)


def solution(mesh):
    return jax.shard_map(
        local,
        mesh=mesh,
        in_specs=(
            P(None, ("span", "axial"), "circ"),
            P(),
            P(),
            P("span"),
            P("span"),
            P(None, "span", "axial", "circ"),
            P("span", "axial", "circ"),
            P(),
        ),
        out_specs=(P(None, "span", "axial", "circ"), P(None, "span", "axial", "circ")),
        check_vma=False,
    )
```

```python
import functools

import jax
import jax.numpy as jnp
import numpy as np
from jax import lax
from jax.experimental import pallas as pl
from jax.experimental.pallas import tpu as pltpu
from jax.sharding import PartitionSpec as P

SEGMENT_COEF = (0.25, 1.0 / 3.0, 0.5, 1.0)
DISSIP = 0.2
STEP = 4
W = 4
HIGH = lax.Precision.HIGHEST
VMEM = pl.BlockSpec(memory_space=pltpu.VMEM)
SMEM = pl.BlockSpec(memory_space=pltpu.SMEM)
HBM = pl.BlockSpec(memory_space=pltpu.HBM)
ANY = pl.BlockSpec(memory_space=pl.ANY)
AXES = ("circ", "span", "axial")


def make_basis(harm, blade, nh, cells, ncells):
    width = cells.shape[1]
    row = lax.broadcasted_iota(jnp.int32, (nh, width), 0)
    waves = jnp.zeros((nh, width), jnp.int32)
    for k in range(nh):
        waves = jnp.where(row == k, harm[k] * blade[0], waves)
    phase = waves * cells
    phase = phase & (ncells - 1) if ncells & (ncells - 1) == 0 else phase % ncells
    angle = (2.0 * np.pi) * phase.astype(jnp.float32) / ncells
    return jnp.concatenate([jnp.cos(angle), jnp.sin(angle)], axis=0)


def dot(a, b, dims):
    return lax.dot_general(a, b, (dims, ((), ())), precision=HIGH, preferred_element_type=jnp.float32)


def axial_kernel(dims, state, dt, rotor, blade, harm, edge, bulk, part, *scratch):
    nv, sl, al, cl, nh = (dims[k] for k in ("nv", "sl", "al", "cl", "nh"))
    cells, dt_cells, rotor_v, blade_s, harm_s, sems = scratch
    axial = lax.axis_index("axial")
    circ = lax.axis_index("circ")
    swap = dims["n_axial"] == 2
    size = cells.shape[2]
    at = pl.multiple_of(jnp.where(axial == 0, al - size, 0), 8) if swap else 0
    copies = [
        pltpu.make_async_copy(state.at[:, :, pl.ds(at, size), :], cells, sems.at[0]),
        pltpu.make_async_copy(dt.at[:, pl.ds(at, size), :], dt_cells, sems.at[1]),
        pltpu.make_async_copy(rotor, rotor_v, sems.at[2]),
        pltpu.make_async_copy(blade, blade_s, sems.at[3]),
        pltpu.make_async_copy(harm, harm_s, sems.at[4]),
    ]
    for copy in copies:
        copy.start()
    for copy in copies[2:]:
        copy.wait()
    ncells = cl * dims["n_circ"]
    here = circ * cl + lax.broadcasted_iota(jnp.int32, (1, cl), 1)
    basis = make_basis(harm_s, blade_s, nh, here, ncells)
    rl = rotor_v.shape[1]
    flat = rotor_v[...].reshape(nv * rl, cl)
    part[...] = jnp.zeros_like(part)
    part[:, : nv * rl] = dot(basis, flat, ((1,), (1,))) * (2.0 / ncells)
    for copy in copies[:2]:
        copy.wait()

    def put(side, base):
        for f in range(nv + 1):
            for i in range(W):
                ref = cells.at[f] if f < nv else dt_cells
                rows = ref[:, base + i, :]
                edge[side, f, i, 0:W] = rows[0:W]
                edge[side, f, i, W:] = rows[sl - W :]
                bulk[side, f, i] = rows[W : sl - W]

    if swap:

        @pl.when(axial == 0)
        def _():
            put(0, size - W)

        @pl.when(axial != 0)
        def _():
            put(0, 0)

    else:
        put(0, size - W)
        put(1, 0)


def inter_rows(dims, parts, firsts, donor, weight):
    nv = dims["nv"]
    rl = dims["rl"]
    table = jnp.concatenate([p[:, : nv * rl] for p in parts], axis=1)
    rows = table.shape[1]
    row = lax.broadcasted_iota(jnp.int32, (rows, 128), 0)
    station = row % rl
    for i, first in enumerate(firsts):
        station = station + jnp.where(row // (nv * rl) == i, first, 0)
    mix = jnp.where(station == donor, 1.0 - weight, jnp.where(station == donor + 1, weight, 0.0))
    var = row // rl % nv
    return [dot(table, jnp.where(var == v, mix, 0.0), ((1,), (0,))) for v in range(nv)]


def span_kernel(dims, s_head, s_tail, d_head, d_tail, lo, hi, part, other, before, donor, weight, down, up, inter):
    nv, sl, al, cl, br, nh = (dims[k] for k in ("nv", "sl", "al", "cl", "br", "nh"))
    span = lax.axis_index("span")
    faces = (lo,) if dims["n_axial"] == 2 else (lo, hi)
    rows_of = (nv + 1) * W * (al + W * len(faces))
    for out, s_ref, d_ref, at in ((down, s_head, d_head, 0), (up, s_tail, d_tail, W)):
        for f in range(nv + 1):
            rows = slice(f * W * al, (f + 1) * W * al)
            out[rows, :] = s_ref[f] if f < nv else d_ref[...]
            for side, src in enumerate(faces):
                for i in range(W):
                    to = (nv + 1) * W * al + ((side * (nv + 1) + f) * W + i) * W
                    out[to : to + W, :] = src[f, i, at : at + W, :]

    if not dims["ride"]:
        return
    rl = dims["rl"]
    first = span * 2 * rl
    shares = inter_rows(
        dims, [part[...], other[...], before[...]], [first, first + rl, first - rl], donor[...], weight[...]
    )
    lane = lax.broadcasted_iota(jnp.int32, (2 * nh, 128), 1)
    head = tail = jnp.zeros((2 * nh, 128), jnp.float32)
    for v in range(nv):
        inter[v] = shares[v]
        mine = lane // W == v
        head = jnp.where(mine, pltpu.roll(shares[v], W * v, 1), head)
        tail = jnp.where(mine, pltpu.roll(shares[v], (W * v - (sl - W)) % 128, 1), tail)
    down[rows_of:, :] = head
    up[rows_of:, :] = tail


def lane_ids(rows=8):
    return lax.broadcasted_iota(jnp.int32, (rows, 128), 1)


def gather_strips(dims, load, store, tiles):
    nb, ng, br = dims["nb"], dims["ng"], dims["br"]
    group = lane_ids() // 8
    for g in range(ng):
        for t in tiles:
            acc = jnp.zeros((8, 128), jnp.float32)
            for r in range((nb - 1 - g) // ng + 1):
                part = pltpu.roll(load((ng * r + g) * br + 8 * t), (8 * r + 4) % 128, 1)
                acc = jnp.where(group == r, part, acc)
            store(g * br + 8 * t, acc)


def circ_kernel(
    dims, state, dt, lo_edge, hi_edge, lo, hi, below, above, inter, ext, left, right, share, strips
):
    nv, sl, al, cl, br, nb, ng, nh = (dims[k] for k in ("nv", "sl", "al", "cl", "br", "nb", "ng", "nh"))
    axial = lax.axis_index("axial")
    turns = al // 8
    for f in range(nv + 1):
        for s in range(sl):
            for t in range(turns):
                rows = pl.ds(s * al + t, 8, stride=turns)
                at = (s + W) * br + 8 * (t + 1)
                ext[f, at : at + 8, :] = state[f, rows, :] if f < nv else dt[rows, :]

    swap = dims["n_axial"] == 2
    for side, (edge, bulk, valid) in enumerate(
        ((lo_edge, lo, axial > 0), (hi_edge, hi, axial < dims["n_axial"] - 1))
    ):
        base = 0 if side else W

        def fill(edge, bulk, side, base):
            for f in range(nv + 1):
                for i in range(W):
                    part = (nv + 1) * W * al + (((0 if swap else side) * (nv + 1) + f) * W + i) * W
                    pieces = (
                        (0, W, lambda: below[part : part + W, :]),
                        (W, W, lambda: edge[f, i, 0:W]),
                        (2 * W, sl - 2 * W, lambda: bulk[f, i]),
                        (sl, W, lambda: edge[f, i, W:]),
                        (sl + W, W, lambda: above[part : part + W, :]),
                    )
                    for at, n, read in pieces:
                        val = jnp.zeros((n, cl), jnp.float32) if edge is None else read()
                        ext[f, pl.ds(base + at * br + i, n, stride=br), :] = val

        @pl.when(valid)
        def _(edge=edge, bulk=bulk, side=side, base=base):
            fill(edge, bulk, side, base)

        @pl.when(jnp.logical_not(valid))
        def _(side=side, base=base):
            fill(None, None, side, base)

    for f in range(nv + 1):
        for j in range(W):
            for src, b in ((below, j), (above, sl + W + j)):
                for t in range(turns):
                    at = b * br + 8 * (t + 1)
                    ext[f, at : at + 8, :] = src[pl.ds((f * W + j) * al + t, 8, stride=turns), :]

    def each(f, carry):
        def store(row, val):
            strips[f, row : row + 8, :] = val

        gather_strips(dims, lambda row: ext[f, row : row + 8, :], store, range(br // 8))
        return carry

    lax.fori_loop(0, nv + 1, each, 0)
    half = (nv + 1) // 2
    low = lane_ids(ng * br) % 8 < 4
    for f in range(half):
        one, two = strips[f], strips[f + half]
        rows = slice(f * ng * br, (f + 1) * ng * br)
        right[rows, :] = jnp.where(low, one, pltpu.roll(two, 4, 1))
        left[rows, :] = jnp.where(low, pltpu.roll(one, 124, 1), two)

    if not dims["ride"]:
        return
    wide = sl + 2 * W
    lane = lax.broadcasted_iota(jnp.int32, (2 * nh, 128), 1)
    rows = slice((nv + 1) * W * (al + W * (1 if swap else 2)), None)
    packed = [jnp.zeros((2 * nh, 128), jnp.float32)] * dims["packs"]
    for v in range(nv):
        whole = pltpu.roll(inter[v], W, 1)
        whole = jnp.where(lane < W, pltpu.roll(below[rows, :], (-W * v) % 128, 1), whole)
        whole = jnp.where(lane >= sl + W, pltpu.roll(above[rows, :], sl + W - W * v, 1), whole)
        pack, first = divmod(v, 128 // wide)
        first = first * wide
        packed[pack] = jnp.where(
            (lane >= first) & (lane < first + wide), pltpu.roll(whole, first, 1), packed[pack]
        )
    for i in range(dims["packs"]):
        at = half * ng * br + i * 2 * nh
        left[at : at + 2 * nh, :] = packed[i]
        right[at : at + 2 * nh, :] = packed[i]
        share[i * 2 * nh : (i + 1) * 2 * nh, :] = packed[i]


def ghost_table(dims, table, span):
    nv, sl, nh = (dims[k] for k in ("nv", "sl", "nh"))
    rows, width = table.shape
    donors = pltpu.roll(table[rows - 8 :, :], lax.rem(width - span * sl + W, width), 1)[:, :128]
    lane = lax.broadcasted_iota(jnp.int32, (1, 128), 1)
    where = span * sl - W + lane
    inside = (where >= 0) & (where < sl * dims["n_span"]) & (lane < sl + 2 * W)
    station = lax.broadcasted_iota(jnp.int32, (width, 128), 0)
    donor = (donors[0:1, :] + 0.5).astype(jnp.int32)
    weight = donors[1:2, :]
    mix = jnp.where(station == donor, 1.0 - weight, jnp.where(station == donor + 1, weight, 0.0))
    mix = jnp.where(inside, mix, 0.0)
    inter = dot(table[0 : rows - 8, :], mix, ((1,), (0,)))
    return [inter[v * 2 * nh : (v + 1) * 2 * nh, :] for v in range(nv)]


def step_kernel(
    dims, jac, harm, blade, shares, _, from_left, from_right, new, res, ext, new_v, res_v, q_a, q_b, p_0, p_a, p_b, edge, coef, sem
):
    nv, sl, al, cl, br, nb, ng, nh = (dims[k] for k in ("nv", "sl", "al", "cl", "br", "nb", "ng", "nh"))
    axial = lax.axis_index("axial")
    span = lax.axis_index("span")
    circ = lax.axis_index("circ")
    spare = (W - 1) * al
    parts = 4 if sl % 8 == 0 else 1
    for d in range(3):
        for u in range(nv):
            for v in range(nv):
                value = (jac[d, u, v] * 0.5 - (DISSIP if u == v else 0.0)) * (0.5 / DISSIP)
                coef[(d * nv + u) * nv + v] = jnp.full((8, 128), value, jnp.float32)

    half = (nv + 1) // 2
    low = lane_ids(ng * br) % 8 < 4
    for f in range(half):
        rows = slice(f * ng * br, (f + 1) * ng * br)
        one, two = from_left[rows, :], from_right[rows, :]
        p_0[f, br : (ng + 1) * br, :] = jnp.where(low, one, pltpu.roll(two, 4, 1))
        p_0[f + half, br : (ng + 1) * br, :] = jnp.where(low, pltpu.roll(one, 124, 1), two)

    ncells = cl * dims["n_circ"]
    lane = lax.broadcasted_iota(jnp.int32, (1, 128), 1)
    wide = sl + 2 * W
    if dims["ride"]:
        rows = slice(half * ng * br, None)
        packed = from_left[rows, :] + from_right[rows, :] + shares[0][...] + shares[1][...]
        inter = []
        for v in range(nv):
            pack, first = divmod(v, 128 // wide)
            part = pltpu.roll(packed[pack * 2 * nh : (pack + 1) * 2 * nh, :], (-first * wide) % 128, 1)
            inter.append(jnp.where(lane < wide, part, 0.0))
    else:
        inter = ghost_table(dims, shares, span)
    start = circ * cl
    own = make_basis(harm, blade, nh, start + lax.broadcasted_iota(jnp.int32, (1, cl), 1), ncells)
    pos = lane % 8
    halo_cells = lax.rem(start + jnp.where(pos < 4, pos - 4, pos + cl - 4) + ncells, ncells)
    halo = make_basis(harm, blade, nh, halo_cells, ncells)
    s_id = lax.broadcasted_iota(jnp.int32, (128, 128), 0)
    r_id = lax.broadcasted_iota(jnp.int32, (128, 128), 1) // 8

    @pl.when(axial == 0)
    def _():
        for v in range(nv):
            part = inter[v]
            ghost = dot(part, own, ((0,), (0,)))
            ext[v, pl.ds(7, sl + 2 * W, stride=br), :] = ghost[: sl + 2 * W, :]
            ghost = dot(part, halo, ((0,), (0,)))
            for g in range(ng):
                picked = jnp.where(s_id == ng * r_id + g, ghost, 0.0)
                at = (g + 1) * br + 7
                p_0[v, at : at + 1, :] = jnp.sum(picked, axis=0, keepdims=True)

    lanes = lane_ids()
    first_lane, last_lane = lanes == 0, lanes == 127
    pos3, pos4 = lanes % 8 == 3, lanes % 8 == 4
    last = (ng + 1) * br

    def apply(cells):
        sums = [[3.0 * q for q in c["q"]] for c in cells]
        for d, name in enumerate(("axial", "span", "theta")):
            diff = []
            for c, total in zip(cells, sums):
                diff.append([p - m for p, m in zip(c[name + "+"], c[name + "-"])])
                for u in range(nv):
                    total[u] = total[u] - c[name + "-"][u]
            for v in range(nv):
                for u in range(nv):
                    k = coef[(d * nv + u) * nv + v]
                    for i in range(len(cells)):
                        sums[i][u] = sums[i][u] + k * diff[i][v]
        return sums

    turns = al // 8
    sub = lax.broadcasted_iota(jnp.int32, (8, 128), 0)
    top, bottom = sub == 0, sub == 7

    def block_cells(view, at):
        memo = {}

        def load(t, off=0):
            if (t, off) not in memo:
                row = at + off + 8 * t
                memo[t, off] = [view[v, row : row + 8, :] for v in range(nv)]
            return memo[t, off]

        def rolled(t, amount):
            if (t, "roll", amount) not in memo:
                memo[t, "roll", amount] = [pltpu.roll(x, amount, 0) for x in load(t)]
            return memo[t, "roll", amount]

        def choose(mask, one, two):
            return [jnp.where(mask, x, y) for x, y in zip(one, two)]

        def values(t):
            if t == 0:
                plus = choose(bottom, rolled(1, 7), rolled(0, 7))
                minus = choose(top, rolled(turns, 1), rolled(0, 1))
            else:
                plus = load(t + 1) if t < turns else choose(bottom, rolled(0, 7), rolled(1, 7))
                minus = load(t - 1) if t > 1 else choose(top, rolled(0, 1), rolled(turns, 1))
            return {"q": load(t), "axial-": minus, "axial+": plus, "span-": load(t, -br), "span+": load(t, br)}

        return values

    def turn(cell, beyond, at_plus, at_minus):
        cell["theta+"] = [
            pltpu.roll(jnp.where(at_plus, z, q), 127, 1) for z, q in zip(beyond, cell["q"])
        ]
        cell["theta-"] = [pltpu.roll(jnp.where(at_minus, z, q), 1, 1) for z, q in zip(beyond, cell["q"])]

    writes = [pltpu.make_async_copy(res_v.at[:, pl.ds(spare, sl * al), :], res, sem.at[0])]

    def stage(number, src, p_src, dst, p_dst):
        width = W - 1 - number
        factor = SEGMENT_COEF[number]
        final = number == len(SEGMENT_COEF) - 1
        for v in range(nv):
            p_src[v, 0:br, :] = pltpu.roll(p_src[v, last - br : last, :], 8, 1)
            p_src[v, last : last + br, :] = pltpu.roll(p_src[v, br : 2 * br, :], 120, 1)

        def blocks(b, count, first):
            around = pl.multiple_of((b - 1) * br, 8)
            view = src.at[:, pl.ds(around, (count + 2) * br), :]
            values = [block_cells(view, (i + 1) * br) for i in range(count)]
            groups = [
                [(i, t) for i in range(j, min(j + 2, count)) for t in range(1, turns + 1)] for j in range(0, count, 2)
            ]
            if first == 0:
                groups.append([(i, 0) for i in range(count)])

            def prepare(group):
                cells = []
                for i, t in group:
                    r = (b + i) // ng
                    g = b + i - r * ng
                    p_row = pl.multiple_of((g + 1) * br, 8) + 8 * t
                    row = pl.multiple_of((b + i) * br, 8) + 8 * t
                    cell = values[i](t)
                    beyond = [pltpu.roll(p_src[v, pl.ds(p_row, 8), :], 124 - 8 * r, 1) for v in range(nv)]
                    turn(cell, beyond, first_lane, last_lane)
                    cell["base"] = [ext[u, pl.ds(row, 8), :] for u in range(nv)] if number else cell["q"]
                    cell["step"] = (2.0 * DISSIP * factor) * ext[nv, pl.ds(row, 8), :]
                    cells.append(cell)
                return cells

            cells = prepare(groups[0])
            for n, group in enumerate(groups):
                following = prepare(groups[n + 1]) if n + 1 < len(groups) else None
                results = apply(cells)
                for (i, t), cell, result in zip(group, cells, results):
                    row = pl.multiple_of((b + i) * br, 8) + 8 * t
                    for u in range(nv):
                        value = cell["base"][u] - cell["step"] * result[u]
                        if final:
                            rows = pl.ds(pl.multiple_of((b + i - W) * al, 8) + t - 1, 8, stride=turns)
                            new_v[u, rows, :] = value
                        else:
                            dst[u, pl.ds(row, 8), :] = value
                            if t > 0 and number == 0:
                                rows = pl.ds(pl.multiple_of((b + i - 1) * al, 8) + t - 1, 8, stride=turns)
                                res_v[u, rows, :] = (2.0 * DISSIP) * result[u]
                cells = following

        def run(start, count, first):
            def loop(j, carry):
                blocks(start + STEP * j, STEP, first)
                return carry

            lax.fori_loop(0, count // STEP, loop, 0)
            if count % STEP:
                blocks(start + count // STEP * STEP, count % STEP, first)

        if final:
            for i in range(parts):
                run(W + i * (sl // parts), sl // parts, 1)
                rows = pl.ds(i * (sl // parts) * al, sl // parts * al)
                copy = pltpu.make_async_copy(new_v.at[:, rows, :], new.at[:, rows, :], sem.at[i + 1])
                copy.start()
                writes.append(copy)
        else:
            run(W - width, sl + 2 * width, 0)
        if number == 0:
            writes[0].start()
        if final:
            return

        def edges(v, carry):
            def store(row, val):
                edge[v, row : row + 8, :] = val

            gather_strips(dims, lambda row: src[v, row : row + 8, :], store, range(br // 8))
            return carry

        lax.fori_loop(0, nv, edges, 0)

        def strip(g, carry):
            base = pl.multiple_of((g + 1) * br, 8)
            around = pl.multiple_of(g * br, 8)
            view = p_src.at[:, pl.ds(around, 3 * br), :]

            values = block_cells(view, br)
            for t in range(br // 8):
                cell = values(t)
                turn(cell, [edge[v, pl.ds(around + 8 * t, 8), :] for v in range(nv)], pos4, pos3)
                (result,) = apply([cell])
                step = (2.0 * DISSIP * factor) * p_0[nv, pl.ds(base + 8 * t, 8), :]
                for u in range(nv):
                    p_dst[u, pl.ds(base + 8 * t, 8), :] = p_0[u, pl.ds(base + 8 * t, 8), :] - step * result[u]
            return carry

        lax.fori_loop(0, ng, strip, 0)

    stage(0, ext, p_0, q_a, p_a)
    stage(1, q_a, p_a, q_b, p_b)
    stage(2, q_b, p_b, q_a, p_a)
    stage(3, q_a, p_a, None, None)
    for copy in writes:
        copy.wait()


def shift_pairs(count, step, closed):
    return [(i, (i + step) % count) for i in range(count) if closed or 0 <= i + step < count]


def coef_table(part, donor_index, donor_weight, rl, nv, sizes):
    n_circ, n_span, n_axial = sizes
    modes, sl = part.shape[0], donor_index.shape[0]
    width = -(-max(rl * n_span * n_axial, sl * n_span) // 128) * 128
    circ, span, axial = (lax.axis_index(a) for a in AXES)
    rows = part[:, : nv * rl].reshape(modes, nv, rl).transpose(1, 0, 2).reshape(nv * modes, rl)
    table = jnp.zeros((nv * modes + 8, width), jnp.float32)
    table = lax.dynamic_update_slice(table, rows, (0, (span * n_axial + axial) * rl))
    donors = jnp.stack([donor_index.astype(jnp.float32), donor_weight])
    donors = jnp.where((circ == 0) & (axial == 0), donors, 0.0)
    table = lax.dynamic_update_slice(table, donors, (nv * modes, span * sl))
    return lax.psum(table, AXES)


def local(rotor_outlet, blade_count, harmonic_list, donor_index, donor_weight, state, time_step, flux_jacobian):
    f32 = jnp.float32
    n_circ, n_span, n_axial = (lax.axis_size(a) for a in AXES)
    nv, sl, al, cl = state.shape
    br = al + 2 * W
    nb = sl + 2 * W
    ng = -(-nb // 16)
    nh = harmonic_list.shape[0]
    dims = dict(
        nv=nv, sl=sl, al=al, cl=cl, br=br, nb=nb, ng=ng, nh=nh, n_circ=n_circ, n_span=n_span, n_axial=n_axial
    )
    rl = rotor_outlet.shape[1]
    packs = -(-nv // (128 // (sl + 2 * W)))
    ride = n_axial == 2 and n_circ == 4 and nv * rl <= 128
    dims.update(rl=rl, packs=packs, ride=ride)
    params = pltpu.CompilerParams(vmem_limit_bytes=48 * 2**20)
    sides = 1 if n_axial == 2 else 2
    deep = 8 if n_axial == 2 else al

    edge, bulk, part = pl.pallas_call(
        functools.partial(axial_kernel, dims),
        out_shape=[
            jax.ShapeDtypeStruct((sides, nv + 1, W, 2 * W, cl), f32),
            jax.ShapeDtypeStruct((sides, nv + 1, W, sl - 2 * W, cl), f32),
            jax.ShapeDtypeStruct((2 * nh, -(-nv * rl // 128) * 128), f32),
        ],
        in_specs=[HBM] * 5,
        out_specs=[VMEM] * 3,
        scratch_shapes=[
            pltpu.VMEM((nv, sl, deep, cl), f32),
            pltpu.VMEM((sl, deep, cl), f32),
            pltpu.VMEM(rotor_outlet.shape, f32),
            pltpu.SMEM(blade_count.shape, jnp.int32),
            pltpu.SMEM(harmonic_list.shape, jnp.int32),
            pltpu.SemaphoreType.DMA((5,)),
        ],
        compiler_params=pltpu.CompilerParams(vmem_limit_bytes=63 * 2**20),
        name="axial_faces",
    )(state, time_step, rotor_outlet, blade_count, harmonic_list)
    state = state.reshape(nv, sl * al, cl)
    time_step = time_step.reshape(sl * al, cl)

    def axial_move(faces):
        if n_axial == 2:
            moved = lax.ppermute(faces[0], "axial", [(0, 1), (1, 0)])
            return moved, moved
        lo = lax.ppermute(faces[0], "axial", shift_pairs(n_axial, 1, False))
        hi = lax.ppermute(faces[1], "axial", shift_pairs(n_axial, -1, False))
        return lo, hi

    lo_edge, hi_edge = axial_move(edge)
    bulk, lo_edge, hi_edge = lax.optimization_barrier((bulk, lo_edge, hi_edge))
    if ride:
        other = lax.ppermute(part, "axial", [(0, 1), (1, 0)])
        before = lax.ppermute(part, ("span", "axial"), shift_pairs(n_span * n_axial, 1, False))
        shares = None
    else:
        other = before = part
        shares = coef_table(part, donor_index, donor_weight, rl, nv, (n_circ, n_span, n_axial))
    lo, hi = axial_move(bulk)

    def spec(shape, *index):
        index = index or (0,) * len(shape)
        return pl.BlockSpec(shape, lambda i: index)

    faces = (nv + 1, W, 2 * W, cl)
    message = ((nv + 1) * W * (al + W * sides) + (2 * nh if ride else 0), cl)
    end = sl // W - 1
    pad = lambda x: jnp.pad(x, (0, 128 - sl))[None]
    down, up, inter = pl.pallas_call(
        functools.partial(span_kernel, dims),
        grid=(1,),
        out_shape=[jax.ShapeDtypeStruct(message, f32)] * 2 + [jax.ShapeDtypeStruct((nv, 2 * nh, 128), f32)],
        in_specs=[
            spec((nv, W * al, cl)),
            spec((nv, W * al, cl), 0, end, 0),
            spec((W * al, cl)),
            spec((W * al, cl), end, 0),
            spec(faces),
            spec(faces),
            spec(part.shape),
            spec(part.shape),
            spec(part.shape),
            spec((1, 128)),
            spec((1, 128)),
        ],
        out_specs=[spec(message), spec(message), spec((nv, 2 * nh, 128))],
        compiler_params=params,
        name="span_faces",
    )(
        state, state, time_step, time_step, lo_edge, hi_edge, part, other, before, pad(donor_index), pad(donor_weight)
    )
    below = lax.ppermute(up, "span", shift_pairs(n_span, 1, False))
    above = lax.ppermute(down, "span", shift_pairs(n_span, -1, False))

    strip = jax.ShapeDtypeStruct(((nv + 1) // 2 * ng * br + (packs * 2 * nh if ride else 0), 128), f32)
    ext, left, right, share = pl.pallas_call(
        functools.partial(circ_kernel, dims),
        out_shape=[
            jax.ShapeDtypeStruct((nv + 1, nb * br, cl), f32),
            strip,
            strip,
            jax.ShapeDtypeStruct((packs * 2 * nh, 128), f32),
        ],
        in_specs=[VMEM] * 9,
        out_specs=[VMEM] * 4,
        scratch_shapes=[pltpu.VMEM((nv + 1, ng * br, 128), f32)],
        compiler_params=params,
        name="circ_faces",
    )(state, time_step, lo_edge, hi_edge, lo, hi, below, above, inter)
    from_left = lax.ppermute(right, "circ", shift_pairs(n_circ, 1, True))
    from_right = lax.ppermute(left, "circ", shift_pairs(n_circ, -1, True))
    if ride:
        shares = [share, lax.ppermute(share, "circ", shift_pairs(n_circ, 2, True))]

    block = jax.ShapeDtypeStruct((nv, sl * al, cl), f32)
    field = pltpu.VMEM((nv, nb * br, cl), f32)
    strips = pltpu.VMEM((nv, (ng + 2) * br, 128), f32)
    new, res, _ = pl.pallas_call(
        functools.partial(step_kernel, dims),
        out_shape=[block, block, jax.ShapeDtypeStruct(ext.shape, f32)],
        in_specs=[SMEM, SMEM, SMEM, [VMEM, VMEM] if ride else VMEM, VMEM, VMEM, VMEM],
        out_specs=[HBM, HBM, VMEM],
        input_output_aliases={(5 if ride else 4): 2},
        scratch_shapes=[
            pltpu.VMEM((nv, sl * al, cl), f32),
            pltpu.VMEM((nv, (sl + 2 * W - 2) * al, cl), f32),
            field,
            field,
            pltpu.VMEM((nv + 1, (ng + 2) * br, 128), f32),
            strips,
            strips,
            pltpu.VMEM((nv, ng * br, 128), f32),
            pltpu.VMEM((3 * nv * nv, 8, 128), f32),
            pltpu.SemaphoreType.DMA((5,)),
        ],
        compiler_params=params,
        name="segments",
    )(flux_jacobian, harmonic_list, blade_count, shares, ext, from_left, from_right)
    return new.reshape(nv, sl, al, cl), res.reshape(nv, sl, al, cl)


def solution(mesh):
    return jax.shard_map(
        local,
        mesh=mesh,
        in_specs=(
            P(None, ("span", "axial"), "circ"),
            P(),
            P(),
            P("span"),
            P("span"),
            P(None, "span", "axial", "circ"),
            P("span", "axial", "circ"),
            P(),
        ),
        out_specs=(P(None, "span", "axial", "circ"), P(None, "span", "axial", "circ")),
        check_vma=False,
    )
```

```python
import functools

import jax
import jax.numpy as jnp
import numpy as np
from jax import lax
from jax.experimental import pallas as pl
from jax.experimental.pallas import tpu as pltpu
from jax.sharding import PartitionSpec as P

SEGMENT_COEF = (0.25, 1.0 / 3.0, 0.5, 1.0)
DISSIP = 0.2
STEP = 4
W = 4
HIGH = lax.Precision.HIGHEST
VMEM = pl.BlockSpec(memory_space=pltpu.VMEM)
SMEM = pl.BlockSpec(memory_space=pltpu.SMEM)
HBM = pl.BlockSpec(memory_space=pltpu.HBM)
ANY = pl.BlockSpec(memory_space=pl.ANY)
AXES = ("circ", "span", "axial")


def make_basis(harm, blade, nh, cells, ncells):
    width = cells.shape[1]
    row = lax.broadcasted_iota(jnp.int32, (nh, width), 0)
    waves = jnp.zeros((nh, width), jnp.int32)
    for k in range(nh):
        waves = jnp.where(row == k, harm[k] * blade[0], waves)
    phase = waves * cells
    phase = phase & (ncells - 1) if ncells & (ncells - 1) == 0 else phase % ncells
    angle = (2.0 * np.pi) * phase.astype(jnp.float32) / ncells
    return jnp.concatenate([jnp.cos(angle), jnp.sin(angle)], axis=0)


def dot(a, b, dims):
    return lax.dot_general(a, b, (dims, ((), ())), precision=HIGH, preferred_element_type=jnp.float32)


def coef_kernel(dims, rotor, blade, harm, after, part):
    del after
    nv, cl = dims["nv"], dims["cl"]
    ncells = cl * dims["n_circ"]
    here = lax.axis_index("circ") * cl + lax.broadcasted_iota(jnp.int32, (1, cl), 1)
    basis = make_basis(harm, blade, dims["nh"], here, ncells)
    rl = rotor.shape[1]
    part[...] = jnp.zeros_like(part)
    part[:, : nv * rl] = dot(basis, rotor[...].reshape(nv * rl, cl), ((1,), (1,))) * (2.0 / ncells)


def axial_kernel(dims, state, dt, edge, bulk, after):
    nv, sl, al = (dims[k] for k in ("nv", "sl", "al"))
    axial = lax.axis_index("axial")
    swap = dims["n_axial"] == 2
    size = al
    after[...] = jnp.zeros_like(after)

    def put(side, base):
        for f in range(nv + 1):
            for i in range(W):
                rows = state[f, :, base + i, :] if f < nv else dt[:, base + i, :]
                edge[side, f, i, 0:W] = rows[0:W]
                edge[side, f, i, W:] = rows[sl - W :]
                bulk[side, f, i] = rows[W : sl - W]

    if swap:

        @pl.when(axial == 0)
        def _():
            put(0, size - W)

        @pl.when(axial != 0)
        def _():
            put(0, 0)

    else:
        put(0, size - W)
        put(1, 0)


def inter_rows(dims, parts, firsts, donor, weight):
    nv = dims["nv"]
    rl = dims["rl"]
    table = jnp.concatenate([p[:, : nv * rl] for p in parts], axis=1)
    rows = table.shape[1]
    row = lax.broadcasted_iota(jnp.int32, (rows, 128), 0)
    station = row % rl
    for i, first in enumerate(firsts):
        station = station + jnp.where(row // (nv * rl) == i, first, 0)
    mix = jnp.where(station == donor, 1.0 - weight, jnp.where(station == donor + 1, weight, 0.0))
    var = row // rl % nv
    return [dot(table, jnp.where(var == v, mix, 0.0), ((1,), (0,))) for v in range(nv)]


def span_kernel(dims, s_head, s_tail, d_head, d_tail, lo, hi, part, other, before, donor, weight, down, up, inter):
    nv, sl, al, cl, br, nh = (dims[k] for k in ("nv", "sl", "al", "cl", "br", "nh"))
    span = lax.axis_index("span")
    faces = (lo,) if dims["n_axial"] == 2 else (lo, hi)
    rows_of = (nv + 1) * W * (al + W * len(faces))
    for out, s_ref, d_ref, at in ((down, s_head, d_head, 0), (up, s_tail, d_tail, W)):
        for f in range(nv + 1):
            rows = slice(f * W * al, (f + 1) * W * al)
            out[rows, :] = s_ref[f] if f < nv else d_ref[...]
            for side, src in enumerate(faces):
                for i in range(W):
                    to = (nv + 1) * W * al + ((side * (nv + 1) + f) * W + i) * W
                    out[to : to + W, :] = src[f, i, at : at + W, :]

    if not dims["ride"]:
        return
    rl = dims["rl"]
    first = span * 2 * rl
    shares = inter_rows(
        dims, [part[...], other[...], before[...]], [first, first + rl, first - rl], donor[...], weight[...]
    )
    lane = lax.broadcasted_iota(jnp.int32, (2 * nh, 128), 1)
    head = tail = jnp.zeros((2 * nh, 128), jnp.float32)
    for v in range(nv):
        inter[v] = shares[v]
        mine = lane // W == v
        head = jnp.where(mine, pltpu.roll(shares[v], W * v, 1), head)
        tail = jnp.where(mine, pltpu.roll(shares[v], (W * v - (sl - W)) % 128, 1), tail)
    down[rows_of:, :] = head
    up[rows_of:, :] = tail


def lane_ids(rows=8):
    return lax.broadcasted_iota(jnp.int32, (rows, 128), 1)


def gather_strips(dims, load, store, tiles):
    nb, ng, br = dims["nb"], dims["ng"], dims["br"]
    group = lane_ids() // 8
    for g in range(ng):
        for t in tiles:
            acc = jnp.zeros((8, 128), jnp.float32)
            for r in range((nb - 1 - g) // ng + 1):
                part = pltpu.roll(load((ng * r + g) * br + 8 * t), (8 * r + 4) % 128, 1)
                acc = jnp.where(group == r, part, acc)
            store(g * br + 8 * t, acc)


def circ_kernel(
    dims, state, dt, lo_edge, hi_edge, lo, hi, below, above, inter, ext, left, right, share, strips
):
    nv, sl, al, cl, br, nb, ng, nh = (dims[k] for k in ("nv", "sl", "al", "cl", "br", "nb", "ng", "nh"))
    axial = lax.axis_index("axial")
    turns = al // 8
    for f in range(nv + 1):
        for s in range(sl):
            for t in range(turns):
                rows = pl.ds(s * al + t, 8, stride=turns)
                at = (s + W) * br + 8 * (t + 1)
                ext[f, at : at + 8, :] = state[f, rows, :] if f < nv else dt[rows, :]

    swap = dims["n_axial"] == 2
    for side, (edge, bulk, valid) in enumerate(
        ((lo_edge, lo, axial > 0), (hi_edge, hi, axial < dims["n_axial"] - 1))
    ):
        base = 0 if side else W

        def fill(edge, bulk, side, base):
            for f in range(nv + 1):
                for i in range(W):
                    part = (nv + 1) * W * al + (((0 if swap else side) * (nv + 1) + f) * W + i) * W
                    pieces = (
                        (0, W, lambda: below[part : part + W, :]),
                        (W, W, lambda: edge[f, i, 0:W]),
                        (2 * W, sl - 2 * W, lambda: bulk[f, i]),
                        (sl, W, lambda: edge[f, i, W:]),
                        (sl + W, W, lambda: above[part : part + W, :]),
                    )
                    for at, n, read in pieces:
                        val = jnp.zeros((n, cl), jnp.float32) if edge is None else read()
                        ext[f, pl.ds(base + at * br + i, n, stride=br), :] = val

        @pl.when(valid)
        def _(edge=edge, bulk=bulk, side=side, base=base):
            fill(edge, bulk, side, base)

        @pl.when(jnp.logical_not(valid))
        def _(side=side, base=base):
            fill(None, None, side, base)

    for f in range(nv + 1):
        for j in range(W):
            for src, b in ((below, j), (above, sl + W + j)):
                for t in range(turns):
                    at = b * br + 8 * (t + 1)
                    ext[f, at : at + 8, :] = src[pl.ds((f * W + j) * al + t, 8, stride=turns), :]

    def each(f, carry):
        def store(row, val):
            strips[f, row : row + 8, :] = val

        gather_strips(dims, lambda row: ext[f, row : row + 8, :], store, range(br // 8))
        return carry

    lax.fori_loop(0, nv + 1, each, 0)
    half = (nv + 1) // 2
    low = lane_ids(ng * br) % 8 < 4
    for f in range(half):
        one, two = strips[f], strips[f + half]
        rows = slice(f * ng * br, (f + 1) * ng * br)
        right[rows, :] = jnp.where(low, one, pltpu.roll(two, 4, 1))
        left[rows, :] = jnp.where(low, pltpu.roll(one, 124, 1), two)

    if not dims["ride"]:
        return
    wide = sl + 2 * W
    lane = lax.broadcasted_iota(jnp.int32, (2 * nh, 128), 1)
    rows = slice((nv + 1) * W * (al + W * (1 if swap else 2)), None)
    packed = [jnp.zeros((2 * nh, 128), jnp.float32)] * dims["packs"]
    for v in range(nv):
        whole = pltpu.roll(inter[v], W, 1)
        whole = jnp.where(lane < W, pltpu.roll(below[rows, :], (-W * v) % 128, 1), whole)
        whole = jnp.where(lane >= sl + W, pltpu.roll(above[rows, :], sl + W - W * v, 1), whole)
        pack, first = divmod(v, 128 // wide)
        first = first * wide
        packed[pack] = jnp.where(
            (lane >= first) & (lane < first + wide), pltpu.roll(whole, first, 1), packed[pack]
        )
    for i in range(dims["packs"]):
        at = half * ng * br + i * 2 * nh
        left[at : at + 2 * nh, :] = packed[i]
        right[at : at + 2 * nh, :] = packed[i]
        share[i * 2 * nh : (i + 1) * 2 * nh, :] = packed[i]


def ghost_table(dims, table, span):
    nv, sl, nh = (dims[k] for k in ("nv", "sl", "nh"))
    rows, width = table.shape
    donors = pltpu.roll(table[rows - 8 :, :], lax.rem(width - span * sl + W, width), 1)[:, :128]
    lane = lax.broadcasted_iota(jnp.int32, (1, 128), 1)
    where = span * sl - W + lane
    inside = (where >= 0) & (where < sl * dims["n_span"]) & (lane < sl + 2 * W)
    station = lax.broadcasted_iota(jnp.int32, (width, 128), 0)
    donor = (donors[0:1, :] + 0.5).astype(jnp.int32)
    weight = donors[1:2, :]
    mix = jnp.where(station == donor, 1.0 - weight, jnp.where(station == donor + 1, weight, 0.0))
    mix = jnp.where(inside, mix, 0.0)
    inter = dot(table[0 : rows - 8, :], mix, ((1,), (0,)))
    return [inter[v * 2 * nh : (v + 1) * 2 * nh, :] for v in range(nv)]


def step_kernel(
    dims, jac, harm, blade, shares, _, from_left, from_right, new, res, ext, new_v, res_v, q_a, q_b, p_0, p_a, p_b, edge, coef, sem
):
    nv, sl, al, cl, br, nb, ng, nh = (dims[k] for k in ("nv", "sl", "al", "cl", "br", "nb", "ng", "nh"))
    axial = lax.axis_index("axial")
    span = lax.axis_index("span")
    circ = lax.axis_index("circ")
    spare = (W - 1) * al
    parts = 4 if sl % 8 == 0 else 1
    for d in range(3):
        for u in range(nv):
            for v in range(nv):
                value = (jac[d, u, v] * 0.5 - (DISSIP if u == v else 0.0)) * (0.5 / DISSIP)
                coef[(d * nv + u) * nv + v] = jnp.full((8, 128), value, jnp.float32)

    half = (nv + 1) // 2
    low = lane_ids(ng * br) % 8 < 4
    for f in range(half):
        rows = slice(f * ng * br, (f + 1) * ng * br)
        one, two = from_left[rows, :], from_right[rows, :]
        p_0[f, br : (ng + 1) * br, :] = jnp.where(low, one, pltpu.roll(two, 4, 1))
        p_0[f + half, br : (ng + 1) * br, :] = jnp.where(low, pltpu.roll(one, 124, 1), two)

    ncells = cl * dims["n_circ"]
    lane = lax.broadcasted_iota(jnp.int32, (1, 128), 1)
    wide = sl + 2 * W
    if dims["ride"]:
        rows = slice(half * ng * br, None)
        packed = from_left[rows, :] + from_right[rows, :] + shares[0][...] + shares[1][...]
        inter = []
        for v in range(nv):
            pack, first = divmod(v, 128 // wide)
            part = pltpu.roll(packed[pack * 2 * nh : (pack + 1) * 2 * nh, :], (-first * wide) % 128, 1)
            inter.append(jnp.where(lane < wide, part, 0.0))
    else:
        inter = ghost_table(dims, shares, span)
    start = circ * cl
    own = make_basis(harm, blade, nh, start + lax.broadcasted_iota(jnp.int32, (1, cl), 1), ncells)
    pos = lane % 8
    halo_cells = lax.rem(start + jnp.where(pos < 4, pos - 4, pos + cl - 4) + ncells, ncells)
    halo = make_basis(harm, blade, nh, halo_cells, ncells)
    s_id = lax.broadcasted_iota(jnp.int32, (128, 128), 0)
    r_id = lax.broadcasted_iota(jnp.int32, (128, 128), 1) // 8

    @pl.when(axial == 0)
    def _():
        for v in range(nv):
            part = inter[v]
            ghost = dot(part, own, ((0,), (0,)))
            ext[v, pl.ds(7, sl + 2 * W, stride=br), :] = ghost[: sl + 2 * W, :]
            ghost = dot(part, halo, ((0,), (0,)))
            for g in range(ng):
                picked = jnp.where(s_id == ng * r_id + g, ghost, 0.0)
                at = (g + 1) * br + 7
                p_0[v, at : at + 1, :] = jnp.sum(picked, axis=0, keepdims=True)

    lanes = lane_ids()
    first_lane, last_lane = lanes == 0, lanes == 127
    pos3, pos4 = lanes % 8 == 3, lanes % 8 == 4
    last = (ng + 1) * br

    def apply(cells):
        sums = [[3.0 * q for q in c["q"]] for c in cells]
        for d, name in enumerate(("axial", "span", "theta")):
            diff = []
            for c, total in zip(cells, sums):
                diff.append([p - m for p, m in zip(c[name + "+"], c[name + "-"])])
                for u in range(nv):
                    total[u] = total[u] - c[name + "-"][u]
            for v in range(nv):
                for u in range(nv):
                    k = coef[(d * nv + u) * nv + v]
                    for i in range(len(cells)):
                        sums[i][u] = sums[i][u] + k * diff[i][v]
        return sums

    turns = al // 8
    sub = lax.broadcasted_iota(jnp.int32, (8, 128), 0)
    top, bottom = sub == 0, sub == 7

    def block_cells(view, at):
        memo = {}

        def load(t, off=0):
            if (t, off) not in memo:
                row = at + off + 8 * t
                memo[t, off] = [view[v, row : row + 8, :] for v in range(nv)]
            return memo[t, off]

        def rolled(t, amount):
            if (t, "roll", amount) not in memo:
                memo[t, "roll", amount] = [pltpu.roll(x, amount, 0) for x in load(t)]
            return memo[t, "roll", amount]

        def choose(mask, one, two):
            return [jnp.where(mask, x, y) for x, y in zip(one, two)]

        def values(t):
            if t == 0:
                plus = choose(bottom, rolled(1, 7), rolled(0, 7))
                minus = choose(top, rolled(turns, 1), rolled(0, 1))
            else:
                plus = load(t + 1) if t < turns else choose(bottom, rolled(0, 7), rolled(1, 7))
                minus = load(t - 1) if t > 1 else choose(top, rolled(0, 1), rolled(turns, 1))
            return {"q": load(t), "axial-": minus, "axial+": plus, "span-": load(t, -br), "span+": load(t, br)}

        return values

    def turn(cell, beyond, at_plus, at_minus):
        cell["theta+"] = [
            pltpu.roll(jnp.where(at_plus, z, q), 127, 1) for z, q in zip(beyond, cell["q"])
        ]
        cell["theta-"] = [pltpu.roll(jnp.where(at_minus, z, q), 1, 1) for z, q in zip(beyond, cell["q"])]

    writes = [pltpu.make_async_copy(res_v.at[:, pl.ds(spare, sl * al), :], res, sem.at[0])]

    def stage(number, src, p_src, dst, p_dst):
        width = W - 1 - number
        factor = SEGMENT_COEF[number]
        final = number == len(SEGMENT_COEF) - 1
        for v in range(nv):
            p_src[v, 0:br, :] = pltpu.roll(p_src[v, last - br : last, :], 8, 1)
            p_src[v, last : last + br, :] = pltpu.roll(p_src[v, br : 2 * br, :], 120, 1)

        def blocks(b, count, first):
            around = pl.multiple_of((b - 1) * br, 8)
            view = src.at[:, pl.ds(around, (count + 2) * br), :]
            values = [block_cells(view, (i + 1) * br) for i in range(count)]
            groups = [
                [(i, t) for i in range(j, min(j + 2, count)) for t in range(1, turns + 1)] for j in range(0, count, 2)
            ]
            if first == 0:
                groups.append([(i, 0) for i in range(count)])

            def prepare(group):
                cells = []
                for i, t in group:
                    r = (b + i) // ng
                    g = b + i - r * ng
                    p_row = pl.multiple_of((g + 1) * br, 8) + 8 * t
                    row = pl.multiple_of((b + i) * br, 8) + 8 * t
                    cell = values[i](t)
                    beyond = [pltpu.roll(p_src[v, pl.ds(p_row, 8), :], 124 - 8 * r, 1) for v in range(nv)]
                    turn(cell, beyond, first_lane, last_lane)
                    cell["base"] = [ext[u, pl.ds(row, 8), :] for u in range(nv)] if number else cell["q"]
                    cell["step"] = (2.0 * DISSIP * factor) * ext[nv, pl.ds(row, 8), :]
                    cells.append(cell)
                return cells

            cells = prepare(groups[0])
            for n, group in enumerate(groups):
                following = prepare(groups[n + 1]) if n + 1 < len(groups) else None
                results = apply(cells)
                for (i, t), cell, result in zip(group, cells, results):
                    row = pl.multiple_of((b + i) * br, 8) + 8 * t
                    for u in range(nv):
                        value = cell["base"][u] - cell["step"] * result[u]
                        if final:
                            rows = pl.ds(pl.multiple_of((b + i - W) * al, 8) + t - 1, 8, stride=turns)
                            new_v[u, rows, :] = value
                        else:
                            dst[u, pl.ds(row, 8), :] = value
                            if t > 0 and number == 0:
                                rows = pl.ds(pl.multiple_of((b + i - 1) * al, 8) + t - 1, 8, stride=turns)
                                res_v[u, rows, :] = (2.0 * DISSIP) * result[u]
                cells = following

        def run(start, count, first):
            def loop(j, carry):
                blocks(start + STEP * j, STEP, first)
                return carry

            lax.fori_loop(0, count // STEP, loop, 0)
            if count % STEP:
                blocks(start + count // STEP * STEP, count % STEP, first)

        if final:
            for i in range(parts):
                run(W + i * (sl // parts), sl // parts, 1)
                rows = pl.ds(i * (sl // parts) * al, sl // parts * al)
                copy = pltpu.make_async_copy(new_v.at[:, rows, :], new.at[:, rows, :], sem.at[i + 1])
                copy.start()
                writes.append(copy)
        else:
            run(W - width, sl + 2 * width, 0)
        if number == 0:
            writes[0].start()
        if final:
            return

        def edges(v, carry):
            def store(row, val):
                edge[v, row : row + 8, :] = val

            gather_strips(dims, lambda row: src[v, row : row + 8, :], store, range(br // 8))
            return carry

        lax.fori_loop(0, nv, edges, 0)

        def strip(g, carry):
            base = pl.multiple_of((g + 1) * br, 8)
            around = pl.multiple_of(g * br, 8)
            view = p_src.at[:, pl.ds(around, 3 * br), :]

            values = block_cells(view, br)
            cells = [values(t) for t in range(br // 8)]
            for t, cell in enumerate(cells):
                turn(cell, [edge[v, pl.ds(around + 8 * t, 8), :] for v in range(nv)], pos4, pos3)
            for t, result in enumerate(apply(cells)):
                step = (2.0 * DISSIP * factor) * p_0[nv, pl.ds(base + 8 * t, 8), :]
                for u in range(nv):
                    p_dst[u, pl.ds(base + 8 * t, 8), :] = p_0[u, pl.ds(base + 8 * t, 8), :] - step * result[u]
            return carry

        lax.fori_loop(0, ng, strip, 0)

    stage(0, ext, p_0, q_a, p_a)
    stage(1, q_a, p_a, q_b, p_b)
    stage(2, q_b, p_b, q_a, p_a)
    stage(3, q_a, p_a, None, None)
    for copy in writes:
        copy.wait()


def shift_pairs(count, step, closed):
    return [(i, (i + step) % count) for i in range(count) if closed or 0 <= i + step < count]


def coef_table(part, donor_index, donor_weight, rl, nv, sizes):
    n_circ, n_span, n_axial = sizes
    modes, sl = part.shape[0], donor_index.shape[0]
    width = -(-max(rl * n_span * n_axial, sl * n_span) // 128) * 128
    circ, span, axial = (lax.axis_index(a) for a in AXES)
    rows = part[:, : nv * rl].reshape(modes, nv, rl).transpose(1, 0, 2).reshape(nv * modes, rl)
    table = jnp.zeros((nv * modes + 8, width), jnp.float32)
    table = lax.dynamic_update_slice(table, rows, (0, (span * n_axial + axial) * rl))
    donors = jnp.stack([donor_index.astype(jnp.float32), donor_weight])
    donors = jnp.where((circ == 0) & (axial == 0), donors, 0.0)
    table = lax.dynamic_update_slice(table, donors, (nv * modes, span * sl))
    return lax.psum(table, AXES)


def local(rotor_outlet, blade_count, harmonic_list, donor_index, donor_weight, state, time_step, flux_jacobian):
    f32 = jnp.float32
    n_circ, n_span, n_axial = (lax.axis_size(a) for a in AXES)
    nv, sl, al, cl = state.shape
    br = al + 2 * W
    nb = sl + 2 * W
    ng = -(-nb // 16)
    nh = harmonic_list.shape[0]
    dims = dict(
        nv=nv, sl=sl, al=al, cl=cl, br=br, nb=nb, ng=ng, nh=nh, n_circ=n_circ, n_span=n_span, n_axial=n_axial
    )
    rl = rotor_outlet.shape[1]
    packs = -(-nv // (128 // (sl + 2 * W)))
    ride = n_axial == 2 and n_circ == 4 and nv * rl <= 128
    dims.update(rl=rl, packs=packs, ride=ride)
    params = pltpu.CompilerParams(vmem_limit_bytes=48 * 2**20)
    sides = 1 if n_axial == 2 else 2

    edge, bulk, after = pl.pallas_call(
        functools.partial(axial_kernel, dims),
        out_shape=[
            jax.ShapeDtypeStruct((sides, nv + 1, W, 2 * W, cl), f32),
            jax.ShapeDtypeStruct((sides, nv + 1, W, sl - 2 * W, cl), f32),
            jax.ShapeDtypeStruct((8, 128), f32),
        ],
        in_specs=[VMEM] * 2,
        out_specs=[VMEM] * 3,
        compiler_params=params,
        name="axial_faces",
    )(state, time_step)
    part = pl.pallas_call(
        functools.partial(coef_kernel, dims),
        out_shape=jax.ShapeDtypeStruct((2 * nh, -(-nv * rl // 128) * 128), f32),
        in_specs=[VMEM, SMEM, SMEM, VMEM],
        out_specs=VMEM,
        compiler_params=params,
        name="coef_share",
    )(rotor_outlet, blade_count, harmonic_list, after)
    state = state.reshape(nv, sl * al, cl)
    time_step = time_step.reshape(sl * al, cl)

    def axial_move(faces):
        if n_axial == 2:
            moved = lax.ppermute(faces[0], "axial", [(0, 1), (1, 0)])
            return moved, moved
        lo = lax.ppermute(faces[0], "axial", shift_pairs(n_axial, 1, False))
        hi = lax.ppermute(faces[1], "axial", shift_pairs(n_axial, -1, False))
        return lo, hi

    lo_edge, hi_edge = axial_move(edge)
    if ride:
        other = lax.ppermute(part, "axial", [(0, 1), (1, 0)])
        before = lax.ppermute(part, ("span", "axial"), shift_pairs(n_span * n_axial, 1, False))
        shares = None
    else:
        other = before = part
        shares = coef_table(part, donor_index, donor_weight, rl, nv, (n_circ, n_span, n_axial))
    lo, hi = axial_move(bulk)

    def spec(shape, *index):
        index = index or (0,) * len(shape)
        return pl.BlockSpec(shape, lambda i: index)

    faces = (nv + 1, W, 2 * W, cl)
    message = ((nv + 1) * W * (al + W * sides) + (2 * nh if ride else 0), cl)
    end = sl // W - 1
    pad = lambda x: jnp.pad(x, (0, 128 - sl))[None]
    down, up, inter = pl.pallas_call(
        functools.partial(span_kernel, dims),
        grid=(1,),
        out_shape=[jax.ShapeDtypeStruct(message, f32)] * 2 + [jax.ShapeDtypeStruct((nv, 2 * nh, 128), f32)],
        in_specs=[
            spec((nv, W * al, cl)),
            spec((nv, W * al, cl), 0, end, 0),
            spec((W * al, cl)),
            spec((W * al, cl), end, 0),
            spec(faces),
            spec(faces),
            spec(part.shape),
            spec(part.shape),
            spec(part.shape),
            spec((1, 128)),
            spec((1, 128)),
        ],
        out_specs=[spec(message), spec(message), spec((nv, 2 * nh, 128))],
        compiler_params=params,
        name="span_faces",
    )(
        state, state, time_step, time_step, lo_edge, hi_edge, part, other, before, pad(donor_index), pad(donor_weight)
    )
    below = lax.ppermute(up, "span", shift_pairs(n_span, 1, False))
    above = lax.ppermute(down, "span", shift_pairs(n_span, -1, False))

    strip = jax.ShapeDtypeStruct(((nv + 1) // 2 * ng * br + (packs * 2 * nh if ride else 0), 128), f32)
    ext, left, right, share = pl.pallas_call(
        functools.partial(circ_kernel, dims),
        out_shape=[
            jax.ShapeDtypeStruct((nv + 1, nb * br, cl), f32),
            strip,
            strip,
            jax.ShapeDtypeStruct((packs * 2 * nh, 128), f32),
        ],
        in_specs=[VMEM] * 9,
        out_specs=[VMEM] * 4,
        scratch_shapes=[pltpu.VMEM((nv + 1, ng * br, 128), f32)],
        compiler_params=params,
        name="circ_faces",
    )(state, time_step, lo_edge, hi_edge, lo, hi, below, above, inter)
    from_left = lax.ppermute(right, "circ", shift_pairs(n_circ, 1, True))
    from_right = lax.ppermute(left, "circ", shift_pairs(n_circ, -1, True))
    if ride:
        shares = [share, lax.ppermute(share, "circ", shift_pairs(n_circ, 2, True))]

    block = jax.ShapeDtypeStruct((nv, sl * al, cl), f32)
    field = pltpu.VMEM((nv, nb * br, cl), f32)
    strips = pltpu.VMEM((nv, (ng + 2) * br, 128), f32)
    new, res, _ = pl.pallas_call(
        functools.partial(step_kernel, dims),
        out_shape=[block, block, jax.ShapeDtypeStruct(ext.shape, f32)],
        in_specs=[SMEM, SMEM, SMEM, [VMEM, VMEM] if ride else VMEM, VMEM, VMEM, VMEM],
        out_specs=[HBM, HBM, VMEM],
        input_output_aliases={(5 if ride else 4): 2},
        scratch_shapes=[
            pltpu.VMEM((nv, sl * al, cl), f32),
            pltpu.VMEM((nv, (sl + 2 * W - 2) * al, cl), f32),
            field,
            field,
            pltpu.VMEM((nv + 1, (ng + 2) * br, 128), f32),
            strips,
            strips,
            pltpu.VMEM((nv, ng * br, 128), f32),
            pltpu.VMEM((3 * nv * nv, 8, 128), f32),
            pltpu.SemaphoreType.DMA((5,)),
        ],
        compiler_params=params,
        name="segments",
    )(flux_jacobian, harmonic_list, blade_count, shares, ext, from_left, from_right)
    return new.reshape(nv, sl, al, cl), res.reshape(nv, sl, al, cl)


def solution(mesh):
    return jax.shard_map(
        local,
        mesh=mesh,
        in_specs=(
            P(None, ("span", "axial"), "circ"),
            P(),
            P(),
            P("span"),
            P("span"),
            P(None, "span", "axial", "circ"),
            P("span", "axial", "circ"),
            P(),
        ),
        out_specs=(P(None, "span", "axial", "circ"), P(None, "span", "axial", "circ")),
        check_vma=False,
    )
```

```python
import functools

import jax
import jax.numpy as jnp
import numpy as np
from jax import lax
from jax.experimental import pallas as pl
from jax.experimental.pallas import tpu as pltpu
from jax.sharding import PartitionSpec as P

SEGMENT_COEF = (0.25, 1.0 / 3.0, 0.5, 1.0)
DISSIP = 0.2
STEP = 4
W = 4
HIGH = lax.Precision.HIGHEST
VMEM = pl.BlockSpec(memory_space=pltpu.VMEM)
SMEM = pl.BlockSpec(memory_space=pltpu.SMEM)
HBM = pl.BlockSpec(memory_space=pltpu.HBM)
ANY = pl.BlockSpec(memory_space=pl.ANY)
AXES = ("circ", "span", "axial")


def make_basis(harm, blade, nh, cells, ncells):
    width = cells.shape[1]
    row = lax.broadcasted_iota(jnp.int32, (nh, width), 0)
    waves = jnp.zeros((nh, width), jnp.int32)
    for k in range(nh):
        waves = jnp.where(row == k, harm[k] * blade[0], waves)
    phase = waves * cells
    phase = phase & (ncells - 1) if ncells & (ncells - 1) == 0 else phase % ncells
    angle = (2.0 * np.pi) * phase.astype(jnp.float32) / ncells
    return jnp.concatenate([jnp.cos(angle), jnp.sin(angle)], axis=0)


def dot(a, b, dims):
    return lax.dot_general(a, b, (dims, ((), ())), precision=HIGH, preferred_element_type=jnp.float32)


def coef_kernel(dims, rotor, blade, harm, after, part):
    del after
    nv, cl = dims["nv"], dims["cl"]
    ncells = cl * dims["n_circ"]
    here = lax.axis_index("circ") * cl + lax.broadcasted_iota(jnp.int32, (1, cl), 1)
    basis = make_basis(harm, blade, dims["nh"], here, ncells)
    rl = rotor.shape[1]
    part[...] = jnp.zeros_like(part)
    part[:, : nv * rl] = dot(basis, rotor[...].reshape(nv * rl, cl), ((1,), (1,))) * (2.0 / ncells)


def axial_kernel(dims, state, dt, edge, bulk, after):
    nv, sl, al = (dims[k] for k in ("nv", "sl", "al"))
    axial = lax.axis_index("axial")
    swap = dims["n_axial"] == 2
    size = al
    after[...] = jnp.zeros_like(after)

    def put(side, base):
        for f in range(nv + 1):
            for i in range(W):
                rows = state[f, :, base + i, :] if f < nv else dt[:, base + i, :]
                edge[side, f, i, 0:W] = rows[0:W]
                edge[side, f, i, W:] = rows[sl - W :]
                bulk[side, f, i] = rows[W : sl - W]

    if swap:

        @pl.when(axial == 0)
        def _():
            put(0, size - W)

        @pl.when(axial != 0)
        def _():
            put(0, 0)

    else:
        put(0, size - W)
        put(1, 0)


def inter_rows(dims, parts, firsts, donor, weight):
    nv = dims["nv"]
    rl = dims["rl"]
    table = jnp.concatenate([p[:, : nv * rl] for p in parts], axis=1)
    rows = table.shape[1]
    row = lax.broadcasted_iota(jnp.int32, (rows, 128), 0)
    station = row % rl
    for i, first in enumerate(firsts):
        station = station + jnp.where(row // (nv * rl) == i, first, 0)
    mix = jnp.where(station == donor, 1.0 - weight, jnp.where(station == donor + 1, weight, 0.0))
    var = row // rl % nv
    return [dot(table, jnp.where(var == v, mix, 0.0), ((1,), (0,))) for v in range(nv)]


def span_kernel(dims, s_head, s_tail, d_head, d_tail, lo, hi, part, other, before, donor, weight, down, up, inter):
    nv, sl, al, cl, br, nh = (dims[k] for k in ("nv", "sl", "al", "cl", "br", "nh"))
    span = lax.axis_index("span")
    faces = (lo,) if dims["n_axial"] == 2 else (lo, hi)
    rows_of = (nv + 1) * W * (al + W * len(faces))
    for out, s_ref, d_ref, at in ((down, s_head, d_head, 0), (up, s_tail, d_tail, W)):
        for f in range(nv + 1):
            rows = slice(f * W * al, (f + 1) * W * al)
            out[rows, :] = s_ref[f] if f < nv else d_ref[...]
            for side, src in enumerate(faces):
                for i in range(W):
                    to = (nv + 1) * W * al + ((side * (nv + 1) + f) * W + i) * W
                    out[to : to + W, :] = src[f, i, at : at + W, :]

    if not dims["ride"]:
        return
    rl = dims["rl"]
    first = span * 2 * rl
    shares = inter_rows(
        dims, [part[...], other[...], before[...]], [first, first + rl, first - rl], donor[...], weight[...]
    )
    lane = lax.broadcasted_iota(jnp.int32, (2 * nh, 128), 1)
    head = tail = jnp.zeros((2 * nh, 128), jnp.float32)
    for v in range(nv):
        inter[v] = shares[v]
        mine = lane // W == v
        head = jnp.where(mine, pltpu.roll(shares[v], W * v, 1), head)
        tail = jnp.where(mine, pltpu.roll(shares[v], (W * v - (sl - W)) % 128, 1), tail)
    down[rows_of:, :] = head
    up[rows_of:, :] = tail


def lane_ids(rows=8):
    return lax.broadcasted_iota(jnp.int32, (rows, 128), 1)


def gather_strips(dims, load, store, tiles):
    nb, ng, br = dims["nb"], dims["ng"], dims["br"]
    group = lane_ids() // 8
    for g in range(ng):
        for t in tiles:
            acc = jnp.zeros((8, 128), jnp.float32)
            for r in range((nb - 1 - g) // ng + 1):
                part = pltpu.roll(load((ng * r + g) * br + 8 * t), (8 * r + 4) % 128, 1)
                acc = jnp.where(group == r, part, acc)
            store(g * br + 8 * t, acc)


def circ_kernel(
    dims, state, dt, lo_edge, hi_edge, lo, hi, below, above, inter, ext, left, right, share, strips
):
    nv, sl, al, cl, br, nb, ng, nh = (dims[k] for k in ("nv", "sl", "al", "cl", "br", "nb", "ng", "nh"))
    axial = lax.axis_index("axial")
    turns = al // 8
    for f in range(nv + 1):
        for s in range(sl):
            for t in range(turns):
                rows = pl.ds(s * al + t, 8, stride=turns)
                at = (s + W) * br + 8 * (t + 1)
                ext[f, at : at + 8, :] = state[f, rows, :] if f < nv else dt[rows, :]

    swap = dims["n_axial"] == 2
    for side, (edge, bulk, valid) in enumerate(
        ((lo_edge, lo, axial > 0), (hi_edge, hi, axial < dims["n_axial"] - 1))
    ):
        base = 0 if side else W

        def fill(edge, bulk, side, base):
            for f in range(nv + 1):
                for i in range(W):
                    part = (nv + 1) * W * al + (((0 if swap else side) * (nv + 1) + f) * W + i) * W
                    pieces = (
                        (0, W, lambda: below[part : part + W, :]),
                        (W, W, lambda: edge[f, i, 0:W]),
                        (2 * W, sl - 2 * W, lambda: bulk[f, i]),
                        (sl, W, lambda: edge[f, i, W:]),
                        (sl + W, W, lambda: above[part : part + W, :]),
                    )
                    for at, n, read in pieces:
                        val = jnp.zeros((n, cl), jnp.float32) if edge is None else read()
                        ext[f, pl.ds(base + at * br + i, n, stride=br), :] = val

        @pl.when(valid)
        def _(edge=edge, bulk=bulk, side=side, base=base):
            fill(edge, bulk, side, base)

        @pl.when(jnp.logical_not(valid))
        def _(side=side, base=base):
            fill(None, None, side, base)

    for f in range(nv + 1):
        for j in range(W):
            for src, b in ((below, j), (above, sl + W + j)):
                for t in range(turns):
                    at = b * br + 8 * (t + 1)
                    ext[f, at : at + 8, :] = src[pl.ds((f * W + j) * al + t, 8, stride=turns), :]

    def each(f, carry):
        def store(row, val):
            strips[f, row : row + 8, :] = val

        gather_strips(dims, lambda row: ext[f, row : row + 8, :], store, range(br // 8))
        return carry

    lax.fori_loop(0, nv + 1, each, 0)
    half = (nv + 1) // 2
    low = lane_ids(ng * br) % 8 < 4
    for f in range(half):
        one, two = strips[f], strips[f + half]
        rows = slice(f * ng * br, (f + 1) * ng * br)
        right[rows, :] = jnp.where(low, one, pltpu.roll(two, 4, 1))
        left[rows, :] = jnp.where(low, pltpu.roll(one, 124, 1), two)

    if not dims["ride"]:
        return
    wide = sl + 2 * W
    lane = lax.broadcasted_iota(jnp.int32, (2 * nh, 128), 1)
    rows = slice((nv + 1) * W * (al + W * (1 if swap else 2)), None)
    packed = [jnp.zeros((2 * nh, 128), jnp.float32)] * dims["packs"]
    for v in range(nv):
        whole = pltpu.roll(inter[v], W, 1)
        whole = jnp.where(lane < W, pltpu.roll(below[rows, :], (-W * v) % 128, 1), whole)
        whole = jnp.where(lane >= sl + W, pltpu.roll(above[rows, :], sl + W - W * v, 1), whole)
        pack, first = divmod(v, 128 // wide)
        first = first * wide
        packed[pack] = jnp.where(
            (lane >= first) & (lane < first + wide), pltpu.roll(whole, first, 1), packed[pack]
        )
    for i in range(dims["packs"]):
        at = half * ng * br + i * 2 * nh
        left[at : at + 2 * nh, :] = packed[i]
        right[at : at + 2 * nh, :] = packed[i]
        share[i * 2 * nh : (i + 1) * 2 * nh, :] = packed[i]


def ghost_table(dims, table, span):
    nv, sl, nh = (dims[k] for k in ("nv", "sl", "nh"))
    rows, width = table.shape
    donors = pltpu.roll(table[rows - 8 :, :], lax.rem(width - span * sl + W, width), 1)[:, :128]
    lane = lax.broadcasted_iota(jnp.int32, (1, 128), 1)
    where = span * sl - W + lane
    inside = (where >= 0) & (where < sl * dims["n_span"]) & (lane < sl + 2 * W)
    station = lax.broadcasted_iota(jnp.int32, (width, 128), 0)
    donor = (donors[0:1, :] + 0.5).astype(jnp.int32)
    weight = donors[1:2, :]
    mix = jnp.where(station == donor, 1.0 - weight, jnp.where(station == donor + 1, weight, 0.0))
    mix = jnp.where(inside, mix, 0.0)
    inter = dot(table[0 : rows - 8, :], mix, ((1,), (0,)))
    return [inter[v * 2 * nh : (v + 1) * 2 * nh, :] for v in range(nv)]


def step_kernel(
    dims, jac, harm, blade, shares, _, from_left, from_right, new, res, ext, new_v, res_v, q_a, q_b, p_0, p_a, p_b, edge, coef, sem
):
    nv, sl, al, cl, br, nb, ng, nh = (dims[k] for k in ("nv", "sl", "al", "cl", "br", "nb", "ng", "nh"))
    axial = lax.axis_index("axial")
    span = lax.axis_index("span")
    circ = lax.axis_index("circ")
    spare = (W - 1) * al
    parts = 4 if sl % 8 == 0 else 1
    for d in range(3):
        for u in range(nv):
            for v in range(nv):
                value = (jac[d, u, v] * 0.5 - (DISSIP if u == v else 0.0)) * (0.5 / DISSIP)
                coef[(d * nv + u) * nv + v] = jnp.full((8, 128), value, jnp.float32)

    half = (nv + 1) // 2
    low = lane_ids(ng * br) % 8 < 4
    for f in range(half):
        rows = slice(f * ng * br, (f + 1) * ng * br)
        one, two = from_left[rows, :], from_right[rows, :]
        p_0[f, br : (ng + 1) * br, :] = jnp.where(low, one, pltpu.roll(two, 4, 1))
        p_0[f + half, br : (ng + 1) * br, :] = jnp.where(low, pltpu.roll(one, 124, 1), two)

    ncells = cl * dims["n_circ"]
    lane = lax.broadcasted_iota(jnp.int32, (1, 128), 1)
    wide = sl + 2 * W
    if dims["ride"]:
        rows = slice(half * ng * br, None)
        packed = from_left[rows, :] + from_right[rows, :] + shares[0][...] + shares[1][...]
        inter = [packed[i * 2 * nh : (i + 1) * 2 * nh, :] for i in range(dims["packs"])]
        each = 128 // wide
    else:
        inter = ghost_table(dims, shares, span)
        each = 1
    start = circ * cl
    own = make_basis(harm, blade, nh, start + lax.broadcasted_iota(jnp.int32, (1, cl), 1), ncells)
    pos = lane % 8
    halo_cells = lax.rem(start + jnp.where(pos < 4, pos - 4, pos + cl - 4) + ncells, ncells)
    halo = make_basis(harm, blade, nh, halo_cells, ncells)
    s_id = lax.broadcasted_iota(jnp.int32, (wide, 128), 0)
    r_id = lax.broadcasted_iota(jnp.int32, (wide, 128), 1) // 8

    @pl.when(axial == 0)
    def _():
        ghosts = [dot(part, own, ((0,), (0,))) for part in inter]
        halos = [dot(part, halo, ((0,), (0,))) for part in inter]
        for v in range(nv):
            rows = slice(v % each * wide, (v % each + 1) * wide)
            ext[v, pl.ds(7, wide, stride=br), :] = ghosts[v // each][rows]
            for g in range(ng):
                picked = jnp.where(s_id == ng * r_id + g, halos[v // each][rows], 0.0)
                at = (g + 1) * br + 7
                p_0[v, at : at + 1, :] = jnp.sum(picked, axis=0, keepdims=True)

    lanes = lane_ids()
    first_lane, last_lane = lanes == 0, lanes == 127
    pos3, pos4 = lanes % 8 == 3, lanes % 8 == 4
    last = (ng + 1) * br

    def apply(cells):
        sums = [[3.0 * q for q in c["q"]] for c in cells]
        for d, name in enumerate(("axial", "span", "theta")):
            diff = []
            for c, total in zip(cells, sums):
                diff.append([p - m for p, m in zip(c[name + "+"], c[name + "-"])])
                for u in range(nv):
                    total[u] = total[u] - c[name + "-"][u]
            for v in range(nv):
                for u in range(nv):
                    k = coef[(d * nv + u) * nv + v]
                    for i in range(len(cells)):
                        sums[i][u] = sums[i][u] + k * diff[i][v]
        return sums

    turns = al // 8
    sub = lax.broadcasted_iota(jnp.int32, (8, 128), 0)
    top, bottom = sub == 0, sub == 7

    def block_cells(view, at):
        memo = {}

        def load(t, off=0):
            if (t, off) not in memo:
                row = at + off + 8 * t
                memo[t, off] = [view[v, row : row + 8, :] for v in range(nv)]
            return memo[t, off]

        def rolled(t, amount):
            if (t, "roll", amount) not in memo:
                memo[t, "roll", amount] = [pltpu.roll(x, amount, 0) for x in load(t)]
            return memo[t, "roll", amount]

        def choose(mask, one, two):
            return [jnp.where(mask, x, y) for x, y in zip(one, two)]

        def values(t):
            if t == 0:
                plus = choose(bottom, rolled(1, 7), rolled(0, 7))
                minus = choose(top, rolled(turns, 1), rolled(0, 1))
            else:
                plus = load(t + 1) if t < turns else choose(bottom, rolled(0, 7), rolled(1, 7))
                minus = load(t - 1) if t > 1 else choose(top, rolled(0, 1), rolled(turns, 1))
            return {"q": load(t), "axial-": minus, "axial+": plus, "span-": load(t, -br), "span+": load(t, br)}

        return values

    def turn(cell, beyond, at_plus, at_minus):
        cell["theta+"] = [
            pltpu.roll(jnp.where(at_plus, z, q), 127, 1) for z, q in zip(beyond, cell["q"])
        ]
        cell["theta-"] = [pltpu.roll(jnp.where(at_minus, z, q), 1, 1) for z, q in zip(beyond, cell["q"])]

    writes = [pltpu.make_async_copy(res_v.at[:, pl.ds(spare, sl * al), :], res, sem.at[0])]

    def stage(number, src, p_src, dst, p_dst):
        width = W - 1 - number
        factor = SEGMENT_COEF[number]
        final = number == len(SEGMENT_COEF) - 1
        for v in range(nv):
            p_src[v, 0:br, :] = pltpu.roll(p_src[v, last - br : last, :], 8, 1)
            p_src[v, last : last + br, :] = pltpu.roll(p_src[v, br : 2 * br, :], 120, 1)

        def blocks(b, count, first):
            around = pl.multiple_of((b - 1) * br, 8)
            view = src.at[:, pl.ds(around, (count + 2) * br), :]
            values = [block_cells(view, (i + 1) * br) for i in range(count)]
            groups = [
                [(i, t) for i in range(j, min(j + 2, count)) for t in range(1, turns + 1)] for j in range(0, count, 2)
            ]
            if first == 0:
                groups.append([(i, 0) for i in range(count)])

            def prepare(group):
                cells = []
                for i, t in group:
                    r = (b + i) // ng
                    g = b + i - r * ng
                    p_row = pl.multiple_of((g + 1) * br, 8) + 8 * t
                    row = pl.multiple_of((b + i) * br, 8) + 8 * t
                    cell = values[i](t)
                    beyond = [pltpu.roll(p_src[v, pl.ds(p_row, 8), :], 124 - 8 * r, 1) for v in range(nv)]
                    turn(cell, beyond, first_lane, last_lane)
                    cell["base"] = [ext[u, pl.ds(row, 8), :] for u in range(nv)] if number else cell["q"]
                    cell["step"] = (2.0 * DISSIP * factor) * ext[nv, pl.ds(row, 8), :]
                    cells.append(cell)
                return cells

            cells = prepare(groups[0])
            for n, group in enumerate(groups):
                following = prepare(groups[n + 1]) if n + 1 < len(groups) else None
                results = apply(cells)
                for (i, t), cell, result in zip(group, cells, results):
                    row = pl.multiple_of((b + i) * br, 8) + 8 * t
                    for u in range(nv):
                        value = cell["base"][u] - cell["step"] * result[u]
                        if final:
                            rows = pl.ds(pl.multiple_of((b + i - W) * al, 8) + t - 1, 8, stride=turns)
                            new_v[u, rows, :] = value
                        else:
                            dst[u, pl.ds(row, 8), :] = value
                            if t > 0 and number == 0:
                                rows = pl.ds(pl.multiple_of((b + i - 1) * al, 8) + t - 1, 8, stride=turns)
                                res_v[u, rows, :] = (2.0 * DISSIP) * result[u]
                cells = following

        def run(start, count, first):
            def loop(j, carry):
                blocks(start + STEP * j, STEP, first)
                return carry

            lax.fori_loop(0, count // STEP, loop, 0)
            if count % STEP:
                blocks(start + count // STEP * STEP, count % STEP, first)

        if final:
            for i in range(parts):
                run(W + i * (sl // parts), sl // parts, 1)
                rows = pl.ds(i * (sl // parts) * al, sl // parts * al)
                copy = pltpu.make_async_copy(new_v.at[:, rows, :], new.at[:, rows, :], sem.at[i + 1])
                copy.start()
                writes.append(copy)
        else:
            run(W - width, sl + 2 * width, 0)
        if number == 0:
            writes[0].start()
        if final:
            return

        def edges(v, carry):
            def store(row, val):
                edge[v, row : row + 8, :] = val

            gather_strips(dims, lambda row: src[v, row : row + 8, :], store, range(br // 8))
            return carry

        lax.fori_loop(0, nv, edges, 0)

        def strip(g, carry):
            base = pl.multiple_of((g + 1) * br, 8)
            around = pl.multiple_of(g * br, 8)
            view = p_src.at[:, pl.ds(around, 3 * br), :]

            values = block_cells(view, br)
            cells = [values(t) for t in range(br // 8)]
            for t, cell in enumerate(cells):
                turn(cell, [edge[v, pl.ds(around + 8 * t, 8), :] for v in range(nv)], pos4, pos3)
            for t, result in enumerate(apply(cells)):
                step = (2.0 * DISSIP * factor) * p_0[nv, pl.ds(base + 8 * t, 8), :]
                for u in range(nv):
                    p_dst[u, pl.ds(base + 8 * t, 8), :] = p_0[u, pl.ds(base + 8 * t, 8), :] - step * result[u]
            return carry

        lax.fori_loop(0, ng, strip, 0)

    stage(0, ext, p_0, q_a, p_a)
    stage(1, q_a, p_a, q_b, p_b)
    stage(2, q_b, p_b, q_a, p_a)
    stage(3, q_a, p_a, None, None)
    for copy in writes:
        copy.wait()


def shift_pairs(count, step, closed):
    return [(i, (i + step) % count) for i in range(count) if closed or 0 <= i + step < count]


def coef_table(part, donor_index, donor_weight, rl, nv, sizes):
    n_circ, n_span, n_axial = sizes
    modes, sl = part.shape[0], donor_index.shape[0]
    width = -(-max(rl * n_span * n_axial, sl * n_span) // 128) * 128
    circ, span, axial = (lax.axis_index(a) for a in AXES)
    rows = part[:, : nv * rl].reshape(modes, nv, rl).transpose(1, 0, 2).reshape(nv * modes, rl)
    table = jnp.zeros((nv * modes + 8, width), jnp.float32)
    table = lax.dynamic_update_slice(table, rows, (0, (span * n_axial + axial) * rl))
    donors = jnp.stack([donor_index.astype(jnp.float32), donor_weight])
    donors = jnp.where((circ == 0) & (axial == 0), donors, 0.0)
    table = lax.dynamic_update_slice(table, donors, (nv * modes, span * sl))
    return lax.psum(table, AXES)


def local(rotor_outlet, blade_count, harmonic_list, donor_index, donor_weight, state, time_step, flux_jacobian):
    f32 = jnp.float32
    n_circ, n_span, n_axial = (lax.axis_size(a) for a in AXES)
    nv, sl, al, cl = state.shape
    br = al + 2 * W
    nb = sl + 2 * W
    ng = -(-nb // 16)
    nh = harmonic_list.shape[0]
    dims = dict(
        nv=nv, sl=sl, al=al, cl=cl, br=br, nb=nb, ng=ng, nh=nh, n_circ=n_circ, n_span=n_span, n_axial=n_axial
    )
    rl = rotor_outlet.shape[1]
    packs = -(-nv // (128 // (sl + 2 * W)))
    ride = n_axial == 2 and n_circ == 4 and nv * rl <= 128
    dims.update(rl=rl, packs=packs, ride=ride)
    params = pltpu.CompilerParams(vmem_limit_bytes=48 * 2**20)
    sides = 1 if n_axial == 2 else 2

    edge, bulk, after = pl.pallas_call(
        functools.partial(axial_kernel, dims),
        out_shape=[
            jax.ShapeDtypeStruct((sides, nv + 1, W, 2 * W, cl), f32),
            jax.ShapeDtypeStruct((sides, nv + 1, W, sl - 2 * W, cl), f32),
            jax.ShapeDtypeStruct((8, 128), f32),
        ],
        in_specs=[VMEM] * 2,
        out_specs=[VMEM] * 3,
        compiler_params=params,
        name="axial_faces",
    )(state, time_step)
    part = pl.pallas_call(
        functools.partial(coef_kernel, dims),
        out_shape=jax.ShapeDtypeStruct((2 * nh, -(-nv * rl // 128) * 128), f32),
        in_specs=[VMEM, SMEM, SMEM, VMEM],
        out_specs=VMEM,
        compiler_params=params,
        name="coef_share",
    )(rotor_outlet, blade_count, harmonic_list, after)
    state = state.reshape(nv, sl * al, cl)
    time_step = time_step.reshape(sl * al, cl)

    def axial_move(faces):
        if n_axial == 2:
            moved = lax.ppermute(faces[0], "axial", [(0, 1), (1, 0)])
            return moved, moved
        lo = lax.ppermute(faces[0], "axial", shift_pairs(n_axial, 1, False))
        hi = lax.ppermute(faces[1], "axial", shift_pairs(n_axial, -1, False))
        return lo, hi

    lo_edge, hi_edge = axial_move(edge)
    if ride:
        other = lax.ppermute(part, "axial", [(0, 1), (1, 0)])
        before = lax.ppermute(part, ("span", "axial"), shift_pairs(n_span * n_axial, 1, False))
        shares = None
    else:
        other = before = part
        shares = coef_table(part, donor_index, donor_weight, rl, nv, (n_circ, n_span, n_axial))
    lo, hi = axial_move(bulk)

    def spec(shape, *index):
        index = index or (0,) * len(shape)
        return pl.BlockSpec(shape, lambda i: index)

    faces = (nv + 1, W, 2 * W, cl)
    message = ((nv + 1) * W * (al + W * sides) + (2 * nh if ride else 0), cl)
    end = sl // W - 1
    pad = lambda x: jnp.pad(x, (0, 128 - sl))[None]
    down, up, inter = pl.pallas_call(
        functools.partial(span_kernel, dims),
        grid=(1,),
        out_shape=[jax.ShapeDtypeStruct(message, f32)] * 2 + [jax.ShapeDtypeStruct((nv, 2 * nh, 128), f32)],
        in_specs=[
            spec((nv, W * al, cl)),
            spec((nv, W * al, cl), 0, end, 0),
            spec((W * al, cl)),
            spec((W * al, cl), end, 0),
            spec(faces),
            spec(faces),
            spec(part.shape),
            spec(part.shape),
            spec(part.shape),
            spec((1, 128)),
            spec((1, 128)),
        ],
        out_specs=[spec(message), spec(message), spec((nv, 2 * nh, 128))],
        compiler_params=params,
        name="span_faces",
    )(
        state, state, time_step, time_step, lo_edge, hi_edge, part, other, before, pad(donor_index), pad(donor_weight)
    )
    below = lax.ppermute(up, "span", shift_pairs(n_span, 1, False))
    above = lax.ppermute(down, "span", shift_pairs(n_span, -1, False))

    strip = jax.ShapeDtypeStruct(((nv + 1) // 2 * ng * br + (packs * 2 * nh if ride else 0), 128), f32)
    ext, left, right, share = pl.pallas_call(
        functools.partial(circ_kernel, dims),
        out_shape=[
            jax.ShapeDtypeStruct((nv + 1, nb * br, cl), f32),
            strip,
            strip,
            jax.ShapeDtypeStruct((packs * 2 * nh, 128), f32),
        ],
        in_specs=[VMEM] * 9,
        out_specs=[VMEM] * 4,
        scratch_shapes=[pltpu.VMEM((nv + 1, ng * br, 128), f32)],
        compiler_params=params,
        name="circ_faces",
    )(state, time_step, lo_edge, hi_edge, lo, hi, below, above, inter)
    from_left = lax.ppermute(right, "circ", shift_pairs(n_circ, 1, True))
    from_right = lax.ppermute(left, "circ", shift_pairs(n_circ, -1, True))
    if ride:
        shares = [share, lax.ppermute(share, "circ", shift_pairs(n_circ, 2, True))]

    block = jax.ShapeDtypeStruct((nv, sl * al, cl), f32)
    field = pltpu.VMEM((nv, nb * br, cl), f32)
    strips = pltpu.VMEM((nv, (ng + 2) * br, 128), f32)
    new, res, _ = pl.pallas_call(
        functools.partial(step_kernel, dims),
        out_shape=[block, block, jax.ShapeDtypeStruct(ext.shape, f32)],
        in_specs=[SMEM, SMEM, SMEM, [VMEM, VMEM] if ride else VMEM, VMEM, VMEM, VMEM],
        out_specs=[HBM, HBM, VMEM],
        input_output_aliases={(5 if ride else 4): 2},
        scratch_shapes=[
            pltpu.VMEM((nv, sl * al, cl), f32),
            pltpu.VMEM((nv, (sl + 2 * W - 2) * al, cl), f32),
            field,
            field,
            pltpu.VMEM((nv + 1, (ng + 2) * br, 128), f32),
            strips,
            strips,
            pltpu.VMEM((nv, ng * br, 128), f32),
            pltpu.VMEM((3 * nv * nv, 8, 128), f32),
            pltpu.SemaphoreType.DMA((5,)),
        ],
        compiler_params=params,
        name="segments",
    )(flux_jacobian, harmonic_list, blade_count, shares, ext, from_left, from_right)
    return new.reshape(nv, sl, al, cl), res.reshape(nv, sl, al, cl)


def solution(mesh):
    return jax.shard_map(
        local,
        mesh=mesh,
        in_specs=(
            P(None, ("span", "axial"), "circ"),
            P(),
            P(),
            P("span"),
            P("span"),
            P(None, "span", "axial", "circ"),
            P("span", "axial", "circ"),
            P(),
        ),
        out_specs=(P(None, "span", "axial", "circ"), P(None, "span", "axial", "circ")),
        check_vma=False,
    )
```

```python
import functools

import jax
import jax.numpy as jnp
import numpy as np
from jax import lax
from jax.experimental import pallas as pl
from jax.experimental.pallas import tpu as pltpu
from jax.sharding import PartitionSpec as P

SEGMENT_COEF = (0.25, 1.0 / 3.0, 0.5, 1.0)
DISSIP = 0.2
STEP = 4
W = 4
HIGH = lax.Precision.HIGHEST
VMEM = pl.BlockSpec(memory_space=pltpu.VMEM)
SMEM = pl.BlockSpec(memory_space=pltpu.SMEM)
HBM = pl.BlockSpec(memory_space=pltpu.HBM)
ANY = pl.BlockSpec(memory_space=pl.ANY)
AXES = ("circ", "span", "axial")


def make_basis(harm, blade, nh, cells, ncells):
    width = cells.shape[1]
    row = lax.broadcasted_iota(jnp.int32, (nh, width), 0)
    waves = jnp.zeros((nh, width), jnp.int32)
    for k in range(nh):
        waves = jnp.where(row == k, harm[k] * blade[0], waves)
    phase = waves * cells
    phase = phase & (ncells - 1) if ncells & (ncells - 1) == 0 else phase % ncells
    angle = (2.0 * np.pi) * phase.astype(jnp.float32) / ncells
    return jnp.concatenate([jnp.cos(angle), jnp.sin(angle)], axis=0)


def dot(a, b, dims):
    return lax.dot_general(a, b, (dims, ((), ())), precision=HIGH, preferred_element_type=jnp.float32)


def coef_kernel(dims, rotor, blade, harm, after, part):
    del after
    nv, cl = dims["nv"], dims["cl"]
    ncells = cl * dims["n_circ"]
    here = lax.axis_index("circ") * cl + lax.broadcasted_iota(jnp.int32, (1, cl), 1)
    basis = make_basis(harm, blade, dims["nh"], here, ncells)
    rl = rotor.shape[1]
    part[...] = jnp.zeros_like(part)
    part[:, : nv * rl] = dot(basis, rotor[...].reshape(nv * rl, cl), ((1,), (1,))) * (2.0 / ncells)


def axial_kernel(dims, state, dt, edge, bulk, after):
    nv, sl, al = (dims[k] for k in ("nv", "sl", "al"))
    axial = lax.axis_index("axial")
    swap = dims["n_axial"] == 2
    size = al
    after[...] = jnp.zeros_like(after)

    def put(side, base):
        for f in range(nv + 1):
            for i in range(W):
                rows = state[f, :, base + i, :] if f < nv else dt[:, base + i, :]
                edge[side, f, i, 0:W] = rows[0:W]
                edge[side, f, i, W:] = rows[sl - W :]
                bulk[side, f, i] = rows[W : sl - W]

    if swap:

        @pl.when(axial == 0)
        def _():
            put(0, size - W)

        @pl.when(axial != 0)
        def _():
            put(0, 0)

    else:
        put(0, size - W)
        put(1, 0)


def inter_rows(dims, parts, firsts, donor, weight):
    nv = dims["nv"]
    rl = dims["rl"]
    table = jnp.concatenate([p[:, : nv * rl] for p in parts], axis=1)
    rows = table.shape[1]
    row = lax.broadcasted_iota(jnp.int32, (rows, 128), 0)
    station = row % rl
    for i, first in enumerate(firsts):
        station = station + jnp.where(row // (nv * rl) == i, first, 0)
    mix = jnp.where(station == donor, 1.0 - weight, jnp.where(station == donor + 1, weight, 0.0))
    var = row // rl % nv
    return [dot(table, jnp.where(var == v, mix, 0.0), ((1,), (0,))) for v in range(nv)]


def span_kernel(dims, s_head, s_tail, d_head, d_tail, lo, hi, part, other, before, donor, weight, down, up, inter):
    nv, sl, al, cl, br, nh = (dims[k] for k in ("nv", "sl", "al", "cl", "br", "nh"))
    span = lax.axis_index("span")
    faces = (lo,) if dims["n_axial"] == 2 else (lo, hi)
    rows_of = (nv + 1) * W * (al + W * len(faces))
    for out, s_ref, d_ref, at in ((down, s_head, d_head, 0), (up, s_tail, d_tail, W)):
        for f in range(nv + 1):
            rows = slice(f * W * al, (f + 1) * W * al)
            out[rows, :] = s_ref[f] if f < nv else d_ref[...]
            for side, src in enumerate(faces):
                for i in range(W):
                    to = (nv + 1) * W * al + ((side * (nv + 1) + f) * W + i) * W
                    out[to : to + W, :] = src[f, i, at : at + W, :]

    if not dims["ride"]:
        return
    rl = dims["rl"]
    first = span * 2 * rl
    shares = inter_rows(
        dims, [part[...], other[...], before[...]], [first, first + rl, first - rl], donor[...], weight[...]
    )
    lane = lax.broadcasted_iota(jnp.int32, (2 * nh, 128), 1)
    head = tail = jnp.zeros((2 * nh, 128), jnp.float32)
    for v in range(nv):
        inter[v] = shares[v]
        mine = lane // W == v
        head = jnp.where(mine, pltpu.roll(shares[v], W * v, 1), head)
        tail = jnp.where(mine, pltpu.roll(shares[v], (W * v - (sl - W)) % 128, 1), tail)
    down[rows_of:, :] = head
    up[rows_of:, :] = tail


def lane_ids(rows=8):
    return lax.broadcasted_iota(jnp.int32, (rows, 128), 1)


def gather_strips(dims, load, store, tiles):
    nb, ng, br = dims["nb"], dims["ng"], dims["br"]
    group = lane_ids() // 8
    for g in range(ng):
        for t in tiles:
            acc = jnp.zeros((8, 128), jnp.float32)
            for r in range((nb - 1 - g) // ng + 1):
                part = pltpu.roll(load((ng * r + g) * br + 8 * t), (8 * r + 4) % 128, 1)
                acc = jnp.where(group == r, part, acc)
            store(g * br + 8 * t, acc)


def circ_kernel(
    dims, state, dt, lo_edge, hi_edge, lo, hi, below, above, inter, ext, left, right, share, strips
):
    nv, sl, al, cl, br, nb, ng, nh = (dims[k] for k in ("nv", "sl", "al", "cl", "br", "nb", "ng", "nh"))
    axial = lax.axis_index("axial")
    turns = al // 8
    for f in range(nv + 1):
        for s in range(sl):
            for t in range(turns):
                rows = pl.ds(s * al + t, 8, stride=turns)
                at = (s + W) * br + 8 * (t + 1)
                ext[f, at : at + 8, :] = state[f, rows, :] if f < nv else dt[rows, :]

    swap = dims["n_axial"] == 2
    for side, (edge, bulk, valid) in enumerate(
        ((lo_edge, lo, axial > 0), (hi_edge, hi, axial < dims["n_axial"] - 1))
    ):
        base = 0 if side else W

        def fill(edge, bulk, side, base):
            for f in range(nv + 1):
                for i in range(W):
                    part = (nv + 1) * W * al + (((0 if swap else side) * (nv + 1) + f) * W + i) * W
                    pieces = (
                        (0, W, lambda: below[part : part + W, :]),
                        (W, W, lambda: edge[f, i, 0:W]),
                        (2 * W, sl - 2 * W, lambda: bulk[f, i]),
                        (sl, W, lambda: edge[f, i, W:]),
                        (sl + W, W, lambda: above[part : part + W, :]),
                    )
                    for at, n, read in pieces:
                        val = jnp.zeros((n, cl), jnp.float32) if edge is None else read()
                        ext[f, pl.ds(base + at * br + i, n, stride=br), :] = val

        @pl.when(valid)
        def _(edge=edge, bulk=bulk, side=side, base=base):
            fill(edge, bulk, side, base)

        @pl.when(jnp.logical_not(valid))
        def _(side=side, base=base):
            fill(None, None, side, base)

    for f in range(nv + 1):
        for j in range(W):
            for src, b in ((below, j), (above, sl + W + j)):
                for t in range(turns):
                    at = b * br + 8 * (t + 1)
                    ext[f, at : at + 8, :] = src[pl.ds((f * W + j) * al + t, 8, stride=turns), :]

    def each(f, carry):
        def store(row, val):
            strips[f, row : row + 8, :] = val

        gather_strips(dims, lambda row: ext[f, row : row + 8, :], store, range(br // 8))
        return carry

    lax.fori_loop(0, nv + 1, each, 0)
    half = (nv + 1) // 2
    low = lane_ids(ng * br) % 8 < 4
    for f in range(half):
        one, two = strips[f], strips[f + half]
        rows = slice(f * ng * br, (f + 1) * ng * br)
        right[rows, :] = jnp.where(low, one, pltpu.roll(two, 4, 1))
        left[rows, :] = jnp.where(low, pltpu.roll(one, 124, 1), two)

    if not dims["ride"]:
        return
    wide = sl + 2 * W
    lane = lax.broadcasted_iota(jnp.int32, (2 * nh, 128), 1)
    rows = slice((nv + 1) * W * (al + W * (1 if swap else 2)), None)
    packed = [jnp.zeros((2 * nh, 128), jnp.float32)] * dims["packs"]
    for v in range(nv):
        whole = pltpu.roll(inter[v], W, 1)
        whole = jnp.where(lane < W, pltpu.roll(below[rows, :], (-W * v) % 128, 1), whole)
        whole = jnp.where(lane >= sl + W, pltpu.roll(above[rows, :], sl + W - W * v, 1), whole)
        pack, first = divmod(v, 128 // wide)
        first = first * wide
        packed[pack] = jnp.where(
            (lane >= first) & (lane < first + wide), pltpu.roll(whole, first, 1), packed[pack]
        )
    for i in range(dims["packs"]):
        at = half * ng * br + i * 2 * nh
        left[at : at + 2 * nh, :] = packed[i]
        right[at : at + 2 * nh, :] = packed[i]
        share[i * 2 * nh : (i + 1) * 2 * nh, :] = packed[i]


def ghost_table(dims, table, span):
    nv, sl, nh = (dims[k] for k in ("nv", "sl", "nh"))
    rows, width = table.shape
    donors = pltpu.roll(table[rows - 8 :, :], lax.rem(width - span * sl + W, width), 1)[:, :128]
    lane = lax.broadcasted_iota(jnp.int32, (1, 128), 1)
    where = span * sl - W + lane
    inside = (where >= 0) & (where < sl * dims["n_span"]) & (lane < sl + 2 * W)
    station = lax.broadcasted_iota(jnp.int32, (width, 128), 0)
    donor = (donors[0:1, :] + 0.5).astype(jnp.int32)
    weight = donors[1:2, :]
    mix = jnp.where(station == donor, 1.0 - weight, jnp.where(station == donor + 1, weight, 0.0))
    mix = jnp.where(inside, mix, 0.0)
    inter = dot(table[0 : rows - 8, :], mix, ((1,), (0,)))
    return [inter[v * 2 * nh : (v + 1) * 2 * nh, :] for v in range(nv)]


def step_kernel(
    dims, jac, harm, blade, shares, _, from_left, from_right, new, res, ext, new_v, res_v, q_a, q_b, p_0, p_a, p_b, edge, coef, sem
):
    nv, sl, al, cl, br, nb, ng, nh = (dims[k] for k in ("nv", "sl", "al", "cl", "br", "nb", "ng", "nh"))
    axial = lax.axis_index("axial")
    span = lax.axis_index("span")
    circ = lax.axis_index("circ")
    spare = (W - 1) * al
    parts = 4 if sl % 8 == 0 else 1
    for d in range(3):
        for u in range(nv):
            for v in range(nv):
                value = (jac[d, u, v] * 0.5 - (DISSIP if u == v else 0.0)) * (0.5 / DISSIP)
                coef[(d * nv + u) * nv + v] = jnp.full((8, 128), value, jnp.float32)

    half = (nv + 1) // 2
    low = lane_ids(ng * br) % 8 < 4
    for f in range(half):
        rows = slice(f * ng * br, (f + 1) * ng * br)
        one, two = from_left[rows, :], from_right[rows, :]
        p_0[f, br : (ng + 1) * br, :] = jnp.where(low, one, pltpu.roll(two, 4, 1))
        p_0[f + half, br : (ng + 1) * br, :] = jnp.where(low, pltpu.roll(one, 124, 1), two)

    ncells = cl * dims["n_circ"]
    lane = lax.broadcasted_iota(jnp.int32, (1, 128), 1)
    wide = sl + 2 * W
    if dims["ride"]:
        rows = slice(half * ng * br, None)
        packed = from_left[rows, :] + from_right[rows, :] + shares[0][...] + shares[1][...]
        inter = [packed[i * 2 * nh : (i + 1) * 2 * nh, :] for i in range(dims["packs"])]
        each = 128 // wide
    else:
        inter = ghost_table(dims, shares, span)
        each = 1
    start = circ * cl
    own = make_basis(harm, blade, nh, start + lax.broadcasted_iota(jnp.int32, (1, cl), 1), ncells)
    pos = lane % 8
    halo_cells = lax.rem(start + jnp.where(pos < 4, pos - 4, pos + cl - 4) + ncells, ncells)
    halo = make_basis(harm, blade, nh, halo_cells, ncells)
    s_id = lax.broadcasted_iota(jnp.int32, (wide, 128), 0)
    r_id = lax.broadcasted_iota(jnp.int32, (wide, 128), 1) // 8

    @pl.when(axial == 0)
    def _():
        ghosts = [dot(part, own, ((0,), (0,))) for part in inter]
        halos = [dot(part, halo, ((0,), (0,))) for part in inter]
        for v in range(nv):
            rows = slice(v % each * wide, (v % each + 1) * wide)
            ext[v, pl.ds(7, wide, stride=br), :] = ghosts[v // each][rows]
            for g in range(ng):
                picked = jnp.where(s_id == ng * r_id + g, halos[v // each][rows], 0.0)
                at = (g + 1) * br + 7
                p_0[v, at : at + 1, :] = jnp.sum(picked, axis=0, keepdims=True)

    lanes = lane_ids()
    first_lane, last_lane = lanes == 0, lanes == 127
    pos3, pos4 = lanes % 8 == 3, lanes % 8 == 4
    last = (ng + 1) * br

    def apply(cells):
        sums = [[3.0 * q for q in c["q"]] for c in cells]
        for d, name in enumerate(("axial", "span", "theta")):
            diff = []
            for c, total in zip(cells, sums):
                diff.append([p - m for p, m in zip(c[name + "+"], c[name + "-"])])
                for u in range(nv):
                    total[u] = total[u] - c[name + "-"][u]
            for v in range(nv):
                for u in range(nv):
                    k = coef[(d * nv + u) * nv + v]
                    for i in range(len(cells)):
                        sums[i][u] = sums[i][u] + k * diff[i][v]
        return sums

    turns = al // 8
    sub = lax.broadcasted_iota(jnp.int32, (8, 128), 0)
    top, bottom = sub == 0, sub == 7

    def block_cells(view, at):
        memo = {}

        def load(t, off=0):
            if (t, off) not in memo:
                row = at + off + 8 * t
                memo[t, off] = [view[v, row : row + 8, :] for v in range(nv)]
            return memo[t, off]

        def rolled(t, amount):
            if (t, "roll", amount) not in memo:
                memo[t, "roll", amount] = [pltpu.roll(x, amount, 0) for x in load(t)]
            return memo[t, "roll", amount]

        def choose(mask, one, two):
            return [jnp.where(mask, x, y) for x, y in zip(one, two)]

        def values(t):
            if t == 0:
                plus = choose(bottom, rolled(1, 7), rolled(0, 7))
                minus = choose(top, rolled(turns, 1), rolled(0, 1))
            else:
                plus = load(t + 1) if t < turns else choose(bottom, rolled(0, 7), rolled(1, 7))
                minus = load(t - 1) if t > 1 else choose(top, rolled(0, 1), rolled(turns, 1))
            return {"q": load(t), "axial-": minus, "axial+": plus, "span-": load(t, -br), "span+": load(t, br)}

        return values

    def turn(cell, beyond, at_plus, at_minus):
        cell["theta+"] = [
            pltpu.roll(jnp.where(at_plus, z, q), 127, 1) for z, q in zip(beyond, cell["q"])
        ]
        cell["theta-"] = [pltpu.roll(jnp.where(at_minus, z, q), 1, 1) for z, q in zip(beyond, cell["q"])]

    writes = [pltpu.make_async_copy(res_v.at[:, pl.ds(spare, sl * al), :], res, sem.at[0])]

    def stage(number, src, p_src, dst, p_dst):
        width = W - 1 - number
        factor = SEGMENT_COEF[number]
        final = number == len(SEGMENT_COEF) - 1
        for v in range(nv):
            p_src[v, 0:br, :] = pltpu.roll(p_src[v, last - br : last, :], 8, 1)
            p_src[v, last : last + br, :] = pltpu.roll(p_src[v, br : 2 * br, :], 120, 1)

        def blocks(b, count, first):
            around = pl.multiple_of((b - 1) * br, 8)
            view = src.at[:, pl.ds(around, (count + 2) * br), :]
            values = [block_cells(view, (i + 1) * br) for i in range(count)]
            groups = [
                [(i, t) for i in range(j, min(j + 2, count)) for t in range(1, turns + 1)] for j in range(0, count, 2)
            ]
            if first == 0:
                groups.append([(i, 0) for i in range(count)])

            def prepare(group):
                cells = []
                for i, t in group:
                    r = (b + i) // ng
                    g = b + i - r * ng
                    p_row = pl.multiple_of((g + 1) * br, 8) + 8 * t
                    row = pl.multiple_of((b + i) * br, 8) + 8 * t
                    cell = values[i](t)
                    beyond = [pltpu.roll(p_src[v, pl.ds(p_row, 8), :], 124 - 8 * r, 1) for v in range(nv)]
                    turn(cell, beyond, first_lane, last_lane)
                    cell["base"] = [ext[u, pl.ds(row, 8), :] for u in range(nv)] if number else cell["q"]
                    cell["step"] = (2.0 * DISSIP * factor) * ext[nv, pl.ds(row, 8), :]
                    cells.append(cell)
                return cells

            cells = prepare(groups[0])
            for n, group in enumerate(groups):
                results = apply(cells)
                for (i, t), cell, result in zip(group, cells, results):
                    row = pl.multiple_of((b + i) * br, 8) + 8 * t
                    for u in range(nv):
                        value = cell["base"][u] - cell["step"] * result[u]
                        if final:
                            rows = pl.ds(pl.multiple_of((b + i - W) * al, 8) + t - 1, 8, stride=turns)
                            new_v[u, rows, :] = value
                        else:
                            dst[u, pl.ds(row, 8), :] = value
                            if t > 0 and number == 0:
                                rows = pl.ds(pl.multiple_of((b + i - 1) * al, 8) + t - 1, 8, stride=turns)
                                res_v[u, rows, :] = (2.0 * DISSIP) * result[u]
                cells = prepare(groups[n + 1]) if n + 1 < len(groups) else None

        def run(start, count, first):
            def loop(j, carry):
                blocks(start + STEP * j, STEP, first)
                return carry

            lax.fori_loop(0, count // STEP, loop, 0)
            if count % STEP:
                blocks(start + count // STEP * STEP, count % STEP, first)

        if final:
            for i in range(parts):
                run(W + i * (sl // parts), sl // parts, 1)
                rows = pl.ds(i * (sl // parts) * al, sl // parts * al)
                copy = pltpu.make_async_copy(new_v.at[:, rows, :], new.at[:, rows, :], sem.at[i + 1])
                copy.start()
                writes.append(copy)
        else:
            run(W - width, sl + 2 * width, 0)
        if number == 0:
            writes[0].start()
        if final:
            return

        def edges(v, carry):
            def store(row, val):
                edge[v, row : row + 8, :] = val

            gather_strips(dims, lambda row: src[v, row : row + 8, :], store, range(br // 8))
            return carry

        lax.fori_loop(0, nv, edges, 0)

        def strip(g, carry):
            base = pl.multiple_of((g + 1) * br, 8)
            around = pl.multiple_of(g * br, 8)
            view = p_src.at[:, pl.ds(around, 3 * br), :]

            values = block_cells(view, br)
            cells = [values(t) for t in range(br // 8)]
            for t, cell in enumerate(cells):
                turn(cell, [edge[v, pl.ds(around + 8 * t, 8), :] for v in range(nv)], pos4, pos3)
            for t, result in enumerate(apply(cells)):
                step = (2.0 * DISSIP * factor) * p_0[nv, pl.ds(base + 8 * t, 8), :]
                for u in range(nv):
                    p_dst[u, pl.ds(base + 8 * t, 8), :] = p_0[u, pl.ds(base + 8 * t, 8), :] - step * result[u]
            return carry

        lax.fori_loop(0, ng, strip, 0)

    stage(0, ext, p_0, q_a, p_a)
    stage(1, q_a, p_a, q_b, p_b)
    stage(2, q_b, p_b, q_a, p_a)
    stage(3, q_a, p_a, None, None)
    for copy in writes:
        copy.wait()


def shift_pairs(count, step, closed):
    return [(i, (i + step) % count) for i in range(count) if closed or 0 <= i + step < count]


def coef_table(part, donor_index, donor_weight, rl, nv, sizes):
    n_circ, n_span, n_axial = sizes
    modes, sl = part.shape[0], donor_index.shape[0]
    width = -(-max(rl * n_span * n_axial, sl * n_span) // 128) * 128
    circ, span, axial = (lax.axis_index(a) for a in AXES)
    rows = part[:, : nv * rl].reshape(modes, nv, rl).transpose(1, 0, 2).reshape(nv * modes, rl)
    table = jnp.zeros((nv * modes + 8, width), jnp.float32)
    table = lax.dynamic_update_slice(table, rows, (0, (span * n_axial + axial) * rl))
    donors = jnp.stack([donor_index.astype(jnp.float32), donor_weight])
    donors = jnp.where((circ == 0) & (axial == 0), donors, 0.0)
    table = lax.dynamic_update_slice(table, donors, (nv * modes, span * sl))
    return lax.psum(table, AXES)


def local(rotor_outlet, blade_count, harmonic_list, donor_index, donor_weight, state, time_step, flux_jacobian):
    f32 = jnp.float32
    n_circ, n_span, n_axial = (lax.axis_size(a) for a in AXES)
    nv, sl, al, cl = state.shape
    br = al + 2 * W
    nb = sl + 2 * W
    ng = -(-nb // 16)
    nh = harmonic_list.shape[0]
    dims = dict(
        nv=nv, sl=sl, al=al, cl=cl, br=br, nb=nb, ng=ng, nh=nh, n_circ=n_circ, n_span=n_span, n_axial=n_axial
    )
    rl = rotor_outlet.shape[1]
    packs = -(-nv // (128 // (sl + 2 * W)))
    ride = n_axial == 2 and n_circ == 4 and nv * rl <= 128
    dims.update(rl=rl, packs=packs, ride=ride)
    params = pltpu.CompilerParams(vmem_limit_bytes=48 * 2**20)
    sides = 1 if n_axial == 2 else 2

    edge, bulk, after = pl.pallas_call(
        functools.partial(axial_kernel, dims),
        out_shape=[
            jax.ShapeDtypeStruct((sides, nv + 1, W, 2 * W, cl), f32),
            jax.ShapeDtypeStruct((sides, nv + 1, W, sl - 2 * W, cl), f32),
            jax.ShapeDtypeStruct((8, 128), f32),
        ],
        in_specs=[VMEM] * 2,
        out_specs=[VMEM] * 3,
        compiler_params=params,
        name="axial_faces",
    )(state, time_step)
    part = pl.pallas_call(
        functools.partial(coef_kernel, dims),
        out_shape=jax.ShapeDtypeStruct((2 * nh, -(-nv * rl // 128) * 128), f32),
        in_specs=[VMEM, SMEM, SMEM, VMEM],
        out_specs=VMEM,
        compiler_params=params,
        name="coef_share",
    )(rotor_outlet, blade_count, harmonic_list, after)
    state = state.reshape(nv, sl * al, cl)
    time_step = time_step.reshape(sl * al, cl)

    def axial_move(faces):
        if n_axial == 2:
            moved = lax.ppermute(faces[0], "axial", [(0, 1), (1, 0)])
            return moved, moved
        lo = lax.ppermute(faces[0], "axial", shift_pairs(n_axial, 1, False))
        hi = lax.ppermute(faces[1], "axial", shift_pairs(n_axial, -1, False))
        return lo, hi

    lo_edge, hi_edge = axial_move(edge)
    if ride:
        other = lax.ppermute(part, "axial", [(0, 1), (1, 0)])
        before = lax.ppermute(part, ("span", "axial"), shift_pairs(n_span * n_axial, 1, False))
        shares = None
    else:
        other = before = part
        shares = coef_table(part, donor_index, donor_weight, rl, nv, (n_circ, n_span, n_axial))
    lo, hi = axial_move(bulk)

    def spec(shape, *index):
        index = index or (0,) * len(shape)
        return pl.BlockSpec(shape, lambda i: index)

    faces = (nv + 1, W, 2 * W, cl)
    message = ((nv + 1) * W * (al + W * sides) + (2 * nh if ride else 0), cl)
    end = sl // W - 1
    pad = lambda x: jnp.pad(x, (0, 128 - sl))[None]
    down, up, inter = pl.pallas_call(
        functools.partial(span_kernel, dims),
        grid=(1,),
        out_shape=[jax.ShapeDtypeStruct(message, f32)] * 2 + [jax.ShapeDtypeStruct((nv, 2 * nh, 128), f32)],
        in_specs=[
            spec((nv, W * al, cl)),
            spec((nv, W * al, cl), 0, end, 0),
            spec((W * al, cl)),
            spec((W * al, cl), end, 0),
            spec(faces),
            spec(faces),
            spec(part.shape),
            spec(part.shape),
            spec(part.shape),
            spec((1, 128)),
            spec((1, 128)),
        ],
        out_specs=[spec(message), spec(message), spec((nv, 2 * nh, 128))],
        compiler_params=params,
        name="span_faces",
    )(
        state, state, time_step, time_step, lo_edge, hi_edge, part, other, before, pad(donor_index), pad(donor_weight)
    )
    below = lax.ppermute(up, "span", shift_pairs(n_span, 1, False))
    above = lax.ppermute(down, "span", shift_pairs(n_span, -1, False))

    strip = jax.ShapeDtypeStruct(((nv + 1) // 2 * ng * br + (packs * 2 * nh if ride else 0), 128), f32)
    ext, left, right, share = pl.pallas_call(
        functools.partial(circ_kernel, dims),
        out_shape=[
            jax.ShapeDtypeStruct((nv + 1, nb * br, cl), f32),
            strip,
            strip,
            jax.ShapeDtypeStruct((packs * 2 * nh, 128), f32),
        ],
        in_specs=[VMEM] * 9,
        out_specs=[VMEM] * 4,
        scratch_shapes=[pltpu.VMEM((nv + 1, ng * br, 128), f32)],
        compiler_params=params,
        name="circ_faces",
    )(state, time_step, lo_edge, hi_edge, lo, hi, below, above, inter)
    from_left = lax.ppermute(right, "circ", shift_pairs(n_circ, 1, True))
    from_right = lax.ppermute(left, "circ", shift_pairs(n_circ, -1, True))
    if ride:
        shares = [share, lax.ppermute(share, "circ", shift_pairs(n_circ, 2, True))]

    block = jax.ShapeDtypeStruct((nv, sl * al, cl), f32)
    field = pltpu.VMEM((nv, nb * br, cl), f32)
    strips = pltpu.VMEM((nv, (ng + 2) * br, 128), f32)
    new, res, _ = pl.pallas_call(
        functools.partial(step_kernel, dims),
        out_shape=[block, block, jax.ShapeDtypeStruct(ext.shape, f32)],
        in_specs=[SMEM, SMEM, SMEM, [VMEM, VMEM] if ride else VMEM, VMEM, VMEM, VMEM],
        out_specs=[HBM, HBM, VMEM],
        input_output_aliases={(5 if ride else 4): 2},
        scratch_shapes=[
            pltpu.VMEM((nv, sl * al, cl), f32),
            pltpu.VMEM((nv, (sl + 2 * W - 2) * al, cl), f32),
            field,
            field,
            pltpu.VMEM((nv + 1, (ng + 2) * br, 128), f32),
            strips,
            strips,
            pltpu.VMEM((nv, ng * br, 128), f32),
            pltpu.VMEM((3 * nv * nv, 8, 128), f32),
            pltpu.SemaphoreType.DMA((5,)),
        ],
        compiler_params=params,
        name="segments",
    )(flux_jacobian, harmonic_list, blade_count, shares, ext, from_left, from_right)
    return new.reshape(nv, sl, al, cl), res.reshape(nv, sl, al, cl)


def solution(mesh):
    return jax.shard_map(
        local,
        mesh=mesh,
        in_specs=(
            P(None, ("span", "axial"), "circ"),
            P(),
            P(),
            P("span"),
            P("span"),
            P(None, "span", "axial", "circ"),
            P("span", "axial", "circ"),
            P(),
        ),
        out_specs=(P(None, "span", "axial", "circ"), P(None, "span", "axial", "circ")),
        check_vma=False,
    )
```
